32 devices in a mesh: seq: 4 (over z), head: 2 (over x), batch: 4 (over y, core).
Axes of the slice: x: 2, y: 2, z: 4, core: 2. Of those that a mesh axis runs over, the one named last changes fastest.
Arguments:
- query: bfloat16 [8, 4, 128, 32, 128], P('batch', 'seq', None, 'head'), parts along dimension 0, may hold values from -6 to 6
- keys: bfloat16 [8, 4, 128, 8, 128], P('batch', 'seq', None, 'head'), parts along dimension 0, may hold values from -6 to 6
- values: bfloat16 [8, 4, 128, 8, 128], P('batch', 'seq', None, 'head'), parts along dimension 0, may hold values from -6 to 6
- grad_out: bfloat16 [8, 4, 128, 32, 128], P('batch', 'seq', None, 'head'), parts along dimension 0, may hold values from -6 to 6
- doc_starts: int32 [2048], P('batch'), parts along dimension 0, may hold values from 0 to 1024, as said below
Outputs:
- attended: bfloat16 [8, 4, 128, 32, 128], P('batch', 'seq', None, 'head'), parts along dimension 0
- grad_query: bfloat16 [8, 4, 128, 32, 128], P('batch', 'seq', None, 'head'), parts along dimension 0
- grad_keys: bfloat16 [8, 4, 128, 8, 128], P('batch', 'seq', None, 'head'), parts along dimension 0
- grad_values: bfloat16 [8, 4, 128, 8, 128], P('batch', 'seq', None, 'head'), parts along dimension 0
The draws below stay inside these ranges and needn't reach their ends.
There are 4 independent parts, one for each index of `batch`. The reference program is written for one: setup_inputs(seed, part) draws one part's arguments, and reference() takes and returns one part's arrays. A program takes and returns all parts, laid end to end along the dimension named above; each array names one. Nothing has to cross between parts.
Inputs may be any that keep to these rules, and one draw needn't show every extreme that they name: `doc_starts`: entry 0 is 0; entries rise with differences of 2 to 256 until an entry reaches 1024, and every later entry equals 1024; one difference is exactly 256. So every document has at most 256 tokens.
All inputs are finite; a program needn't handle non-finite values.
Results may differ from the reference program's by a relative error of at most 0.0065.
Values may be sent and summed in bfloat16 or wider, within the bound.
No kernel may reach another device: no remote copies, remote signals or barrier semaphores. Data moves between devices by JAX's collectives and lax.ppermute only.
A program may use at most 128 MiB of HBM per device.

```python
import jax
import jax.numpy as jnp
from jax import lax

QUERY_HEADS = 32
KEY_VALUE_HEADS = 8
HEAD_WIDTH = 128
SPAN_TOKENS = 128
WINDOW = 2
N_SEQ = 4


def doc_bounds(key):
    sequence_length = 2 * SPAN_TOKENS * N_SEQ
    longest = WINDOW * SPAN_TOKENS
    count = sequence_length // 2
    bits = jax.random.randint(jax.random.fold_in(key, 15), (count,), 1, longest.bit_length())
    limits = jnp.minimum(jnp.left_shift(jnp.ones((count,), jnp.int32), bits), longest)
    lengths = jax.random.randint(jax.random.fold_in(key, 11), (count,), 2, limits + 1)
    chosen = jax.random.randint(jax.random.fold_in(key, 12), (), 0, 4)
    lengths = jnp.where(jnp.arange(count) == chosen, longest, lengths).astype(jnp.int32)
    ends = jnp.cumsum(lengths).astype(jnp.int32)
    starts = jnp.concatenate([jnp.zeros((1,), jnp.int32), ends[:-1]])
    return jnp.minimum(starts, sequence_length).astype(jnp.int32)


def mirror_layout(full):
    spans = full.reshape((2 * N_SEQ, SPAN_TOKENS) + full.shape[1:])
    return jnp.stack([spans[:N_SEQ], spans[N_SEQ:][::-1]], axis=0)


def draw_query(key, part):
    sequence_length = 2 * SPAN_TOKENS * N_SEQ
    base_offset = jnp.clip(jax.random.normal(jax.random.fold_in(key, 21), (sequence_length, QUERY_HEADS, HEAD_WIDTH), jnp.float32), -6.0, 6.0)
    return mirror_layout(base_offset).astype(jnp.bfloat16)


def draw_keys(key, part):
    sequence_length = 2 * SPAN_TOKENS * N_SEQ
    base_offset = jnp.clip(jax.random.normal(jax.random.fold_in(key, 22), (sequence_length, KEY_VALUE_HEADS, HEAD_WIDTH), jnp.float32), -6.0, 6.0)
    return mirror_layout(base_offset).astype(jnp.bfloat16)


def draw_doc_starts(key, part):
    return doc_bounds(key)


def level_of(own_key, dims, cuts, smallest, largest):
    def one(position, blocks):
        steps = jax.random.uniform(jax.random.fold_in(jax.random.fold_in(own_key, 6), position), (blocks,), jnp.float32, smallest / len(cuts), largest / len(cuts))
        return jnp.repeat(jnp.exp(steps), dims[position] // blocks).reshape((-1,) + (1,) * (len(dims) - position - 1))

    gain = one(*cuts[0])
    for cut in cuts[1:]:
        gain = gain * one(*cut)
    return gain


def centred(own_key, shape, spread, most, cuts=(), kind=jnp.bfloat16):
    result = spread * jax.random.normal(own_key, shape, jnp.float32)
    if cuts:
        result = result * level_of(own_key, shape, cuts, -0.22, 0.18)
    return jnp.clip(result, -most, most).astype(kind)


def setup_inputs(seed: int = 0, part: int = 0) -> dict:
    seeds = jax.random.split(jax.random.key(seed), 6)
    part_splits = jax.random.split(jax.random.fold_in(seeds[5], part), 6)
    return {
        "query": draw_query(jax.random.fold_in(jax.random.fold_in(seeds[5], part), 71), part),
        "keys": draw_keys(jax.random.fold_in(jax.random.fold_in(seeds[5], part), 71), part),
        "values": centred(part_splits[2], (2, N_SEQ, SPAN_TOKENS, KEY_VALUE_HEADS, HEAD_WIDTH), 1.0, 6.0, ((1, 4), (3, 2))),
        "grad_out": centred(part_splits[3], (2, N_SEQ, SPAN_TOKENS, QUERY_HEADS, HEAD_WIDTH), 1.0, 6.0, ((1, 4), (3, 2))),
        "doc_starts": draw_doc_starts(jax.random.fold_in(jax.random.fold_in(seeds[5], part), 71), part),
    }


def in_order(array):
    return jnp.concatenate([array[0], array[1][::-1]], axis=0)


def mirrored(array):
    half_count = array.shape[0] // 2
    return jnp.stack([array[:half_count], array[half_count:][::-1]], axis=0)


def doc_index(doc_starts, positions):
    return jnp.searchsorted(doc_starts, positions, side="right").astype(jnp.int32) - 1


def head_terms(pieces, allowed, score_scale):
    query_wide = pieces[0].astype(jnp.float32)
    key_wide = pieces[1].astype(jnp.float32)
    value_wide = pieces[2].astype(jnp.float32)
    grad_wide = pieces[3].astype(jnp.float32)
    scores = jnp.einsum("rgd,jd->grj", query_wide, key_wide) * score_scale
    scores = jnp.where(allowed[None], scores, -jnp.inf)
    top_score = jnp.max(scores, axis=-1, keepdims=True)
    expons = jnp.exp(scores - top_score)
    weights = expons / jnp.sum(expons, axis=-1, keepdims=True)
    weights_low = weights.astype(jnp.bfloat16)
    weights_wide = weights_low.astype(jnp.float32)
    attended = jnp.einsum("grj,jd->rgd", weights_wide, value_wide).astype(jnp.bfloat16)
    grad_weights = jnp.einsum("rgd,jd->grj", grad_wide, value_wide)
    delta = jnp.transpose(jnp.sum(grad_wide * attended.astype(jnp.float32), axis=-1), (1, 0))
    grad_scores = (weights * (grad_weights - delta[..., None]) * score_scale).astype(jnp.bfloat16)
    grad_scores_wide = grad_scores.astype(jnp.float32)
    grad_query = jnp.einsum("grj,jd->rgd", grad_scores_wide, key_wide).astype(jnp.bfloat16)
    grad_keys = jnp.einsum("grj,rgd->jd", grad_scores_wide, query_wide)
    grad_values = jnp.einsum("grj,rgd->jd", weights_wide, grad_wide)
    return attended, grad_query, grad_keys, grad_values


def reference(query, keys, values, grad_out, doc_starts):
    query_ord = in_order(query)
    keys_ord = in_order(keys)
    values_ord = in_order(values)
    grad_ord = in_order(grad_out)
    span_count, span_len, head_count, head_dim = query_ord.shape
    kv_heads = keys_ord.shape[2]
    group_size = head_count // kv_heads
    score_scale = head_dim ** -0.5
    window = WINDOW
    key_count = (window + 1) * span_len
    keys_pad = jnp.concatenate([jnp.zeros((window,) + keys_ord.shape[1:], keys_ord.dtype), keys_ord], axis=0)
    values_pad = jnp.concatenate([jnp.zeros((window,) + values_ord.shape[1:], values_ord.dtype), values_ord], axis=0)

    def one_span(totals, pieces):
        key_total, value_total = totals
        queries, grad_output, span_idx = pieces
        token_pos = span_idx * span_len + jnp.arange(span_len, dtype=jnp.int32)
        key_pos = (span_idx - window) * span_len + jnp.arange(key_count, dtype=jnp.int32)
        query_doc = doc_index(doc_starts, token_pos)
        key_doc = doc_index(doc_starts, key_pos)
        allowed = (query_doc[:, None] == key_doc[None, :]) & (key_pos[None, :] <= token_pos[:, None])
        key_window = lax.dynamic_slice_in_dim(keys_pad, span_idx, window + 1, 0).reshape(key_count, kv_heads, head_dim)
        value_window = lax.dynamic_slice_in_dim(values_pad, span_idx, window + 1, 0).reshape(key_count, kv_heads, head_dim)
        query_heads = jnp.transpose(queries.reshape(span_len, kv_heads, group_size, head_dim), (1, 0, 2, 3))
        grad_heads = jnp.transpose(grad_output.reshape(span_len, kv_heads, group_size, head_dim), (1, 0, 2, 3))
        attended, grad_query, grad_keys, grad_values = lax.map(
            lambda parts: head_terms(parts, allowed, score_scale),
            (query_heads, jnp.transpose(key_window, (1, 0, 2)), jnp.transpose(value_window, (1, 0, 2)), grad_heads))
        key_terms = jnp.transpose(grad_keys, (1, 0, 2)).reshape(window + 1, span_len, kv_heads, head_dim)
        value_terms = jnp.transpose(grad_values, (1, 0, 2)).reshape(window + 1, span_len, kv_heads, head_dim)
        key_total = lax.dynamic_update_slice_in_dim(
            key_total, lax.dynamic_slice_in_dim(key_total, span_idx, window + 1, 0) + key_terms, span_idx, 0)
        value_total = lax.dynamic_update_slice_in_dim(
            value_total, lax.dynamic_slice_in_dim(value_total, span_idx, window + 1, 0) + value_terms, span_idx, 0)
        attended = jnp.transpose(attended, (1, 0, 2, 3)).reshape(span_len, head_count, head_dim)
        grad_query = jnp.transpose(grad_query, (1, 0, 2, 3)).reshape(span_len, head_count, head_dim)
        return (key_total, value_total), (attended, grad_query)

    zero_total = jnp.zeros((window + span_count, span_len, kv_heads, head_dim), jnp.float32)
    totals, outputs = lax.scan(one_span, (zero_total, zero_total),
                               (query_ord, grad_ord, jnp.arange(span_count, dtype=jnp.int32)))
    grad_keys = totals[0][window:].astype(jnp.bfloat16)
    grad_values = totals[1][window:].astype(jnp.bfloat16)
    return (mirrored(outputs[0]), mirrored(outputs[1]), mirrored(grad_keys), mirrored(grad_values))
```

```python
import functools

import jax
import jax.numpy as jnp
from jax import lax
from jax.experimental import pallas as pl
from jax.experimental.pallas import tpu as pltpu
from jax.sharding import PartitionSpec as P

LOG2E = 1.4426950408889634
NEG = -1e30


def swap_pairs(count):
    pairs_a = []
    for i in range(0, count - 1, 2):
        pairs_a += [(i, i + 1), (i + 1, i)]
    pairs_b = []
    for i in range(1, count - 1, 2):
        pairs_b += [(i, i + 1), (i + 1, i)]
    pairs_b.append((count - 1, count - 1))
    return pairs_a, pairs_b


def contract(lhs, rhs, lhs_dim, rhs_dim):
    return lax.dot_general(
        lhs, rhs, (((lhs_dim,), (rhs_dim,)), ((), ())), preferred_element_type=jnp.float32
    )


def attention_kernel(blocks, scale, info_ref, q_ref, do_ref, starts_ref, *refs):
    kv_refs = (refs[0:blocks], refs[blocks : 2 * blocks])
    o_ref, dq_ref = refs[2 * blocks : 2 * blocks + 2]
    deep_refs = refs[2 * blocks + 2 : 2 * blocks + 4]
    rest_refs = refs[2 * blocks + 4 : 2 * blocks + 6]
    k_all, v_all, s_all, p_all = refs[2 * blocks + 6 :]
    group, span, dim = q_ref.shape[1:]
    rows = group * span

    def each(body, init):
        if blocks <= 4:
            for t in range(blocks):
                init = body(t, init)
            return init
        return lax.fori_loop(0, blocks, body, init)

    for slot in range(2):
        half = info_ref[slot]
        span_first = info_ref[2 + slot] * span
        for t in range(blocks):
            k_all[t] = kv_refs[slot][t][0, 0]
            v_all[t] = kv_refs[slot][t][1, 0]
        queries = q_ref[half].reshape(rows, dim)
        grad_out = do_ref[half].reshape(rows, dim)
        start = starts_ref[half]
        token = span_first + lax.broadcasted_iota(jnp.int32, (1, span), 1)
        key_row = span_first + lax.broadcasted_iota(jnp.int32, (span, span), 0)

        def scores(t, top):
            key_pos = key_row - t * span
            allowed = (key_pos >= start) & (key_pos <= token)
            bias = jnp.where(allowed, 0.0, NEG)
            value = contract(k_all[t], queries, 1, 1) + jnp.concatenate([bias] * group, axis=1)
            s_all[t] = value
            return jnp.maximum(top, jnp.max(value, axis=0, keepdims=True))

        top = each(scores, jnp.full((1, rows), NEG, jnp.float32))

        def expons(t, total):
            value = jnp.exp2((s_all[t] - top) * (scale * LOG2E))
            s_all[t] = value
            return total + jnp.sum(value, axis=0, keepdims=True)

        total = each(expons, jnp.zeros((1, rows), jnp.float32))
        inverse = 1.0 / total

        def forward(t, carry):
            out, delta = carry
            weights = s_all[t] * inverse
            low = weights.astype(jnp.bfloat16)
            grad_weights = contract(v_all[t], grad_out, 1, 1)
            s_all[t] = weights
            p_all[t] = grad_weights
            delta = delta + jnp.sum(weights * grad_weights, axis=0, keepdims=True)
            out = out + contract(v_all[t], low, 0, 0)
            grad_value = contract(low, grad_out, 1, 0)
            store_term(t, 1, grad_value)
            return out, delta

        def store_term(t, which, value):
            if isinstance(t, int):
                if t == blocks - 1:
                    deep_refs[slot][which, 0] = value.astype(jnp.bfloat16)
                else:
                    rest_refs[slot][t, which, 0] = value
            else:
                @pl.when(t == blocks - 1)
                def _():
                    deep_refs[slot][which, 0] = value.astype(jnp.bfloat16)

                @pl.when(t < blocks - 1)
                def _():
                    rest_refs[slot][t, which, 0] = value

        out, delta = each(
            forward, (jnp.zeros((dim, rows), jnp.float32), jnp.zeros((1, rows), jnp.float32))
        )

        def backward(t, grad_query):
            low = (s_all[t] * (p_all[t] - delta)).astype(jnp.bfloat16)
            store_term(t, 0, contract(low, queries, 1, 0) * scale)
            return grad_query + contract(k_all[t], low, 0, 0)

        grad_query = each(backward, jnp.zeros((dim, rows), jnp.float32)) * scale
        for g in range(group):
            columns = slice(g * span, (g + 1) * span)
            o_ref[half, g] = out[:, columns].T.astype(jnp.bfloat16)
            dq_ref[half, g] = grad_query[:, columns].T.astype(jnp.bfloat16)


def attention_chunk(info, q_t, do_t, starts, kv_blocks, first_head, scale):
    blocks = len(kv_blocks[0])
    _, heads, span, dim = q_t.shape
    chunk = kv_blocks[0][0].shape[1]
    group = 4
    rows = group * span
    window = blocks - 1
    q_spec = pl.BlockSpec((2, group, span, dim), lambda m, info: (0, first_head + m, 0, 0))
    o_spec = pl.BlockSpec((2, group, span, dim), lambda m, info: (0, m, 0, 0))
    kv_spec = pl.BlockSpec((2, 1, span, dim), lambda m, info: (0, m, 0, 0))
    rest_spec = pl.BlockSpec((window, 2, 1, span, dim), lambda m, info: (0, 0, m, 0, 0))
    starts_spec = pl.BlockSpec((2, 1, span), lambda m, info: (0, 0, 0))
    deep = jax.ShapeDtypeStruct((2, chunk, span, dim), jnp.bfloat16)
    rest = jax.ShapeDtypeStruct((window, 2, chunk, span, dim), jnp.float32)
    out = jax.ShapeDtypeStruct((2, chunk * group, span, dim), jnp.bfloat16)
    macs = 2 * chunk * 5 * rows * blocks * span * dim
    return pl.pallas_call(
        functools.partial(attention_kernel, blocks, scale),
        grid_spec=pltpu.PrefetchScalarGridSpec(
            num_scalar_prefetch=1,
            grid=(chunk,),
            in_specs=[q_spec, q_spec, starts_spec] + [kv_spec] * (2 * blocks),
            out_specs=[o_spec, o_spec, kv_spec, kv_spec, rest_spec, rest_spec],
            scratch_shapes=[
                pltpu.VMEM((blocks, span, dim), jnp.bfloat16),
                pltpu.VMEM((blocks, span, dim), jnp.bfloat16),
                pltpu.VMEM((blocks, span, rows), jnp.float32),
                pltpu.VMEM((blocks, span, rows), jnp.float32),
            ],
        ),
        out_shape=[out, out, deep, deep, rest, rest],
        compiler_params=pltpu.CompilerParams(vmem_limit_bytes=48 * 1024 * 1024),
        cost_estimate=pl.CostEstimate(
            flops=2 * macs, bytes_accessed=8 * 1024 * 1024, transcendentals=0
        ),
        name="attention",
    )(info, q_t, do_t, starts, *kv_blocks[0], *kv_blocks[1])


def body(query, keys, values, grad_out, doc_starts):
    count = lax.axis_size("seq")
    device = lax.axis_index("seq")
    window = min(16, count // 2)
    span = query.shape[2]
    heads = query.shape[3]
    kv_heads = keys.shape[3]
    dim = query.shape[4]
    scale = dim ** (-0.5)
    pairs_a, pairs_b = swap_pairs(count)
    parity = device % 2
    chunks = 2
    chunk = kv_heads // chunks

    both = jnp.stack([keys[:, 0], values[:, 0]], axis=1)
    both = jnp.transpose(both, (0, 3, 1, 2, 4))
    half_of = (1 - parity, parity)
    own = [
        [
            jnp.transpose(
                lax.dynamic_slice(
                    both, (half, c * chunk, 0, 0, 0), (1, chunk, 2, span, dim)
                )[0],
                (1, 0, 2, 3),
            )
            for half in half_of
        ]
        for c in range(chunks)
    ]
    history = [([own[c][0]], [own[c][1]]) for c in range(chunks)]
    for _ in range(window):
        for c in range(chunks):
            line_a, line_b = history[c]
            next_a = lax.ppermute(line_b[-1], "seq", pairs_a)
            next_b = lax.ppermute(line_a[-1], "seq", pairs_b)
            line_a.append(next_a)
            line_b.append(next_b)

    q_t = jnp.transpose(query[:, 0], (0, 2, 1, 3))
    do_t = jnp.transpose(grad_out[:, 0], (0, 2, 1, 3))
    spans = jnp.stack([device, 2 * count - 1 - device])
    token = (spans[:, None] * span + jnp.arange(span, dtype=jnp.int32)[None, :]).astype(jnp.int32)
    starts = jnp.max(
        jnp.where(doc_starts[None, None, :] <= token[:, :, None], doc_starts[None, None, :], 0),
        axis=2,
    )[:, None, :]
    half_a, half_b = half_of
    info = jnp.stack(
        [half_a, half_b, jnp.where(half_a == 0, device, 2 * count - 1 - device),
         jnp.where(half_b == 0, device, 2 * count - 1 - device)]
    ).astype(jnp.int32)

    outs, dqs, totals = [], [], []
    for c in range(chunks):
        out, dq, deep_a, deep_b, rest_a, rest_b = attention_chunk(
            info, q_t, do_t, starts, history[c], c * chunk, scale
        )
        outs.append(out)
        dqs.append(dq)
        totals.append((deep_a, deep_b, rest_a, rest_b))
    finals = []
    for c in range(chunks):
        now_a, now_b, rest_a, rest_b = totals[c]
        for t in range(window - 1, -1, -1):
            from_a = lax.ppermute(now_a, "seq", pairs_a)
            from_b = lax.ppermute(now_b, "seq", pairs_b)
            now_a = (rest_a[t] + from_b.astype(jnp.float32)).astype(jnp.bfloat16)
            now_b = (rest_b[t] + from_a.astype(jnp.float32)).astype(jnp.bfloat16)
        finals.append((now_a, now_b))
    slots = jnp.stack(
        [jnp.concatenate([f[s] for f in finals], axis=1) for s in range(2)], axis=0
    )
    halves = jnp.where(parity == 0, slots[::-1], slots)
    halves = jnp.transpose(halves, (1, 0, 3, 2, 4))[:, :, None]
    out = jnp.transpose(jnp.concatenate(outs, axis=1), (0, 2, 1, 3))[:, None]
    dq = jnp.transpose(jnp.concatenate(dqs, axis=1), (0, 2, 1, 3))[:, None]
    return out, dq, halves[0], halves[1]


def solution(mesh):
    spec = P("batch", "seq", None, "head", None)
    return jax.shard_map(
        body,
        mesh=mesh,
        in_specs=(spec, spec, spec, spec, P("batch")),
        out_specs=(spec, spec, spec, spec),
        check_vma=False,
    )
```

```python
import functools

import jax
import jax.numpy as jnp
from jax import lax
from jax.experimental import pallas as pl
from jax.experimental.pallas import tpu as pltpu
from jax.sharding import PartitionSpec as P

LOG2E = 1.4426950408889634
NEG = -1e30


def swap_pairs(count):
    pairs_a = []
    for i in range(0, count - 1, 2):
        pairs_a += [(i, i + 1), (i + 1, i)]
    pairs_b = []
    for i in range(1, count - 1, 2):
        pairs_b += [(i, i + 1), (i + 1, i)]
    pairs_b.append((count - 1, count - 1))
    return pairs_a, pairs_b


def contract(lhs, rhs, lhs_dim, rhs_dim):
    return lax.dot_general(
        lhs, rhs, (((lhs_dim,), (rhs_dim,)), ((), ())), preferred_element_type=jnp.float32
    )


def attention_kernel(blocks, scale, info_ref, q_ref, do_ref, starts_ref, *refs):
    kv_refs = (refs[0:blocks], refs[blocks : 2 * blocks])
    o_ref, dq_ref = refs[2 * blocks : 2 * blocks + 2]
    deep_refs = refs[2 * blocks + 2 : 2 * blocks + 4]
    rest_refs = refs[2 * blocks + 4 : 2 * blocks + 6]
    k_all, v_all, s_all, p_all = refs[2 * blocks + 6 :]
    group, span, dim = q_ref.shape[1:]
    rows = group * span

    def each(body, init):
        if blocks <= 4:
            for t in range(blocks):
                init = body(t, init)
            return init
        return lax.fori_loop(0, blocks, body, init)

    for slot in range(2):
        half = info_ref[slot]
        span_first = info_ref[2 + slot] * span
        for t in range(blocks):
            k_all[t] = kv_refs[slot][t][0, 0]
            v_all[t] = kv_refs[slot][t][1, 0]
        queries = q_ref[half].reshape(rows, dim)
        grad_out = do_ref[half].reshape(rows, dim)
        start = starts_ref[half]
        token = span_first + lax.broadcasted_iota(jnp.int32, (1, span), 1)
        key_row = span_first + lax.broadcasted_iota(jnp.int32, (span, span), 0)

        def scores(t, top):
            key_pos = key_row - t * span
            allowed = (key_pos >= start) & (key_pos <= token)
            bias = jnp.where(allowed, 0.0, NEG)
            value = contract(k_all[t], queries, 1, 1) + jnp.concatenate([bias] * group, axis=1)
            s_all[t] = value
            return jnp.maximum(top, jnp.max(value, axis=0, keepdims=True))

        top = each(scores, jnp.full((1, rows), NEG, jnp.float32))

        def expons(t, total):
            value = jnp.exp2((s_all[t] - top) * (scale * LOG2E))
            s_all[t] = value
            return total + jnp.sum(value, axis=0, keepdims=True)

        total = each(expons, jnp.zeros((1, rows), jnp.float32))
        inverse = 1.0 / total

        def forward(t, carry):
            out, delta = carry
            weights = s_all[t] * inverse
            low = weights.astype(jnp.bfloat16)
            grad_weights = contract(v_all[t], grad_out, 1, 1)
            s_all[t] = weights
            p_all[t] = grad_weights
            delta = delta + jnp.sum(weights * grad_weights, axis=0, keepdims=True)
            out = out + contract(v_all[t], low, 0, 0)
            grad_value = contract(low, grad_out, 1, 0)
            store_term(t, 1, grad_value)
            return out, delta

        def store_term(t, which, value):
            if isinstance(t, int):
                if t == blocks - 1:
                    deep_refs[slot][which, 0] = value.astype(jnp.bfloat16)
                else:
                    rest_refs[slot][t, which, 0] = value
            else:
                @pl.when(t == blocks - 1)
                def _():
                    deep_refs[slot][which, 0] = value.astype(jnp.bfloat16)

                @pl.when(t < blocks - 1)
                def _():
                    rest_refs[slot][t, which, 0] = value

        out, delta = each(
            forward, (jnp.zeros((dim, rows), jnp.float32), jnp.zeros((1, rows), jnp.float32))
        )

        def backward(t, grad_query):
            low = (s_all[t] * (p_all[t] - delta)).astype(jnp.bfloat16)
            store_term(t, 0, contract(low, queries, 1, 0) * scale)
            return grad_query + contract(k_all[t], low, 0, 0)

        grad_query = each(backward, jnp.zeros((dim, rows), jnp.float32)) * scale
        for g in range(group):
            columns = slice(g * span, (g + 1) * span)
            o_ref[half, g] = out[:, columns].T.astype(jnp.bfloat16)
            dq_ref[half, g] = grad_query[:, columns].T.astype(jnp.bfloat16)


def attention_chunk(info, q_t, do_t, starts, kv_blocks, first_head, scale):
    blocks = len(kv_blocks[0])
    _, heads, span, dim = q_t.shape
    chunk = kv_blocks[0][0].shape[1]
    group = 4
    rows = group * span
    window = blocks - 1
    q_spec = pl.BlockSpec((2, group, span, dim), lambda m, info: (0, first_head + m, 0, 0))
    o_spec = pl.BlockSpec((2, group, span, dim), lambda m, info: (0, m, 0, 0))
    kv_spec = pl.BlockSpec((2, 1, span, dim), lambda m, info: (0, m, 0, 0))
    rest_spec = pl.BlockSpec((window, 2, 1, span, dim), lambda m, info: (0, 0, m, 0, 0))
    starts_spec = pl.BlockSpec((2, 1, span), lambda m, info: (0, 0, 0))
    deep = jax.ShapeDtypeStruct((2, chunk, span, dim), jnp.bfloat16)
    rest = jax.ShapeDtypeStruct((window, 2, chunk, span, dim), jnp.float32)
    out = jax.ShapeDtypeStruct((2, chunk * group, span, dim), jnp.bfloat16)
    macs = 2 * chunk * 5 * rows * blocks * span * dim
    return pl.pallas_call(
        functools.partial(attention_kernel, blocks, scale),
        grid_spec=pltpu.PrefetchScalarGridSpec(
            num_scalar_prefetch=1,
            grid=(chunk,),
            in_specs=[q_spec, q_spec, starts_spec] + [kv_spec] * (2 * blocks),
            out_specs=[o_spec, o_spec, kv_spec, kv_spec, rest_spec, rest_spec],
            scratch_shapes=[
                pltpu.VMEM((blocks, span, dim), jnp.bfloat16),
                pltpu.VMEM((blocks, span, dim), jnp.bfloat16),
                pltpu.VMEM((blocks, span, rows), jnp.float32),
                pltpu.VMEM((blocks, span, rows), jnp.float32),
            ],
        ),
        out_shape=[out, out, deep, deep, rest, rest],
        compiler_params=pltpu.CompilerParams(vmem_limit_bytes=48 * 1024 * 1024),
        cost_estimate=pl.CostEstimate(
            flops=2 * macs, bytes_accessed=8 * 1024 * 1024, transcendentals=0
        ),
        name="attention",
    )(info, q_t, do_t, starts, *kv_blocks[0], *kv_blocks[1])


def vmem_call(kernel, out_shape, macs, name, *args):
    whole = pl.BlockSpec(memory_space=pltpu.VMEM)
    moved = sum(a.size * a.dtype.itemsize for a in args[1:])
    return pl.pallas_call(
        kernel,
        in_specs=[pl.BlockSpec(memory_space=pltpu.SMEM)] + [whole] * (len(args) - 1),
        out_specs=[whole] * len(out_shape),
        out_shape=out_shape,
        compiler_params=pltpu.CompilerParams(vmem_limit_bytes=16 * 1024 * 1024),
        cost_estimate=pl.CostEstimate(flops=8 * macs, bytes_accessed=moved, transcendentals=0),
        name=name,
    )(*args)


def group_of(ref, half, m, group):
    return ref[half, pl.ds(m * group, group)].reshape(group * ref.shape[2], ref.shape[3])


def scores_kernel(info_ref, q_ref, do_ref, kv_a_ref, kv_b_ref, s_ref, dp_ref):
    heads = kv_a_ref.shape[1]
    group = q_ref.shape[1] // heads

    def one_head(m, carry):
        for slot, kv_ref in enumerate((kv_a_ref, kv_b_ref)):
            half = info_ref[slot]
            s_ref[slot, m] = contract(kv_ref[0, m], group_of(q_ref, half, m, group), 1, 1)
            dp_ref[slot, m] = contract(kv_ref[1, m], group_of(do_ref, half, m, group), 1, 1)
        return carry

    lax.fori_loop(0, heads, one_head, 0)


def later_keys(span, group, dtype):
    row = lax.broadcasted_iota(jnp.int32, (span, span), 0)
    column = lax.broadcasted_iota(jnp.int32, (span, span), 1)
    return jnp.concatenate([(row > column).astype(jnp.float32).astype(dtype)] * group, axis=1)


def softmax_kernel(scale, info_ref, starts_ref, q_ref, do_ref, kv_a_ref, kv_b_ref, s0_ref, dp0_ref, s1_ref,
                   dp1_ref, deep_a_ref, deep_b_ref, low_ref, ds_ref):
    heads, span, rows = s0_ref.shape[1:]
    group = rows // span
    row = lax.broadcasted_iota(jnp.int32, (span, span), 0)
    column = lax.broadcasted_iota(jnp.int32, (span, span), 1)
    far = row > column
    far_wide = jnp.concatenate([far] * group, axis=1)
    far_low = later_keys(span, group, jnp.bfloat16)

    def one_head(m, carry):
        for slot, (kv_ref, deep_ref) in enumerate(((kv_a_ref, deep_a_ref), (kv_b_ref, deep_b_ref))):
            half = info_ref[slot]
            first = info_ref[2 + slot] * span
            start = starts_ref[half]
            queries = group_of(q_ref, half, m, group)
            grad_out = group_of(do_ref, half, m, group)
            near_pos = jnp.where(far, first - 2 * span + row, first + row)
            bias = jnp.where(near_pos >= start, 0.0, NEG)
            bias_prev = jnp.where(first - span + row >= start, 0.0, NEG)
            s2 = contract(kv_ref[0, m], queries, 1, 1)
            dp2 = contract(kv_ref[1, m], grad_out, 1, 1)
            s = jnp.where(far_wide, s2, s0_ref[slot, m]) + jnp.concatenate([bias] * group, axis=1)
            dp = jnp.where(far_wide, dp2, dp0_ref[slot, m])
            s_prev = s1_ref[slot, m] + jnp.concatenate([bias_prev] * group, axis=1)
            dp_prev = dp1_ref[slot, m]
            top = jnp.max(jnp.maximum(s, s_prev), axis=0, keepdims=True)
            e = jnp.exp2((s - top) * (scale * LOG2E))
            e_prev = jnp.exp2((s_prev - top) * (scale * LOG2E))
            inverse = 1.0 / jnp.sum(e + e_prev, axis=0, keepdims=True)
            w = e * inverse
            w_prev = e_prev * inverse
            delta = jnp.sum(w * dp + w_prev * dp_prev, axis=0, keepdims=True)
            low = w.astype(jnp.bfloat16)
            ds = (w * (dp - delta)).astype(jnp.bfloat16)
            low_ref[slot, m, 0] = low
            ds_ref[slot, m, 0] = ds
            low_ref[slot, m, 1] = w_prev.astype(jnp.bfloat16)
            ds_ref[slot, m, 1] = (w_prev * (dp_prev - delta)).astype(jnp.bfloat16)
            deep_ref[0, m] = (contract(ds * far_low, queries, 1, 0) * scale).astype(jnp.bfloat16)
            deep_ref[1, m] = contract(low * far_low, grad_out, 1, 0).astype(jnp.bfloat16)
        return carry

    lax.fori_loop(0, heads, one_head, 0)


def terms_kernel(scale, info_ref, q_ref, do_ref, low_ref, ds_ref, prev_a_ref, prev_b_ref, own_a_ref, own_b_ref):
    heads, _, span, rows = low_ref.shape[1:]
    group = rows // span
    own_low = 1 - later_keys(span, group, jnp.bfloat16)

    def one_head(m, carry):
        for slot, (prev_ref, own_ref) in enumerate(((prev_a_ref, own_a_ref), (prev_b_ref, own_b_ref))):
            half = info_ref[slot]
            queries = group_of(q_ref, half, m, group)
            grad_out = group_of(do_ref, half, m, group)
            ds = jnp.concatenate([ds_ref[slot, m, 1], ds_ref[slot, m, 0] * own_low], axis=0)
            low = jnp.concatenate([low_ref[slot, m, 1], low_ref[slot, m, 0] * own_low], axis=0)
            grad_key = contract(ds, queries, 1, 0) * scale
            grad_value = contract(low, grad_out, 1, 0)
            prev_ref[0, m] = grad_key[:span]
            prev_ref[1, m] = grad_value[:span]
            own_ref[0, m] = grad_key[span:]
            own_ref[1, m] = grad_value[span:]
        return carry

    lax.fori_loop(0, heads, one_head, 0)


def outputs_kernel(scale, info_ref, low_ref, ds_ref, kv_a0, kv_b0, kv_a1, kv_b1, kv_a2, kv_b2, o_ref, dq_ref):
    heads, _, span, rows = low_ref.shape[1:]
    group = rows // span
    far_low = later_keys(span, group, jnp.bfloat16)
    own_low = 1 - far_low

    def one_head(m, carry):
        for slot, kv_refs in enumerate(((kv_a0, kv_a1, kv_a2), (kv_b0, kv_b1, kv_b2))):
            half = info_ref[slot]
            low = low_ref[slot, m, 0]
            ds = ds_ref[slot, m, 0]
            low = jnp.concatenate([low * own_low, low_ref[slot, m, 1], low * far_low], axis=0)
            ds = jnp.concatenate([ds * own_low, ds_ref[slot, m, 1], ds * far_low], axis=0)
            keys = jnp.concatenate([ref[0, m] for ref in kv_refs], axis=0)
            values = jnp.concatenate([ref[1, m] for ref in kv_refs], axis=0)
            out = contract(values, low, 0, 0)
            grad_query = contract(keys, ds, 0, 0) * scale
            for g in range(group):
                columns = slice(g * span, (g + 1) * span)
                o_ref[half, m * group + g] = out[:, columns].T.astype(jnp.bfloat16)
                dq_ref[half, m * group + g] = grad_query[:, columns].T.astype(jnp.bfloat16)
        return carry

    lax.fori_loop(0, heads, one_head, 0)


def two_span_window(info, q_t, do_t, starts, own_a, own_b, pairs_a, pairs_b, scale):
    _, kv_heads, span, dim = own_a.shape
    heads = q_t.shape[1]
    rows = heads // kv_heads * span
    block = 2 * kv_heads * rows * span * dim
    shape = jax.ShapeDtypeStruct
    scores = [shape((2, kv_heads, span, rows), jnp.float32)] * 2
    terms = [shape(own_a.shape, jnp.float32)] * 4
    lows = [shape((2, kv_heads, 2, span, rows), jnp.bfloat16)] * 2
    deeps = [shape(own_a.shape, jnp.bfloat16)] * 2
    outs = [shape(q_t.shape, jnp.bfloat16)] * 2

    b1 = lax.ppermute(own_a, "seq", pairs_b)
    a1 = lax.ppermute(own_b, "seq", pairs_a)
    s0, dp0 = vmem_call(scores_kernel, scores, 2 * block, "scores_own", info, q_t, do_t, own_a, own_b)
    b2 = lax.ppermute(a1, "seq", pairs_b)
    a2 = lax.ppermute(b1, "seq", pairs_a)
    s1, dp1 = vmem_call(scores_kernel, scores, 2 * block, "scores_prev", info, q_t, do_t, a1, b1)
    deep_a, deep_b, low, ds = vmem_call(
        functools.partial(softmax_kernel, scale), deeps + lows, 4 * block, "softmax",
        info, starts, q_t, do_t, a2, b2, s0, dp0, s1, dp1,
    )
    from_b = lax.ppermute(deep_b, "seq", pairs_b)
    from_a = lax.ppermute(deep_a, "seq", pairs_a)
    prev_a, prev_b, own_term_a, own_term_b = vmem_call(
        functools.partial(terms_kernel, scale), terms, 4 * block, "terms", info, q_t, do_t, low, ds
    )
    out, dq = vmem_call(
        functools.partial(outputs_kernel, scale), outs, 6 * block, "outputs",
        info, low, ds, own_a, own_b, a1, b1, a2, b2,
    )
    next_b = (prev_b + from_a.astype(jnp.float32)).astype(jnp.bfloat16)
    next_a = (prev_a + from_b.astype(jnp.float32)).astype(jnp.bfloat16)
    last_b = lax.ppermute(next_b, "seq", pairs_b)
    last_a = lax.ppermute(next_a, "seq", pairs_a)
    final_a = (own_term_a + last_b.astype(jnp.float32)).astype(jnp.bfloat16)
    final_b = (own_term_b + last_a.astype(jnp.float32)).astype(jnp.bfloat16)
    return out, dq, final_a, final_b


def any_window(info, q_t, do_t, starts, own_a, own_b, pairs_a, pairs_b, window, scale):
    kv_heads = own_a.shape[1]
    chunks = 2
    chunk = kv_heads // chunks
    parts = []
    for c in range(chunks):
        line_a = [own_a[:, c * chunk : (c + 1) * chunk]]
        line_b = [own_b[:, c * chunk : (c + 1) * chunk]]
        for _ in range(window):
            next_a = lax.ppermute(line_b[-1], "seq", pairs_a)
            next_b = lax.ppermute(line_a[-1], "seq", pairs_b)
            line_a.append(next_a)
            line_b.append(next_b)
        out, dq, now_a, now_b, rest_a, rest_b = attention_chunk(
            info, q_t, do_t, starts, (line_a, line_b), c * chunk, scale
        )
        for t in range(window - 1, -1, -1):
            from_a = lax.ppermute(now_a, "seq", pairs_a)
            from_b = lax.ppermute(now_b, "seq", pairs_b)
            now_a = (rest_a[t] + from_b.astype(jnp.float32)).astype(jnp.bfloat16)
            now_b = (rest_b[t] + from_a.astype(jnp.float32)).astype(jnp.bfloat16)
        parts.append((out, dq, now_a, now_b))
    return tuple(jnp.concatenate(arrays, axis=1) for arrays in zip(*parts))


def body(query, keys, values, grad_out, doc_starts):
    count = lax.axis_size("seq")
    device = lax.axis_index("seq")
    window = min(16, count // 2)
    span = query.shape[2]
    kv_heads = keys.shape[3]
    dim = query.shape[4]
    scale = dim ** (-0.5)
    pairs_a, pairs_b = swap_pairs(count)
    parity = device % 2

    half_a, half_b = 1 - parity, parity
    both = jnp.transpose(jnp.stack([keys[:, 0], values[:, 0]], axis=1), (0, 1, 3, 2, 4))
    own_a, own_b = (
        lax.dynamic_index_in_dim(both, half, 0, keepdims=False) for half in (half_a, half_b)
    )
    q_t = jnp.transpose(query[:, 0], (0, 2, 1, 3))
    do_t = jnp.transpose(grad_out[:, 0], (0, 2, 1, 3))
    spans = jnp.stack([device, 2 * count - 1 - device])
    token = spans[:, None] * span + jnp.arange(span, dtype=jnp.int32)[None, :]
    below = doc_starts[None, None, :] <= token[:, :, None]
    starts = jnp.max(jnp.where(below, doc_starts[None, None, :], 0), axis=2)[:, None, :]
    span_a = jnp.where(half_a == 0, device, 2 * count - 1 - device)
    info = jnp.stack([half_a, half_b, span_a, 2 * count - 1 - span_a]).astype(jnp.int32)

    if window == 2:
        out, dq, final_a, final_b = two_span_window(
            info, q_t, do_t, starts, own_a, own_b, pairs_a, pairs_b, scale
        )
    else:
        out, dq, final_a, final_b = any_window(
            info, q_t, do_t, starts, own_a, own_b, pairs_a, pairs_b, window, scale
        )
    halves = jnp.where(parity == 0, jnp.stack([final_b, final_a]), jnp.stack([final_a, final_b]))
    halves = jnp.transpose(halves, (1, 0, 3, 2, 4))[:, :, None]
    out = jnp.transpose(out, (0, 2, 1, 3))[:, None]
    dq = jnp.transpose(dq, (0, 2, 1, 3))[:, None]
    return out, dq, halves[0], halves[1]


def solution(mesh):
    spec = P("batch", "seq", None, "head", None)
    return jax.shard_map(
        body,
        mesh=mesh,
        in_specs=(spec, spec, spec, spec, P("batch")),
        out_specs=(spec, spec, spec, spec),
        check_vma=False,
    )
```

```python
import functools

import jax
import jax.numpy as jnp
from jax import lax
from jax.experimental import pallas as pl
from jax.experimental.pallas import tpu as pltpu
from jax.sharding import PartitionSpec as P

LOG2E = 1.4426950408889634
NEG = -1e30


def swap_pairs(count):
    pairs_a = []
    for i in range(0, count - 1, 2):
        pairs_a += [(i, i + 1), (i + 1, i)]
    pairs_b = []
    for i in range(1, count - 1, 2):
        pairs_b += [(i, i + 1), (i + 1, i)]
    pairs_b.append((count - 1, count - 1))
    return pairs_a, pairs_b


def contract(lhs, rhs, lhs_dim, rhs_dim):
    return lax.dot_general(
        lhs, rhs, (((lhs_dim,), (rhs_dim,)), ((), ())), preferred_element_type=jnp.float32
    )


def attention_kernel(blocks, scale, info_ref, q_ref, do_ref, starts_ref, *refs):
    kv_refs = (refs[0:blocks], refs[blocks : 2 * blocks])
    o_ref, dq_ref = refs[2 * blocks : 2 * blocks + 2]
    deep_refs = refs[2 * blocks + 2 : 2 * blocks + 4]
    rest_refs = refs[2 * blocks + 4 : 2 * blocks + 6]
    k_all, v_all, s_all, p_all = refs[2 * blocks + 6 :]
    group, span, dim = q_ref.shape[1:]
    rows = group * span

    def each(body, init):
        if blocks <= 4:
            for t in range(blocks):
                init = body(t, init)
            return init
        return lax.fori_loop(0, blocks, body, init)

    for slot in range(2):
        half = info_ref[slot]
        span_first = info_ref[2 + slot] * span
        for t in range(blocks):
            k_all[t] = kv_refs[slot][t][0, 0]
            v_all[t] = kv_refs[slot][t][1, 0]
        queries = q_ref[half].reshape(rows, dim)
        grad_out = do_ref[half].reshape(rows, dim)
        start = starts_ref[half]
        token = span_first + lax.broadcasted_iota(jnp.int32, (1, span), 1)
        key_row = span_first + lax.broadcasted_iota(jnp.int32, (span, span), 0)

        def scores(t, top):
            key_pos = key_row - t * span
            allowed = (key_pos >= start) & (key_pos <= token)
            bias = jnp.where(allowed, 0.0, NEG)
            value = contract(k_all[t], queries, 1, 1) + jnp.concatenate([bias] * group, axis=1)
            s_all[t] = value
            return jnp.maximum(top, jnp.max(value, axis=0, keepdims=True))

        top = each(scores, jnp.full((1, rows), NEG, jnp.float32))

        def expons(t, total):
            value = jnp.exp2((s_all[t] - top) * (scale * LOG2E))
            s_all[t] = value
            return total + jnp.sum(value, axis=0, keepdims=True)

        total = each(expons, jnp.zeros((1, rows), jnp.float32))
        inverse = 1.0 / total

        def forward(t, carry):
            out, delta = carry
            weights = s_all[t] * inverse
            low = weights.astype(jnp.bfloat16)
            grad_weights = contract(v_all[t], grad_out, 1, 1)
            s_all[t] = weights
            p_all[t] = grad_weights
            delta = delta + jnp.sum(weights * grad_weights, axis=0, keepdims=True)
            out = out + contract(v_all[t], low, 0, 0)
            grad_value = contract(low, grad_out, 1, 0)
            store_term(t, 1, grad_value)
            return out, delta

        def store_term(t, which, value):
            if isinstance(t, int):
                if t == blocks - 1:
                    deep_refs[slot][which, 0] = value.astype(jnp.bfloat16)
                else:
                    rest_refs[slot][t, which, 0] = value
            else:
                @pl.when(t == blocks - 1)
                def _():
                    deep_refs[slot][which, 0] = value.astype(jnp.bfloat16)

                @pl.when(t < blocks - 1)
                def _():
                    rest_refs[slot][t, which, 0] = value

        out, delta = each(
            forward, (jnp.zeros((dim, rows), jnp.float32), jnp.zeros((1, rows), jnp.float32))
        )

        def backward(t, grad_query):
            low = (s_all[t] * (p_all[t] - delta)).astype(jnp.bfloat16)
            store_term(t, 0, contract(low, queries, 1, 0) * scale)
            return grad_query + contract(k_all[t], low, 0, 0)

        grad_query = each(backward, jnp.zeros((dim, rows), jnp.float32)) * scale
        for g in range(group):
            columns = slice(g * span, (g + 1) * span)
            o_ref[half, g] = out[:, columns].T.astype(jnp.bfloat16)
            dq_ref[half, g] = grad_query[:, columns].T.astype(jnp.bfloat16)


def attention_chunk(info, q_t, do_t, starts, kv_blocks, first_head, scale):
    blocks = len(kv_blocks[0])
    _, heads, span, dim = q_t.shape
    chunk = kv_blocks[0][0].shape[1]
    group = 4
    rows = group * span
    window = blocks - 1
    q_spec = pl.BlockSpec((2, group, span, dim), lambda m, info: (0, first_head + m, 0, 0))
    o_spec = pl.BlockSpec((2, group, span, dim), lambda m, info: (0, m, 0, 0))
    kv_spec = pl.BlockSpec((2, 1, span, dim), lambda m, info: (0, m, 0, 0))
    rest_spec = pl.BlockSpec((window, 2, 1, span, dim), lambda m, info: (0, 0, m, 0, 0))
    starts_spec = pl.BlockSpec((2, 1, span), lambda m, info: (0, 0, 0))
    deep = jax.ShapeDtypeStruct((2, chunk, span, dim), jnp.bfloat16)
    rest = jax.ShapeDtypeStruct((window, 2, chunk, span, dim), jnp.float32)
    out = jax.ShapeDtypeStruct((2, chunk * group, span, dim), jnp.bfloat16)
    macs = 2 * chunk * 5 * rows * blocks * span * dim
    return pl.pallas_call(
        functools.partial(attention_kernel, blocks, scale),
        grid_spec=pltpu.PrefetchScalarGridSpec(
            num_scalar_prefetch=1,
            grid=(chunk,),
            in_specs=[q_spec, q_spec, starts_spec] + [kv_spec] * (2 * blocks),
            out_specs=[o_spec, o_spec, kv_spec, kv_spec, rest_spec, rest_spec],
            scratch_shapes=[
                pltpu.VMEM((blocks, span, dim), jnp.bfloat16),
                pltpu.VMEM((blocks, span, dim), jnp.bfloat16),
                pltpu.VMEM((blocks, span, rows), jnp.float32),
                pltpu.VMEM((blocks, span, rows), jnp.float32),
            ],
        ),
        out_shape=[out, out, deep, deep, rest, rest],
        compiler_params=pltpu.CompilerParams(vmem_limit_bytes=48 * 1024 * 1024),
        cost_estimate=pl.CostEstimate(
            flops=2 * macs, bytes_accessed=8 * 1024 * 1024, transcendentals=0
        ),
        name="attention",
    )(info, q_t, do_t, starts, *kv_blocks[0], *kv_blocks[1])


def vmem_call(kernel, out_shape, macs, name, *args, aliases=None):
    whole = pl.BlockSpec(memory_space=pltpu.VMEM)
    moved = sum(a.size * a.dtype.itemsize for a in args[1:])
    return pl.pallas_call(
        kernel,
        in_specs=[pl.BlockSpec(memory_space=pltpu.SMEM)] + [whole] * (len(args) - 1),
        out_specs=[whole] * len(out_shape),
        out_shape=out_shape,
        input_output_aliases=aliases or {},
        compiler_params=pltpu.CompilerParams(vmem_limit_bytes=16 * 1024 * 1024),
        cost_estimate=pl.CostEstimate(flops=8 * macs, bytes_accessed=moved, transcendentals=0),
        name=name,
    )(*args)


def group_of(ref, half, m, group):
    return ref[half, pl.ds(m * group, group)].reshape(group * ref.shape[2], ref.shape[3])


def later_keys(span, group, dtype):
    row = lax.broadcasted_iota(jnp.int32, (span, span), 0)
    column = lax.broadcasted_iota(jnp.int32, (span, span), 1)
    return jnp.concatenate([(row > column).astype(jnp.float32).astype(dtype)] * group, axis=1)


def softmax_kernel(scale, first_head, info_ref, starts_ref, q_ref, do_ref, own_a, own_b, prev_a, prev_b, far_a, far_b, *refs):
    deep_refs = refs[-4:-2]
    low_ref, ds_ref = refs[-2:]
    heads, span, rows = low_ref.shape[1], low_ref.shape[3], low_ref.shape[4]
    group = rows // span
    row = lax.broadcasted_iota(jnp.int32, (span, span), 0)
    column = lax.broadcasted_iota(jnp.int32, (span, span), 1)
    far = row > column
    far_wide = jnp.concatenate([far] * group, axis=1)
    far_low = later_keys(span, group, jnp.bfloat16)
    slots = range(2)
    halves, bias, bias_prev = [], [], []
    for slot in slots:
        half = info_ref[slot]
        first = info_ref[2 + slot] * span
        start = starts_ref[half]
        position = jnp.where(far, first - 2 * span + row, first + row)
        halves.append(half)
        bias.append(jnp.where(position >= start, 0.0, NEG))
        bias_prev.append(jnp.where(first - span + row >= start, 0.0, NEG))
    kv_refs = ((own_a, prev_a, far_a), (own_b, prev_b, far_b))

    def one_head(step, carry):
        m = first_head + step
        queries = [group_of(q_ref, halves[i], m, group) for i in slots]
        grad_out = [group_of(do_ref, halves[i], m, group) for i in slots]
        scores, grads = [], []
        for i in slots:
            own, prev, far_kv = kv_refs[i]
            for which, rhs, result in ((0, queries[i], scores), (1, grad_out[i], grads)):
                stack = jnp.concatenate([own[m, which], prev[m, which], far_kv[step, which]], axis=0)
                result.append(contract(stack, rhs, 1, 1))
        near_s = [
            jnp.where(far_wide, x[2 * span :], x[:span]) + jnp.concatenate([bias[i]] * group, axis=1)
            for i, x in enumerate(scores)
        ]
        prev_s = [
            x[span : 2 * span] + jnp.concatenate([bias_prev[i]] * group, axis=1)
            for i, x in enumerate(scores)
        ]
        near_dp = [jnp.where(far_wide, x[2 * span :], x[:span]) for x in grads]
        prev_dp = [x[span : 2 * span] for x in grads]
        top = [jnp.max(jnp.maximum(near_s[i], prev_s[i]), axis=0, keepdims=True) for i in slots]
        near_e = [jnp.exp2((near_s[i] - top[i]) * (scale * LOG2E)) for i in slots]
        prev_e = [jnp.exp2((prev_s[i] - top[i]) * (scale * LOG2E)) for i in slots]
        inverse = [1.0 / jnp.sum(near_e[i] + prev_e[i], axis=0, keepdims=True) for i in slots]
        near_w = [near_e[i] * inverse[i] for i in slots]
        prev_w = [prev_e[i] * inverse[i] for i in slots]
        delta = [
            jnp.sum(near_w[i] * near_dp[i] + prev_w[i] * prev_dp[i], axis=0, keepdims=True)
            for i in slots
        ]
        near_low = [x.astype(jnp.bfloat16) for x in near_w]
        near_ds = [(near_w[i] * (near_dp[i] - delta[i])).astype(jnp.bfloat16) for i in slots]
        for i in slots:
            low_ref[i, m, 0] = near_low[i]
            ds_ref[i, m, 0] = near_ds[i]
            low_ref[i, m, 1] = prev_w[i].astype(jnp.bfloat16)
            ds_ref[i, m, 1] = (prev_w[i] * (prev_dp[i] - delta[i])).astype(jnp.bfloat16)
        for i in slots:
            key_term = contract(near_ds[i] * far_low, queries[i], 1, 0) * scale
            value_term = contract(near_low[i] * far_low, grad_out[i], 1, 0)
            deep_refs[i][m, 0] = key_term.astype(jnp.bfloat16)
            deep_refs[i][m, 1] = value_term.astype(jnp.bfloat16)
        return carry

    lax.fori_loop(0, far_a.shape[0], one_head, 0)


def rest_kernel(scale, info_ref, q_ref, do_ref, low_ref, ds_ref, *refs):
    own_kv, prev_kv, far_kv = refs[0:2], refs[2:4], refs[4:8]
    prev_refs = refs[8:10]
    late_refs, late_scratch, sems = refs[10:14], refs[14:18], refs[18]
    own_refs = late_scratch[:2]
    o_ref, dq_ref = late_scratch[2:]
    heads, _, span, rows = low_ref.shape[1:]
    chunk = far_kv[0].shape[0]
    group = rows // span
    far_low = later_keys(span, group, jnp.bfloat16)
    own_low = 1 - far_low

    def copies(m):
        blocks = (pl.ds(m, 1), pl.ds(m, 1)) + ((slice(None), pl.ds(m * group, group)),) * 2
        return [
            pltpu.make_async_copy(scratch.at[block], ref.at[block], sems.at[m, i])
            for i, (scratch, ref, block) in enumerate(zip(late_scratch, late_refs, blocks))
        ]

    def one_head(far_pair, first_head, step, carry):
        m = first_head + step
        for slot in range(2):
            half = info_ref[slot]
            own, prev, far = own_kv[slot], prev_kv[slot], far_pair[slot]
            queries = group_of(q_ref, half, m, group)
            grad_out = group_of(do_ref, half, m, group)
            low = low_ref[slot, m, 0]
            ds = ds_ref[slot, m, 0]
            low = jnp.concatenate([low_ref[slot, m, 1], low * own_low, low * far_low], axis=0)
            ds = jnp.concatenate([ds_ref[slot, m, 1], ds * own_low, ds * far_low], axis=0)
            grad_key = contract(ds[: 2 * span], queries, 1, 0) * scale
            grad_value = contract(low[: 2 * span], grad_out, 1, 0)
            prev_refs[slot][m, 0] = grad_key[:span]
            prev_refs[slot][m, 1] = grad_value[:span]
            own_refs[slot][m, 0] = grad_key[span:]
            own_refs[slot][m, 1] = grad_value[span:]
            keys = jnp.concatenate([prev[m, 0], own[m, 0], far[step, 0]], axis=0)
            values = jnp.concatenate([prev[m, 1], own[m, 1], far[step, 1]], axis=0)
            out = contract(values, low, 0, 0)
            grad_query = contract(keys, ds, 0, 0) * scale
            for g in range(group):
                columns = slice(g * span, (g + 1) * span)
                o_ref[half, m * group + g] = out[:, columns].T.astype(jnp.bfloat16)
                dq_ref[half, m * group + g] = grad_query[:, columns].T.astype(jnp.bfloat16)
        for copy in copies(m):
            copy.start()
        return carry

    for c in range(heads // chunk):
        lax.fori_loop(0, chunk, functools.partial(one_head, far_kv[2 * c : 2 * c + 2], c * chunk), 0)

    def finish(m, carry):
        for copy in copies(m):
            copy.wait()
        return carry

    lax.fori_loop(0, heads, finish, 0)


def rest_call(scale, macs, info, q_t, do_t, low, ds, own, prev, far):
    kv_heads = own[0].shape[0]
    whole = pl.BlockSpec(memory_space=pltpu.VMEM)
    outside = pl.BlockSpec(memory_space=pltpu.HBM)
    shape = jax.ShapeDtypeStruct
    terms = [shape(own[0].shape, jnp.float32)] * 4
    outs = [shape(q_t.shape, jnp.bfloat16)] * 2
    return pl.pallas_call(
        functools.partial(rest_kernel, scale),
        in_specs=[pl.BlockSpec(memory_space=pltpu.SMEM)] + [whole] * 12,
        out_specs=[whole] * 2 + [outside] * 4,
        out_shape=terms + outs,
        scratch_shapes=[pltpu.VMEM(x.shape, x.dtype) for x in terms[2:] + outs]
        + [pltpu.SemaphoreType.DMA((kv_heads, 4))],
        compiler_params=pltpu.CompilerParams(vmem_limit_bytes=16 * 1024 * 1024),
        cost_estimate=pl.CostEstimate(
            flops=8 * macs, bytes_accessed=8 * 1024 * 1024, transcendentals=0
        ),
        name="rest",
    )(info, q_t, do_t, low, ds, *own, *prev, *far)


def pack_kernel(info_ref, keys_ref, values_ref, own_a_ref, own_b_ref, raw, sems):
    copies = []
    for slot in (1, 0):
        for which, ref in enumerate((keys_ref, values_ref)):
            copies.append(
                pltpu.make_async_copy(
                    ref.at[info_ref[slot], 0], raw.at[slot, which], sems.at[slot, which]
                )
            )
            copies[-1].start()
    index = 0
    for slot in (1, 0):
        own_ref = (own_a_ref, own_b_ref)[slot]
        for which in range(2):
            copies[index].wait()
            index += 1
            tokens = jnp.swapaxes(raw[slot, which].astype(jnp.float32), 0, 1)
            own_ref[:, which] = tokens.astype(jnp.bfloat16)


def pack_call(info, keys, values):
    _, _, span, kv_heads, dim = keys.shape
    outside = pl.BlockSpec(memory_space=pl.ANY)
    whole = pl.BlockSpec(memory_space=pltpu.VMEM)
    return pl.pallas_call(
        pack_kernel,
        in_specs=[pl.BlockSpec(memory_space=pltpu.SMEM), outside, outside],
        out_specs=[whole] * 2,
        out_shape=[jax.ShapeDtypeStruct((kv_heads, 2, span, dim), jnp.bfloat16)] * 2,
        scratch_shapes=[
            pltpu.VMEM((2, 2, span, kv_heads, dim), jnp.bfloat16),
            pltpu.SemaphoreType.DMA((2, 2)),
        ],
        name="pack",
    )(info, keys, values)


def unpack_kernel(info_ref, own_a, own_b, last_a, last_b, grad_keys_ref, grad_values_ref):
    for slot, (own, last) in enumerate(((own_a, last_b), (own_b, last_a))):
        half = info_ref[slot]
        for which, ref in enumerate((grad_keys_ref, grad_values_ref)):
            total = own[:, which] + last[:, which].astype(jnp.float32)
            ref[half, 0] = jnp.swapaxes(total, 0, 1).astype(jnp.bfloat16)


def two_span_window(info, q_t, do_t, starts, own_a, own_b, pairs_a, pairs_b, scale):
    kv_heads, _, span, dim = own_a.shape
    heads = q_t.shape[1]
    rows = heads // kv_heads * span
    block = 2 * kv_heads * rows * span * dim
    chunk = kv_heads // 2
    shape = jax.ShapeDtypeStruct
    lows = [shape((2, kv_heads, 2, span, rows), jnp.bfloat16)] * 2
    deeps = [shape(own_a.shape, jnp.bfloat16)] * 2

    b1 = lax.ppermute(own_a, "seq", pairs_b)
    a1 = lax.ppermute(own_b, "seq", pairs_a)
    far = []
    for c in range(2):
        heads_of = slice(c * chunk, (c + 1) * chunk)
        far_b = lax.ppermute(a1[heads_of], "seq", pairs_b)
        far_a = lax.ppermute(b1[heads_of], "seq", pairs_a)
        far.append((far_a, far_b))
    held = ()
    for c in range(2):
        args = (info, starts, q_t, do_t, own_a, own_b, a1, b1, *far[c])
        held = vmem_call(
            functools.partial(softmax_kernel, scale, c * chunk), deeps + lows, 4 * block, "softmax",
            *args, *held, aliases={len(args) + i: i for i in range(len(held))},
        )
    deep_a, deep_b, low, ds = held
    from_a = lax.ppermute(deep_a, "seq", pairs_a)
    from_b = lax.ppermute(deep_b, "seq", pairs_b)
    prev_a, prev_b, own_term_a, own_term_b, out, dq = rest_call(
        scale, 10 * block, info, q_t, do_t, low, ds, (own_a, own_b), (a1, b1), (*far[0], *far[1])
    )
    next_a = (prev_a + from_b.astype(jnp.float32)).astype(jnp.bfloat16)
    next_b = (prev_b + from_a.astype(jnp.float32)).astype(jnp.bfloat16)
    last_a = lax.ppermute(next_a, "seq", pairs_a)
    last_b = lax.ppermute(next_b, "seq", pairs_b)
    grads = [shape((2, 1, span, kv_heads, dim), jnp.bfloat16)] * 2
    grad_keys, grad_values = vmem_call(
        unpack_kernel, grads, 1024, "unpack", info, own_term_a, own_term_b, last_a, last_b
    )
    return out, dq, grad_keys, grad_values


def any_window(info, q_t, do_t, starts, own_a, own_b, pairs_a, pairs_b, window, scale):
    kv_heads = own_a.shape[0]
    chunks = 2
    chunk = kv_heads // chunks
    parts = []
    for c in range(chunks):
        line_a = [jnp.swapaxes(own_a[c * chunk : (c + 1) * chunk], 0, 1)]
        line_b = [jnp.swapaxes(own_b[c * chunk : (c + 1) * chunk], 0, 1)]
        for _ in range(window):
            next_a = lax.ppermute(line_b[-1], "seq", pairs_a)
            next_b = lax.ppermute(line_a[-1], "seq", pairs_b)
            line_a.append(next_a)
            line_b.append(next_b)
        out, dq, now_a, now_b, rest_a, rest_b = attention_chunk(
            info, q_t, do_t, starts, (line_a, line_b), c * chunk, scale
        )
        for t in range(window - 1, -1, -1):
            from_a = lax.ppermute(now_a, "seq", pairs_a)
            from_b = lax.ppermute(now_b, "seq", pairs_b)
            now_a = (rest_a[t] + from_b.astype(jnp.float32)).astype(jnp.bfloat16)
            now_b = (rest_b[t] + from_a.astype(jnp.float32)).astype(jnp.bfloat16)
        parts.append((out, dq, now_a, now_b))
    out, dq, final_a, final_b = (jnp.concatenate(arrays, axis=1) for arrays in zip(*parts))
    final_a, final_b = jnp.swapaxes(final_a, 0, 1), jnp.swapaxes(final_b, 0, 1)
    halves = jnp.where(info[0] == 1, jnp.stack([final_b, final_a]), jnp.stack([final_a, final_b]))
    halves = jnp.transpose(halves, (2, 0, 3, 1, 4))[:, :, None]
    return out, dq, halves[0], halves[1]


def body(query, keys, values, grad_out, doc_starts):
    count = lax.axis_size("seq")
    device = lax.axis_index("seq")
    window = min(16, count // 2)
    span = query.shape[2]
    dim = query.shape[4]
    scale = dim ** (-0.5)
    pairs_a, pairs_b = swap_pairs(count)
    parity = device % 2

    half_a, half_b = 1 - parity, parity
    span_a = jnp.where(half_a == 0, device, 2 * count - 1 - device)
    info = jnp.stack([half_a, half_b, span_a, 2 * count - 1 - span_a]).astype(jnp.int32)
    own_a, own_b = pack_call(info, keys, values)
    q_t = jnp.transpose(query[:, 0], (0, 2, 1, 3))
    do_t = jnp.transpose(grad_out[:, 0], (0, 2, 1, 3))
    spans = jnp.stack([device, 2 * count - 1 - device])
    token = spans[:, None] * span + jnp.arange(span, dtype=jnp.int32)[None, :]
    below = doc_starts[None, None, :] <= token[:, :, None]
    starts = jnp.max(jnp.where(below, doc_starts[None, None, :], 0), axis=2)[:, None, :]

    if window == 2:
        out, dq, grad_keys, grad_values = two_span_window(
            info, q_t, do_t, starts, own_a, own_b, pairs_a, pairs_b, scale
        )
    else:
        out, dq, grad_keys, grad_values = any_window(
            info, q_t, do_t, starts, own_a, own_b, pairs_a, pairs_b, window, scale
        )
    out = jnp.transpose(out, (0, 2, 1, 3))[:, None]
    dq = jnp.transpose(dq, (0, 2, 1, 3))[:, None]
    return out, dq, grad_keys, grad_values


def solution(mesh):
    spec = P("batch", "seq", None, "head", None)
    return jax.shard_map(
        body,
        mesh=mesh,
        in_specs=(spec, spec, spec, spec, P("batch")),
        out_specs=(spec, spec, spec, spec),
        check_vma=False,
    )
```

```python
import functools

import jax
import jax.numpy as jnp
from jax import lax
from jax.experimental import pallas as pl
from jax.experimental.pallas import tpu as pltpu
from jax.sharding import PartitionSpec as P

LOG2E = 1.4426950408889634
NEG = -1e30


def swap_pairs(count):
    pairs_a = []
    for i in range(0, count - 1, 2):
        pairs_a += [(i, i + 1), (i + 1, i)]
    pairs_b = []
    for i in range(1, count - 1, 2):
        pairs_b += [(i, i + 1), (i + 1, i)]
    pairs_b.append((count - 1, count - 1))
    return pairs_a, pairs_b


def contract(lhs, rhs, lhs_dim, rhs_dim):
    return lax.dot_general(
        lhs, rhs, (((lhs_dim,), (rhs_dim,)), ((), ())), preferred_element_type=jnp.float32
    )


def attention_kernel(blocks, scale, info_ref, q_ref, do_ref, starts_ref, *refs):
    kv_refs = (refs[0:blocks], refs[blocks : 2 * blocks])
    o_ref, dq_ref = refs[2 * blocks : 2 * blocks + 2]
    deep_refs = refs[2 * blocks + 2 : 2 * blocks + 4]
    rest_refs = refs[2 * blocks + 4 : 2 * blocks + 6]
    k_all, v_all, s_all, p_all = refs[2 * blocks + 6 :]
    group, span, dim = q_ref.shape[1:]
    rows = group * span

    def each(body, init):
        if blocks <= 4:
            for t in range(blocks):
                init = body(t, init)
            return init
        return lax.fori_loop(0, blocks, body, init)

    for slot in range(2):
        half = info_ref[slot]
        span_first = info_ref[2 + slot] * span
        for t in range(blocks):
            k_all[t] = kv_refs[slot][t][0, 0]
            v_all[t] = kv_refs[slot][t][1, 0]
        queries = q_ref[half].reshape(rows, dim)
        grad_out = do_ref[half].reshape(rows, dim)
        start = starts_ref[half]
        token = span_first + lax.broadcasted_iota(jnp.int32, (1, span), 1)
        key_row = span_first + lax.broadcasted_iota(jnp.int32, (span, span), 0)

        def scores(t, top):
            key_pos = key_row - t * span
            allowed = (key_pos >= start) & (key_pos <= token)
            bias = jnp.where(allowed, 0.0, NEG)
            value = contract(k_all[t], queries, 1, 1) + jnp.concatenate([bias] * group, axis=1)
            s_all[t] = value
            return jnp.maximum(top, jnp.max(value, axis=0, keepdims=True))

        top = each(scores, jnp.full((1, rows), NEG, jnp.float32))

        def expons(t, total):
            value = jnp.exp2((s_all[t] - top) * (scale * LOG2E))
            s_all[t] = value
            return total + jnp.sum(value, axis=0, keepdims=True)

        total = each(expons, jnp.zeros((1, rows), jnp.float32))
        inverse = 1.0 / total

        def forward(t, carry):
            out, delta = carry
            weights = s_all[t] * inverse
            low = weights.astype(jnp.bfloat16)
            grad_weights = contract(v_all[t], grad_out, 1, 1)
            s_all[t] = weights
            p_all[t] = grad_weights
            delta = delta + jnp.sum(weights * grad_weights, axis=0, keepdims=True)
            out = out + contract(v_all[t], low, 0, 0)
            grad_value = contract(low, grad_out, 1, 0)
            store_term(t, 1, grad_value)
            return out, delta

        def store_term(t, which, value):
            if isinstance(t, int):
                if t == blocks - 1:
                    deep_refs[slot][which, 0] = value.astype(jnp.bfloat16)
                else:
                    rest_refs[slot][t, which, 0] = value
            else:
                @pl.when(t == blocks - 1)
                def _():
                    deep_refs[slot][which, 0] = value.astype(jnp.bfloat16)

                @pl.when(t < blocks - 1)
                def _():
                    rest_refs[slot][t, which, 0] = value

        out, delta = each(
            forward, (jnp.zeros((dim, rows), jnp.float32), jnp.zeros((1, rows), jnp.float32))
        )

        def backward(t, grad_query):
            low = (s_all[t] * (p_all[t] - delta)).astype(jnp.bfloat16)
            store_term(t, 0, contract(low, queries, 1, 0) * scale)
            return grad_query + contract(k_all[t], low, 0, 0)

        grad_query = each(backward, jnp.zeros((dim, rows), jnp.float32)) * scale
        for g in range(group):
            columns = slice(g * span, (g + 1) * span)
            o_ref[half, g] = out[:, columns].T.astype(jnp.bfloat16)
            dq_ref[half, g] = grad_query[:, columns].T.astype(jnp.bfloat16)


def attention_chunk(info, q_t, do_t, starts, kv_blocks, first_head, scale):
    blocks = len(kv_blocks[0])
    _, heads, span, dim = q_t.shape
    chunk = kv_blocks[0][0].shape[1]
    group = 4
    rows = group * span
    window = blocks - 1
    q_spec = pl.BlockSpec((2, group, span, dim), lambda m, info: (0, first_head + m, 0, 0))
    o_spec = pl.BlockSpec((2, group, span, dim), lambda m, info: (0, m, 0, 0))
    kv_spec = pl.BlockSpec((2, 1, span, dim), lambda m, info: (0, m, 0, 0))
    rest_spec = pl.BlockSpec((window, 2, 1, span, dim), lambda m, info: (0, 0, m, 0, 0))
    starts_spec = pl.BlockSpec((2, 1, span), lambda m, info: (0, 0, 0))
    deep = jax.ShapeDtypeStruct((2, chunk, span, dim), jnp.bfloat16)
    rest = jax.ShapeDtypeStruct((window, 2, chunk, span, dim), jnp.float32)
    out = jax.ShapeDtypeStruct((2, chunk * group, span, dim), jnp.bfloat16)
    macs = 2 * chunk * 5 * rows * blocks * span * dim
    return pl.pallas_call(
        functools.partial(attention_kernel, blocks, scale),
        grid_spec=pltpu.PrefetchScalarGridSpec(
            num_scalar_prefetch=1,
            grid=(chunk,),
            in_specs=[q_spec, q_spec, starts_spec] + [kv_spec] * (2 * blocks),
            out_specs=[o_spec, o_spec, kv_spec, kv_spec, rest_spec, rest_spec],
            scratch_shapes=[
                pltpu.VMEM((blocks, span, dim), jnp.bfloat16),
                pltpu.VMEM((blocks, span, dim), jnp.bfloat16),
                pltpu.VMEM((blocks, span, rows), jnp.float32),
                pltpu.VMEM((blocks, span, rows), jnp.float32),
            ],
        ),
        out_shape=[out, out, deep, deep, rest, rest],
        compiler_params=pltpu.CompilerParams(vmem_limit_bytes=48 * 1024 * 1024),
        cost_estimate=pl.CostEstimate(
            flops=2 * macs, bytes_accessed=8 * 1024 * 1024, transcendentals=0
        ),
        name="attention",
    )(info, q_t, do_t, starts, *kv_blocks[0], *kv_blocks[1])


def vmem_call(kernel, out_shape, macs, name, *args, aliases=None):
    whole = pl.BlockSpec(memory_space=pltpu.VMEM)
    moved = sum(a.size * a.dtype.itemsize for a in args[1:])
    return pl.pallas_call(
        kernel,
        in_specs=[pl.BlockSpec(memory_space=pltpu.SMEM)] + [whole] * (len(args) - 1),
        out_specs=[whole] * len(out_shape),
        out_shape=out_shape,
        input_output_aliases=aliases or {},
        compiler_params=pltpu.CompilerParams(vmem_limit_bytes=16 * 1024 * 1024),
        cost_estimate=pl.CostEstimate(flops=8 * macs, bytes_accessed=moved, transcendentals=0),
        name=name,
    )(*args)


def group_of(ref, half, m, group):
    return ref[half, pl.ds(m * group, group)].reshape(group * ref.shape[2], ref.shape[3])


def later_keys(span, group, dtype):
    row = lax.broadcasted_iota(jnp.int32, (span, span), 0)
    column = lax.broadcasted_iota(jnp.int32, (span, span), 1)
    return jnp.concatenate([(row > column).astype(jnp.float32).astype(dtype)] * group, axis=1)


def softmax_kernel(scale, first_head, info_ref, starts_ref, q_ref, do_ref, own_a, own_b, prev_a, prev_b, far_a, far_b, *refs):
    deep_refs = refs[-4:-2]
    low_ref, ds_ref = refs[-2:]
    heads, span, rows = low_ref.shape[1], low_ref.shape[3], low_ref.shape[4]
    group = rows // span
    row = lax.broadcasted_iota(jnp.int32, (span, span), 0)
    column = lax.broadcasted_iota(jnp.int32, (span, span), 1)
    far = row > column
    far_wide = jnp.concatenate([far] * group, axis=1)
    far_low = later_keys(span, group, jnp.bfloat16)
    slots = range(2)
    halves, bias, bias_prev = [], [], []
    for slot in slots:
        half = info_ref[slot]
        first = info_ref[2 + slot] * span
        start = starts_ref[half]
        position = jnp.where(far, first - 2 * span + row, first + row)
        halves.append(half)
        bias.append(jnp.where(position >= start, 0.0, NEG))
        bias_prev.append(jnp.where(first - span + row >= start, 0.0, NEG))
    kv_refs = ((own_a, prev_a, far_a), (own_b, prev_b, far_b))

    def one_head(step, carry):
        m = first_head + step
        queries = [group_of(q_ref, halves[i], m, group) for i in slots]
        grad_out = [group_of(do_ref, halves[i], m, group) for i in slots]
        scores, grads = [], []
        for i in slots:
            own, prev, far_kv = kv_refs[i]
            for which, rhs, result in ((0, queries[i], scores), (1, grad_out[i], grads)):
                stack = jnp.concatenate([own[m, which], prev[m, which], far_kv[step, which]], axis=0)
                result.append(contract(stack, rhs, 1, 1))
        near_s = [
            jnp.where(far_wide, x[2 * span :], x[:span]) + jnp.concatenate([bias[i]] * group, axis=1)
            for i, x in enumerate(scores)
        ]
        prev_s = [
            x[span : 2 * span] + jnp.concatenate([bias_prev[i]] * group, axis=1)
            for i, x in enumerate(scores)
        ]
        near_dp = [jnp.where(far_wide, x[2 * span :], x[:span]) for x in grads]
        prev_dp = [x[span : 2 * span] for x in grads]
        top = [jnp.max(jnp.maximum(near_s[i], prev_s[i]), axis=0, keepdims=True) for i in slots]
        near_e = [jnp.exp2((near_s[i] - top[i]) * (scale * LOG2E)) for i in slots]
        prev_e = [jnp.exp2((prev_s[i] - top[i]) * (scale * LOG2E)) for i in slots]
        inverse = [1.0 / jnp.sum(near_e[i] + prev_e[i], axis=0, keepdims=True) for i in slots]
        near_w = [near_e[i] * inverse[i] for i in slots]
        prev_w = [prev_e[i] * inverse[i] for i in slots]
        delta = [
            jnp.sum(near_w[i] * near_dp[i] + prev_w[i] * prev_dp[i], axis=0, keepdims=True)
            for i in slots
        ]
        near_low = [x.astype(jnp.bfloat16) for x in near_w]
        near_ds = [(near_w[i] * (near_dp[i] - delta[i])).astype(jnp.bfloat16) for i in slots]
        for i in slots:
            low_ref[i, m, 0] = near_low[i]
            ds_ref[i, m, 0] = near_ds[i]
            low_ref[i, m, 1] = prev_w[i].astype(jnp.bfloat16)
            ds_ref[i, m, 1] = (prev_w[i] * (prev_dp[i] - delta[i])).astype(jnp.bfloat16)
        for i in slots:
            key_term = contract(near_ds[i] * far_low, queries[i], 1, 0) * scale
            value_term = contract(near_low[i] * far_low, grad_out[i], 1, 0)
            deep_refs[i][m, 0] = key_term.astype(jnp.bfloat16)
            deep_refs[i][m, 1] = value_term.astype(jnp.bfloat16)
        return carry

    lax.fori_loop(0, far_a.shape[0], one_head, 0)


def rest_kernel(scale, info_ref, q_ref, do_ref, low_ref, ds_ref, *refs):
    own_kv, prev_kv, far_kv = refs[0:2], refs[2:4], refs[4:8]
    prev_refs = refs[8:10]
    late_refs, late_scratch, sems = refs[10:14], refs[14:18], refs[18]
    own_refs = late_scratch[:2]
    o_ref, dq_ref = late_scratch[2:]
    heads, _, span, rows = low_ref.shape[1:]
    chunk = far_kv[0].shape[0]
    group = rows // span
    far_low = later_keys(span, group, jnp.bfloat16)
    own_low = 1 - far_low

    def copies(m):
        blocks = (pl.ds(m, 1), pl.ds(m, 1)) + ((slice(None), pl.ds(m * group, group)),) * 2
        return [
            pltpu.make_async_copy(scratch.at[block], ref.at[block], sems.at[m, i])
            for i, (scratch, ref, block) in enumerate(zip(late_scratch, late_refs, blocks))
        ]

    def one_head(far_pair, first_head, step, carry):
        m = first_head + step
        for slot in range(2):
            half = info_ref[slot]
            own, prev, far = own_kv[slot], prev_kv[slot], far_pair[slot]
            queries = group_of(q_ref, half, m, group)
            grad_out = group_of(do_ref, half, m, group)
            low = low_ref[slot, m, 0]
            ds = ds_ref[slot, m, 0]
            low = jnp.concatenate([low_ref[slot, m, 1], low * own_low, low * far_low], axis=0)
            ds = jnp.concatenate([ds_ref[slot, m, 1], ds * own_low, ds * far_low], axis=0)
            grad_key = contract(ds[: 2 * span], queries, 1, 0) * scale
            grad_value = contract(low[: 2 * span], grad_out, 1, 0)
            prev_refs[slot][m, 0] = grad_key[:span]
            prev_refs[slot][m, 1] = grad_value[:span]
            own_refs[slot][m, 0] = grad_key[span:]
            own_refs[slot][m, 1] = grad_value[span:]
            keys = jnp.concatenate([prev[m, 0], own[m, 0], far[step, 0]], axis=0)
            values = jnp.concatenate([prev[m, 1], own[m, 1], far[step, 1]], axis=0)
            out = contract(values, low, 0, 0)
            grad_query = contract(keys, ds, 0, 0) * scale
            for g in range(group):
                columns = slice(g * span, (g + 1) * span)
                o_ref[half, m * group + g] = out[:, columns].T.astype(jnp.bfloat16)
                dq_ref[half, m * group + g] = grad_query[:, columns].T.astype(jnp.bfloat16)
        for copy in copies(m):
            copy.start()
        return carry

    for c in range(heads // chunk):
        lax.fori_loop(0, chunk, functools.partial(one_head, far_kv[2 * c : 2 * c + 2], c * chunk), 0)

    def finish(m, carry):
        for copy in copies(m):
            copy.wait()
        return carry

    lax.fori_loop(0, heads, finish, 0)


def rest_call(scale, macs, info, q_t, do_t, low, ds, own, prev, far):
    kv_heads = own[0].shape[0]
    whole = pl.BlockSpec(memory_space=pltpu.VMEM)
    outside = pl.BlockSpec(memory_space=pltpu.HBM)
    shape = jax.ShapeDtypeStruct
    terms = [shape(own[0].shape, jnp.float32)] * 4
    outs = [shape(q_t.shape, jnp.bfloat16)] * 2
    return pl.pallas_call(
        functools.partial(rest_kernel, scale),
        in_specs=[pl.BlockSpec(memory_space=pltpu.SMEM)] + [whole] * 12,
        out_specs=[whole] * 2 + [outside] * 4,
        out_shape=terms + outs,
        scratch_shapes=[pltpu.VMEM(x.shape, x.dtype) for x in terms[2:] + outs]
        + [pltpu.SemaphoreType.DMA((kv_heads, 4))],
        compiler_params=pltpu.CompilerParams(vmem_limit_bytes=16 * 1024 * 1024),
        cost_estimate=pl.CostEstimate(
            flops=8 * macs, bytes_accessed=8 * 1024 * 1024, transcendentals=0
        ),
        name="rest",
    )(info, q_t, do_t, low, ds, *own, *prev, *far)


def unpack_kernel(info_ref, own_a, own_b, last_a, last_b, grad_keys_ref, grad_values_ref):
    for slot, (own, last) in enumerate(((own_a, last_b), (own_b, last_a))):
        half = info_ref[slot]
        for which, ref in enumerate((grad_keys_ref, grad_values_ref)):
            total = own[:, which] + last[:, which].astype(jnp.float32)
            ref[half, 0] = jnp.swapaxes(total, 0, 1).astype(jnp.bfloat16)


def two_span_window(info, q_t, do_t, starts, own_a, own_b, pairs_a, pairs_b, scale):
    kv_heads, _, span, dim = own_a.shape
    heads = q_t.shape[1]
    rows = heads // kv_heads * span
    block = 2 * kv_heads * rows * span * dim
    chunk = kv_heads // 2
    shape = jax.ShapeDtypeStruct
    lows = [shape((2, kv_heads, 2, span, rows), jnp.bfloat16)] * 2
    deeps = [shape(own_a.shape, jnp.bfloat16)] * 2

    b1 = lax.ppermute(own_a, "seq", pairs_b)
    a1 = lax.ppermute(own_b, "seq", pairs_a)
    far = []
    for c in range(2):
        heads_of = slice(c * chunk, (c + 1) * chunk)
        far_b = lax.ppermute(a1[heads_of], "seq", pairs_b)
        far_a = lax.ppermute(b1[heads_of], "seq", pairs_a)
        far.append((far_a, far_b))
    held = ()
    for c in range(2):
        args = (info, starts, q_t, do_t, own_a, own_b, a1, b1, *far[c])
        held = vmem_call(
            functools.partial(softmax_kernel, scale, c * chunk), deeps + lows, 4 * block, "softmax",
            *args, *held, aliases={len(args) + i: i for i in range(len(held))},
        )
    deep_a, deep_b, low, ds = held
    from_a = lax.ppermute(deep_a, "seq", pairs_a)
    from_b = lax.ppermute(deep_b, "seq", pairs_b)
    prev_a, prev_b, own_term_a, own_term_b, out, dq = rest_call(
        scale, 10 * block, info, q_t, do_t, low, ds, (own_a, own_b), (a1, b1), (*far[0], *far[1])
    )
    from_a, from_b = lax.optimization_barrier((from_a, from_b))
    next_a = (prev_a + from_b.astype(jnp.float32)).astype(jnp.bfloat16)
    next_b = (prev_b + from_a.astype(jnp.float32)).astype(jnp.bfloat16)
    last_a = lax.ppermute(next_a, "seq", pairs_a)
    last_b = lax.ppermute(next_b, "seq", pairs_b)
    grads = [shape((2, 1, span, kv_heads, dim), jnp.bfloat16)] * 2
    grad_keys, grad_values = vmem_call(
        unpack_kernel, grads, 1024, "unpack", info, own_term_a, own_term_b, last_a, last_b
    )
    return out, dq, grad_keys, grad_values


def any_window(info, q_t, do_t, starts, own_a, own_b, pairs_a, pairs_b, window, scale):
    kv_heads = own_a.shape[0]
    chunks = 2
    chunk = kv_heads // chunks
    parts = []
    for c in range(chunks):
        line_a = [jnp.swapaxes(own_a[c * chunk : (c + 1) * chunk], 0, 1)]
        line_b = [jnp.swapaxes(own_b[c * chunk : (c + 1) * chunk], 0, 1)]
        for _ in range(window):
            next_a = lax.ppermute(line_b[-1], "seq", pairs_a)
            next_b = lax.ppermute(line_a[-1], "seq", pairs_b)
            line_a.append(next_a)
            line_b.append(next_b)
        out, dq, now_a, now_b, rest_a, rest_b = attention_chunk(
            info, q_t, do_t, starts, (line_a, line_b), c * chunk, scale
        )
        for t in range(window - 1, -1, -1):
            from_a = lax.ppermute(now_a, "seq", pairs_a)
            from_b = lax.ppermute(now_b, "seq", pairs_b)
            now_a = (rest_a[t] + from_b.astype(jnp.float32)).astype(jnp.bfloat16)
            now_b = (rest_b[t] + from_a.astype(jnp.float32)).astype(jnp.bfloat16)
        parts.append((out, dq, now_a, now_b))
    out, dq, final_a, final_b = (jnp.concatenate(arrays, axis=1) for arrays in zip(*parts))
    final_a, final_b = jnp.swapaxes(final_a, 0, 1), jnp.swapaxes(final_b, 0, 1)
    halves = jnp.where(info[0] == 1, jnp.stack([final_b, final_a]), jnp.stack([final_a, final_b]))
    halves = jnp.transpose(halves, (2, 0, 3, 1, 4))[:, :, None]
    return out, dq, halves[0], halves[1]


def body(query, keys, values, grad_out, doc_starts):
    count = lax.axis_size("seq")
    device = lax.axis_index("seq")
    window = min(16, count // 2)
    span = query.shape[2]
    dim = query.shape[4]
    scale = dim ** (-0.5)
    pairs_a, pairs_b = swap_pairs(count)
    parity = device % 2

    half_a, half_b = 1 - parity, parity
    span_a = jnp.where(half_a == 0, device, 2 * count - 1 - device)
    info = jnp.stack([half_a, half_b, span_a, 2 * count - 1 - span_a]).astype(jnp.int32)

    def payload(half):
        pair = [lax.dynamic_index_in_dim(x[:, 0], half, 0, keepdims=False) for x in (keys, values)]
        return jnp.transpose(jnp.stack(pair), (2, 0, 1, 3))

    own_a, own_b = payload(half_a), payload(half_b)
    q_t = jnp.transpose(query[:, 0], (0, 2, 1, 3))
    do_t = jnp.transpose(grad_out[:, 0], (0, 2, 1, 3))
    spans = jnp.stack([device, 2 * count - 1 - device])
    token = spans[:, None] * span + jnp.arange(span, dtype=jnp.int32)[None, :]
    below = doc_starts[None, None, :] <= token[:, :, None]
    starts = jnp.max(jnp.where(below, doc_starts[None, None, :], 0), axis=2)[:, None, :]

    if window == 2:
        out, dq, grad_keys, grad_values = two_span_window(
            info, q_t, do_t, starts, own_a, own_b, pairs_a, pairs_b, scale
        )
    else:
        out, dq, grad_keys, grad_values = any_window(
            info, q_t, do_t, starts, own_a, own_b, pairs_a, pairs_b, window, scale
        )
    out = jnp.transpose(out, (0, 2, 1, 3))[:, None]
    dq = jnp.transpose(dq, (0, 2, 1, 3))[:, None]
    return out, dq, grad_keys, grad_values


def solution(mesh):
    spec = P("batch", "seq", None, "head", None)
    return jax.shard_map(
        body,
        mesh=mesh,
        in_specs=(spec, spec, spec, spec, P("batch")),
        out_specs=(spec, spec, spec, spec),
        check_vma=False,
    )
```

```python
import functools

import jax
import jax.numpy as jnp
from jax import lax
from jax.experimental import pallas as pl
from jax.experimental.pallas import tpu as pltpu
from jax.sharding import PartitionSpec as P

LOG2E = 1.4426950408889634
NEG = -1e30


def swap_pairs(count):
    pairs_a = []
    for i in range(0, count - 1, 2):
        pairs_a += [(i, i + 1), (i + 1, i)]
    pairs_b = []
    for i in range(1, count - 1, 2):
        pairs_b += [(i, i + 1), (i + 1, i)]
    pairs_b.append((count - 1, count - 1))
    return pairs_a, pairs_b


def contract(lhs, rhs, lhs_dim, rhs_dim):
    return lax.dot_general(
        lhs, rhs, (((lhs_dim,), (rhs_dim,)), ((), ())), preferred_element_type=jnp.float32
    )


def attention_kernel(blocks, scale, info_ref, q_ref, do_ref, starts_ref, *refs):
    kv_refs = (refs[0:blocks], refs[blocks : 2 * blocks])
    o_ref, dq_ref = refs[2 * blocks : 2 * blocks + 2]
    deep_refs = refs[2 * blocks + 2 : 2 * blocks + 4]
    rest_refs = refs[2 * blocks + 4 : 2 * blocks + 6]
    k_all, v_all, s_all, p_all = refs[2 * blocks + 6 :]
    group, span, dim = q_ref.shape[1:]
    rows = group * span

    def each(body, init):
        if blocks <= 4:
            for t in range(blocks):
                init = body(t, init)
            return init
        return lax.fori_loop(0, blocks, body, init)

    for slot in range(2):
        half = info_ref[slot]
        span_first = info_ref[2 + slot] * span
        for t in range(blocks):
            k_all[t] = kv_refs[slot][t][0, 0]
            v_all[t] = kv_refs[slot][t][1, 0]
        queries = q_ref[half].reshape(rows, dim)
        grad_out = do_ref[half].reshape(rows, dim)
        start = starts_ref[half]
        token = span_first + lax.broadcasted_iota(jnp.int32, (1, span), 1)
        key_row = span_first + lax.broadcasted_iota(jnp.int32, (span, span), 0)

        def scores(t, top):
            key_pos = key_row - t * span
            allowed = (key_pos >= start) & (key_pos <= token)
            bias = jnp.where(allowed, 0.0, NEG)
            value = contract(k_all[t], queries, 1, 1) + jnp.concatenate([bias] * group, axis=1)
            s_all[t] = value
            return jnp.maximum(top, jnp.max(value, axis=0, keepdims=True))

        top = each(scores, jnp.full((1, rows), NEG, jnp.float32))

        def expons(t, total):
            value = jnp.exp2((s_all[t] - top) * (scale * LOG2E))
            s_all[t] = value
            return total + jnp.sum(value, axis=0, keepdims=True)

        total = each(expons, jnp.zeros((1, rows), jnp.float32))
        inverse = 1.0 / total

        def forward(t, carry):
            out, delta = carry
            weights = s_all[t] * inverse
            low = weights.astype(jnp.bfloat16)
            grad_weights = contract(v_all[t], grad_out, 1, 1)
            s_all[t] = weights
            p_all[t] = grad_weights
            delta = delta + jnp.sum(weights * grad_weights, axis=0, keepdims=True)
            out = out + contract(v_all[t], low, 0, 0)
            grad_value = contract(low, grad_out, 1, 0)
            store_term(t, 1, grad_value)
            return out, delta

        def store_term(t, which, value):
            if isinstance(t, int):
                if t == blocks - 1:
                    deep_refs[slot][which, 0] = value.astype(jnp.bfloat16)
                else:
                    rest_refs[slot][t, which, 0] = value
            else:
                @pl.when(t == blocks - 1)
                def _():
                    deep_refs[slot][which, 0] = value.astype(jnp.bfloat16)

                @pl.when(t < blocks - 1)
                def _():
                    rest_refs[slot][t, which, 0] = value

        out, delta = each(
            forward, (jnp.zeros((dim, rows), jnp.float32), jnp.zeros((1, rows), jnp.float32))
        )

        def backward(t, grad_query):
            low = (s_all[t] * (p_all[t] - delta)).astype(jnp.bfloat16)
            store_term(t, 0, contract(low, queries, 1, 0) * scale)
            return grad_query + contract(k_all[t], low, 0, 0)

        grad_query = each(backward, jnp.zeros((dim, rows), jnp.float32)) * scale
        for g in range(group):
            columns = slice(g * span, (g + 1) * span)
            o_ref[half, g] = out[:, columns].T.astype(jnp.bfloat16)
            dq_ref[half, g] = grad_query[:, columns].T.astype(jnp.bfloat16)


def attention_chunk(info, q_t, do_t, starts, kv_blocks, first_head, scale):
    blocks = len(kv_blocks[0])
    _, heads, span, dim = q_t.shape
    chunk = kv_blocks[0][0].shape[1]
    group = 4
    rows = group * span
    window = blocks - 1
    q_spec = pl.BlockSpec((2, group, span, dim), lambda m, info: (0, first_head + m, 0, 0))
    o_spec = pl.BlockSpec((2, group, span, dim), lambda m, info: (0, m, 0, 0))
    kv_spec = pl.BlockSpec((2, 1, span, dim), lambda m, info: (0, m, 0, 0))
    rest_spec = pl.BlockSpec((window, 2, 1, span, dim), lambda m, info: (0, 0, m, 0, 0))
    starts_spec = pl.BlockSpec((2, 1, span), lambda m, info: (0, 0, 0))
    deep = jax.ShapeDtypeStruct((2, chunk, span, dim), jnp.bfloat16)
    rest = jax.ShapeDtypeStruct((window, 2, chunk, span, dim), jnp.float32)
    out = jax.ShapeDtypeStruct((2, chunk * group, span, dim), jnp.bfloat16)
    macs = 2 * chunk * 5 * rows * blocks * span * dim
    return pl.pallas_call(
        functools.partial(attention_kernel, blocks, scale),
        grid_spec=pltpu.PrefetchScalarGridSpec(
            num_scalar_prefetch=1,
            grid=(chunk,),
            in_specs=[q_spec, q_spec, starts_spec] + [kv_spec] * (2 * blocks),
            out_specs=[o_spec, o_spec, kv_spec, kv_spec, rest_spec, rest_spec],
            scratch_shapes=[
                pltpu.VMEM((blocks, span, dim), jnp.bfloat16),
                pltpu.VMEM((blocks, span, dim), jnp.bfloat16),
                pltpu.VMEM((blocks, span, rows), jnp.float32),
                pltpu.VMEM((blocks, span, rows), jnp.float32),
            ],
        ),
        out_shape=[out, out, deep, deep, rest, rest],
        compiler_params=pltpu.CompilerParams(vmem_limit_bytes=48 * 1024 * 1024),
        cost_estimate=pl.CostEstimate(
            flops=2 * macs, bytes_accessed=8 * 1024 * 1024, transcendentals=0
        ),
        name="attention",
    )(info, q_t, do_t, starts, *kv_blocks[0], *kv_blocks[1])


def vmem_call(kernel, out_shape, macs, name, *args, aliases=None):
    whole = pl.BlockSpec(memory_space=pltpu.VMEM)
    moved = sum(a.size * a.dtype.itemsize for a in args[1:])
    return pl.pallas_call(
        kernel,
        in_specs=[pl.BlockSpec(memory_space=pltpu.SMEM)] + [whole] * (len(args) - 1),
        out_specs=[whole] * len(out_shape),
        out_shape=out_shape,
        input_output_aliases=aliases or {},
        compiler_params=pltpu.CompilerParams(vmem_limit_bytes=16 * 1024 * 1024),
        cost_estimate=pl.CostEstimate(flops=8 * macs, bytes_accessed=moved, transcendentals=0),
        name=name,
    )(*args)


def group_of(ref, half, m, group):
    return ref[half, pl.ds(m * group, group)].reshape(group * ref.shape[2], ref.shape[3])


def near_kernel(scale, info_ref, starts_ref, q_ref, do_ref, own_a, own_b, prev_a, prev_b, e_ref, dp_ref, stats_ref):
    heads, span, rows = e_ref.shape[1], e_ref.shape[2] // 2, e_ref.shape[3]
    group = rows // span
    row = lax.broadcasted_iota(jnp.int32, (span, span), 0)
    column = lax.broadcasted_iota(jnp.int32, (span, span), 1)
    slots = range(2)
    kv_refs = ((prev_a, own_a), (prev_b, own_b))
    halves, biases = [], []
    for slot in slots:
        half = info_ref[slot]
        first = info_ref[2 + slot] * span
        start = starts_ref[half]
        prev_bias = jnp.where(first - span + row >= start, 0.0, NEG)
        own_bias = jnp.where((first + row >= start) & (row <= column), 0.0, NEG)
        halves.append(half)
        biases.append(jnp.concatenate([prev_bias, own_bias], axis=0))

    def one_head(m, carry):
        scores, grads = [], []
        for i in slots:
            keys, values = (
                jnp.concatenate([ref[m, which] for ref in kv_refs[i]], axis=0) for which in range(2)
            )
            scores.append(contract(keys, group_of(q_ref, halves[i], m, group), 1, 1))
            grads.append(contract(values, group_of(do_ref, halves[i], m, group), 1, 1))
        scores = [x + jnp.concatenate([biases[i]] * group, axis=1) for i, x in enumerate(scores)]
        top = [jnp.max(x, axis=0, keepdims=True) for x in scores]
        e = [jnp.exp2((scores[i] - top[i]) * (scale * LOG2E)) for i in slots]
        for i in slots:
            e_ref[i, m] = e[i]
            dp_ref[i, m] = grads[i]
            stats_ref[i, m, 0:1] = top[i]
            stats_ref[i, m, 1:2] = jnp.sum(e[i], axis=0, keepdims=True)
            stats_ref[i, m, 2:3] = jnp.sum(e[i] * grads[i], axis=0, keepdims=True)
        return carry

    lax.fori_loop(0, heads, one_head, 0)


def far_kernel(scale, info_ref, starts_ref, q_ref, do_ref, far_a, far_b, stats_ref, deep_a, deep_b, low_ref, ds_ref, norm_ref):
    heads, span, rows = low_ref.shape[1:]
    group = rows // span
    row = lax.broadcasted_iota(jnp.int32, (span, span), 0)
    column = lax.broadcasted_iota(jnp.int32, (span, span), 1)
    factor = scale * LOG2E
    slots = range(2)
    halves, biases = [], []
    for slot in slots:
        half = info_ref[slot]
        first = info_ref[2 + slot] * span
        allowed = (first - 2 * span + row >= starts_ref[half]) & (row > column)
        halves.append(half)
        biases.append(jnp.where(allowed, 0.0, NEG))
    far_refs = (far_a, far_b)
    deep_refs = (deep_a, deep_b)

    def one_head(m, carry):
        queries = [group_of(q_ref, halves[i], m, group) for i in slots]
        grad_out = [group_of(do_ref, halves[i], m, group) for i in slots]
        scores = [
            contract(far_refs[i][m, 0], queries[i], 1, 1)
            + jnp.concatenate([biases[i]] * group, axis=1)
            for i in slots
        ]
        grads = [contract(far_refs[i][m, 1], grad_out[i], 1, 1) for i in slots]
        near_top = [stats_ref[i, m, 0:1] for i in slots]
        top = [
            jnp.maximum(near_top[i], jnp.max(scores[i], axis=0, keepdims=True)) for i in slots
        ]
        near = [jnp.exp2((near_top[i] - top[i]) * factor) for i in slots]
        e = [jnp.exp2((scores[i] - top[i]) * factor) for i in slots]
        inverse = [
            1.0 / (near[i] * stats_ref[i, m, 1:2] + jnp.sum(e[i], axis=0, keepdims=True))
            for i in slots
        ]
        delta = [
            (
                near[i] * stats_ref[i, m, 2:3]
                + jnp.sum(e[i] * grads[i], axis=0, keepdims=True)
            )
            * inverse[i]
            for i in slots
        ]
        weights = [e[i] * inverse[i] for i in slots]
        low = [x.astype(jnp.bfloat16) for x in weights]
        ds = [(weights[i] * (grads[i] - delta[i])).astype(jnp.bfloat16) for i in slots]
        for i in slots:
            low_ref[i, m] = low[i]
            ds_ref[i, m] = ds[i]
            norm_ref[i, m, 0:1] = near[i] * inverse[i]
            norm_ref[i, m, 1:2] = delta[i]
        for i in slots:
            deep_refs[i][m, 0] = (contract(ds[i], queries[i], 1, 0) * scale).astype(jnp.bfloat16)
            deep_refs[i][m, 1] = contract(low[i], grad_out[i], 1, 0).astype(jnp.bfloat16)
        return carry

    lax.fori_loop(0, heads, one_head, 0)


def rest_kernel(scale, info_ref, q_ref, do_ref, e_ref, dp_ref, *refs):
    far_low, far_ds, norm = refs[:3]
    own_kv, prev_kv, far_kv = refs[3:5], refs[5:7], refs[7:9]
    prev_refs, own_refs = refs[9:11], refs[11:13]
    o_ref, dq_ref = refs[13:]
    heads, span, rows = e_ref.shape[1], e_ref.shape[2] // 2, e_ref.shape[3]
    group = rows // span
    slots = range(2)

    def one_head(m, carry):
        queries = [group_of(q_ref, info_ref[i], m, group) for i in slots]
        grad_out = [group_of(do_ref, info_ref[i], m, group) for i in slots]
        low, ds = [], []
        for i in slots:
            weights = e_ref[i, m] * norm[i, m, 0:1]
            near_ds = (weights * (dp_ref[i, m] - norm[i, m, 1:2])).astype(jnp.bfloat16)
            low.append(jnp.concatenate([weights.astype(jnp.bfloat16), far_low[i, m]], axis=0))
            ds.append(jnp.concatenate([near_ds, far_ds[i, m]], axis=0))
        for i in slots:
            grad_key = contract(ds[i][: 2 * span], queries[i], 1, 0) * scale
            grad_value = contract(low[i][: 2 * span], grad_out[i], 1, 0)
            prev_refs[i][m, 0] = grad_key[:span]
            prev_refs[i][m, 1] = grad_value[:span]
            own_refs[i][m, 0] = grad_key[span:]
            own_refs[i][m, 1] = grad_value[span:]
        for i in slots:
            half = info_ref[i]
            keys, values = (
                jnp.concatenate([ref[i][m, which] for ref in (prev_kv, own_kv, far_kv)], axis=0)
                for which in range(2)
            )
            out = contract(values, low[i], 0, 0)
            grad_query = contract(keys, ds[i], 0, 0) * scale
            for g in range(group):
                columns = slice(g * span, (g + 1) * span)
                o_ref[half, m * group + g] = out[:, columns].T.astype(jnp.bfloat16)
                dq_ref[half, m * group + g] = grad_query[:, columns].T.astype(jnp.bfloat16)
        return carry

    lax.fori_loop(0, heads, one_head, 0)


def unpack_kernel(info_ref, own_a, own_b, last_a, last_b, grad_keys_ref, grad_values_ref):
    for slot, (own, last) in enumerate(((own_a, last_b), (own_b, last_a))):
        half = info_ref[slot]
        for which, ref in enumerate((grad_keys_ref, grad_values_ref)):
            total = own[:, which] + last[:, which].astype(jnp.float32)
            ref[half, 0] = jnp.swapaxes(total, 0, 1).astype(jnp.bfloat16)


def by_half(info, final_a, final_b):
    even = info[:1].reshape((1,) * (final_a.ndim + 1)) == 1
    halves = jnp.where(even, jnp.stack([final_b, final_a]), jnp.stack([final_a, final_b]))
    halves = jnp.transpose(halves, (2, 0, 3, 1, 4))[:, :, None]
    return halves[0], halves[1]


def two_span_window(info, q_t, do_t, starts, own_a, own_b, pairs_a, pairs_b, scale):
    kv_heads, _, span, dim = own_a.shape
    heads = q_t.shape[1]
    rows = heads // kv_heads * span
    block = 2 * kv_heads * rows * span * dim
    shape = jax.ShapeDtypeStruct
    near = [shape((2, kv_heads, 2 * span, rows), jnp.float32)] * 2
    near.append(shape((2, kv_heads, 8, rows), jnp.float32))
    deeps = [shape(own_a.shape, jnp.bfloat16)] * 2
    lows = [shape((2, kv_heads, span, rows), jnp.bfloat16)] * 2
    norm = shape((2, kv_heads, 8, rows), jnp.float32)
    terms = [shape(own_a.shape, jnp.float32)] * 4
    outs = [shape(q_t.shape, jnp.bfloat16)] * 2

    b1 = lax.ppermute(own_a, "seq", pairs_b)
    a1 = lax.ppermute(own_b, "seq", pairs_a)
    b2 = lax.ppermute(a1, "seq", pairs_b)
    a2 = lax.ppermute(b1, "seq", pairs_a)
    e, dp, stats = vmem_call(
        functools.partial(near_kernel, scale), near, 4 * block, "near",
        info, starts, q_t, do_t, own_a, own_b, a1, b1,
    )
    deep_a, deep_b, *far_parts = vmem_call(
        functools.partial(far_kernel, scale), deeps + lows + [norm], 2 * block, "far",
        info, starts, q_t, do_t, a2, b2, stats,
    )
    from_a = lax.ppermute(deep_a, "seq", pairs_a)
    from_b = lax.ppermute(deep_b, "seq", pairs_b)
    prev_a, prev_b, own_term_a, own_term_b, out, dq = vmem_call(
        functools.partial(rest_kernel, scale), terms + outs, 10 * block, "rest",
        info, q_t, do_t, e, dp, *far_parts, own_a, own_b, a1, b1, a2, b2,
    )
    from_a, from_b = lax.optimization_barrier((from_a, from_b))
    next_a = (prev_a + from_b.astype(jnp.float32)).astype(jnp.bfloat16)
    next_b = (prev_b + from_a.astype(jnp.float32)).astype(jnp.bfloat16)
    last_a = lax.ppermute(next_a, "seq", pairs_a)
    last_b = lax.ppermute(next_b, "seq", pairs_b)
    grads = [shape((2, 1, span, kv_heads, dim), jnp.bfloat16)] * 2
    grad_keys, grad_values = vmem_call(
        unpack_kernel, grads, 1024, "unpack", info, own_term_a, own_term_b, last_a, last_b
    )
    return out, dq, grad_keys, grad_values


def any_window(info, q_t, do_t, starts, own_a, own_b, pairs_a, pairs_b, window, scale):
    kv_heads = own_a.shape[0]
    chunks = 2
    chunk = kv_heads // chunks
    parts = []
    for c in range(chunks):
        line_a = [jnp.swapaxes(own_a[c * chunk : (c + 1) * chunk], 0, 1)]
        line_b = [jnp.swapaxes(own_b[c * chunk : (c + 1) * chunk], 0, 1)]
        for _ in range(window):
            next_a = lax.ppermute(line_b[-1], "seq", pairs_a)
            next_b = lax.ppermute(line_a[-1], "seq", pairs_b)
            line_a.append(next_a)
            line_b.append(next_b)
        out, dq, now_a, now_b, rest_a, rest_b = attention_chunk(
            info, q_t, do_t, starts, (line_a, line_b), c * chunk, scale
        )
        for t in range(window - 1, -1, -1):
            from_a = lax.ppermute(now_a, "seq", pairs_a)
            from_b = lax.ppermute(now_b, "seq", pairs_b)
            now_a = (rest_a[t] + from_b.astype(jnp.float32)).astype(jnp.bfloat16)
            now_b = (rest_b[t] + from_a.astype(jnp.float32)).astype(jnp.bfloat16)
        parts.append((out, dq, now_a, now_b))
    out, dq, final_a, final_b = (jnp.concatenate(arrays, axis=1) for arrays in zip(*parts))
    return out, dq, *by_half(info, jnp.swapaxes(final_a, 0, 1), jnp.swapaxes(final_b, 0, 1))


def body(query, keys, values, grad_out, doc_starts):
    count = lax.axis_size("seq")
    device = lax.axis_index("seq")
    window = min(16, count // 2)
    span = query.shape[2]
    dim = query.shape[4]
    scale = dim ** (-0.5)
    pairs_a, pairs_b = swap_pairs(count)
    parity = device % 2

    half_a, half_b = 1 - parity, parity
    span_a = jnp.where(half_a == 0, device, 2 * count - 1 - device)
    info = jnp.stack([half_a, half_b, span_a, 2 * count - 1 - span_a]).astype(jnp.int32)

    def payload(half):
        pair = [lax.dynamic_index_in_dim(x[:, 0], half, 0, keepdims=False) for x in (keys, values)]
        return jnp.transpose(jnp.stack(pair), (2, 0, 1, 3))

    own_a, own_b = payload(half_a), payload(half_b)
    q_t = jnp.transpose(query[:, 0], (0, 2, 1, 3))
    do_t = jnp.transpose(grad_out[:, 0], (0, 2, 1, 3))
    spans = jnp.stack([device, 2 * count - 1 - device])
    token = spans[:, None] * span + jnp.arange(span, dtype=jnp.int32)[None, :]
    below = doc_starts[None, None, :] <= token[:, :, None]
    starts = jnp.max(jnp.where(below, doc_starts[None, None, :], 0), axis=2)[:, None, :]

    if window == 2:
        out, dq, grad_keys, grad_values = two_span_window(
            info, q_t, do_t, starts, own_a, own_b, pairs_a, pairs_b, scale
        )
    else:
        out, dq, grad_keys, grad_values = any_window(
            info, q_t, do_t, starts, own_a, own_b, pairs_a, pairs_b, window, scale
        )
    out = jnp.transpose(out, (0, 2, 1, 3))[:, None]
    dq = jnp.transpose(dq, (0, 2, 1, 3))[:, None]
    return out, dq, grad_keys, grad_values


def solution(mesh):
    spec = P("batch", "seq", None, "head", None)
    return jax.shard_map(
        body,
        mesh=mesh,
        in_specs=(spec, spec, spec, spec, P("batch")),
        out_specs=(spec, spec, spec, spec),
        check_vma=False,
    )
```

```python
import functools

import jax
import jax.numpy as jnp
from jax import lax
from jax.experimental import pallas as pl
from jax.experimental.pallas import tpu as pltpu
from jax.sharding import PartitionSpec as P

LOG2E = 1.4426950408889634
NEG = -1e30


def swap_pairs(count):
    pairs_a = []
    for i in range(0, count - 1, 2):
        pairs_a += [(i, i + 1), (i + 1, i)]
    pairs_b = []
    for i in range(1, count - 1, 2):
        pairs_b += [(i, i + 1), (i + 1, i)]
    pairs_b.append((count - 1, count - 1))
    return pairs_a, pairs_b


def contract(lhs, rhs, lhs_dim, rhs_dim):
    return lax.dot_general(
        lhs, rhs, (((lhs_dim,), (rhs_dim,)), ((), ())), preferred_element_type=jnp.float32
    )


def attention_kernel(blocks, scale, info_ref, q_ref, do_ref, starts_ref, *refs):
    kv_refs = (refs[0:blocks], refs[blocks : 2 * blocks])
    o_ref, dq_ref = refs[2 * blocks : 2 * blocks + 2]
    deep_refs = refs[2 * blocks + 2 : 2 * blocks + 4]
    rest_refs = refs[2 * blocks + 4 : 2 * blocks + 6]
    k_all, v_all, s_all, p_all = refs[2 * blocks + 6 :]
    group, span, dim = q_ref.shape[1:]
    rows = group * span

    def each(body, init):
        if blocks <= 4:
            for t in range(blocks):
                init = body(t, init)
            return init
        return lax.fori_loop(0, blocks, body, init)

    for slot in range(2):
        half = info_ref[slot]
        span_first = info_ref[2 + slot] * span
        for t in range(blocks):
            k_all[t] = kv_refs[slot][t][0, 0]
            v_all[t] = kv_refs[slot][t][1, 0]
        queries = q_ref[half].reshape(rows, dim)
        grad_out = do_ref[half].reshape(rows, dim)
        start = starts_ref[half]
        token = span_first + lax.broadcasted_iota(jnp.int32, (1, span), 1)
        key_row = span_first + lax.broadcasted_iota(jnp.int32, (span, span), 0)

        def scores(t, top):
            key_pos = key_row - t * span
            allowed = (key_pos >= start) & (key_pos <= token)
            bias = jnp.where(allowed, 0.0, NEG)
            value = contract(k_all[t], queries, 1, 1) + jnp.concatenate([bias] * group, axis=1)
            s_all[t] = value
            return jnp.maximum(top, jnp.max(value, axis=0, keepdims=True))

        top = each(scores, jnp.full((1, rows), NEG, jnp.float32))

        def expons(t, total):
            value = jnp.exp2((s_all[t] - top) * (scale * LOG2E))
            s_all[t] = value
            return total + jnp.sum(value, axis=0, keepdims=True)

        total = each(expons, jnp.zeros((1, rows), jnp.float32))
        inverse = 1.0 / total

        def forward(t, carry):
            out, delta = carry
            weights = s_all[t] * inverse
            low = weights.astype(jnp.bfloat16)
            grad_weights = contract(v_all[t], grad_out, 1, 1)
            s_all[t] = weights
            p_all[t] = grad_weights
            delta = delta + jnp.sum(weights * grad_weights, axis=0, keepdims=True)
            out = out + contract(v_all[t], low, 0, 0)
            grad_value = contract(low, grad_out, 1, 0)
            store_term(t, 1, grad_value)
            return out, delta

        def store_term(t, which, value):
            if isinstance(t, int):
                if t == blocks - 1:
                    deep_refs[slot][which, 0] = value.astype(jnp.bfloat16)
                else:
                    rest_refs[slot][t, which, 0] = value
            else:
                @pl.when(t == blocks - 1)
                def _():
                    deep_refs[slot][which, 0] = value.astype(jnp.bfloat16)

                @pl.when(t < blocks - 1)
                def _():
                    rest_refs[slot][t, which, 0] = value

        out, delta = each(
            forward, (jnp.zeros((dim, rows), jnp.float32), jnp.zeros((1, rows), jnp.float32))
        )

        def backward(t, grad_query):
            low = (s_all[t] * (p_all[t] - delta)).astype(jnp.bfloat16)
            store_term(t, 0, contract(low, queries, 1, 0) * scale)
            return grad_query + contract(k_all[t], low, 0, 0)

        grad_query = each(backward, jnp.zeros((dim, rows), jnp.float32)) * scale
        for g in range(group):
            columns = slice(g * span, (g + 1) * span)
            o_ref[half, g] = out[:, columns].T.astype(jnp.bfloat16)
            dq_ref[half, g] = grad_query[:, columns].T.astype(jnp.bfloat16)


def attention_chunk(info, q_t, do_t, starts, kv_blocks, first_head, scale):
    blocks = len(kv_blocks[0])
    _, heads, span, dim = q_t.shape
    chunk = kv_blocks[0][0].shape[1]
    group = 4
    rows = group * span
    window = blocks - 1
    q_spec = pl.BlockSpec((2, group, span, dim), lambda m, info: (0, first_head + m, 0, 0))
    o_spec = pl.BlockSpec((2, group, span, dim), lambda m, info: (0, m, 0, 0))
    kv_spec = pl.BlockSpec((2, 1, span, dim), lambda m, info: (0, m, 0, 0))
    rest_spec = pl.BlockSpec((window, 2, 1, span, dim), lambda m, info: (0, 0, m, 0, 0))
    starts_spec = pl.BlockSpec((2, 1, span), lambda m, info: (0, 0, 0))
    deep = jax.ShapeDtypeStruct((2, chunk, span, dim), jnp.bfloat16)
    rest = jax.ShapeDtypeStruct((window, 2, chunk, span, dim), jnp.float32)
    out = jax.ShapeDtypeStruct((2, chunk * group, span, dim), jnp.bfloat16)
    macs = 2 * chunk * 5 * rows * blocks * span * dim
    return pl.pallas_call(
        functools.partial(attention_kernel, blocks, scale),
        grid_spec=pltpu.PrefetchScalarGridSpec(
            num_scalar_prefetch=1,
            grid=(chunk,),
            in_specs=[q_spec, q_spec, starts_spec] + [kv_spec] * (2 * blocks),
            out_specs=[o_spec, o_spec, kv_spec, kv_spec, rest_spec, rest_spec],
            scratch_shapes=[
                pltpu.VMEM((blocks, span, dim), jnp.bfloat16),
                pltpu.VMEM((blocks, span, dim), jnp.bfloat16),
                pltpu.VMEM((blocks, span, rows), jnp.float32),
                pltpu.VMEM((blocks, span, rows), jnp.float32),
            ],
        ),
        out_shape=[out, out, deep, deep, rest, rest],
        compiler_params=pltpu.CompilerParams(vmem_limit_bytes=48 * 1024 * 1024),
        cost_estimate=pl.CostEstimate(
            flops=2 * macs, bytes_accessed=8 * 1024 * 1024, transcendentals=0
        ),
        name="attention",
    )(info, q_t, do_t, starts, *kv_blocks[0], *kv_blocks[1])


def vmem_call(kernel, out_shape, macs, name, *args, aliases=None):
    whole = pl.BlockSpec(memory_space=pltpu.VMEM)
    moved = sum(a.size * a.dtype.itemsize for a in args[1:])
    return pl.pallas_call(
        kernel,
        in_specs=[pl.BlockSpec(memory_space=pltpu.SMEM)] + [whole] * (len(args) - 1),
        out_specs=[whole] * len(out_shape),
        out_shape=out_shape,
        input_output_aliases=aliases or {},
        compiler_params=pltpu.CompilerParams(vmem_limit_bytes=16 * 1024 * 1024),
        cost_estimate=pl.CostEstimate(flops=8 * macs, bytes_accessed=moved, transcendentals=0),
        name=name,
    )(*args)


def group_of(ref, half, m, group):
    return ref[half, pl.ds(m * group, group)].reshape(group * ref.shape[2], ref.shape[3])


def near_kernel(scale, info_ref, starts_ref, q_ref, do_ref, own_a, own_b, prev_a, prev_b, e_ref, dp_ref, stats_ref):
    heads, span, rows = e_ref.shape[1], e_ref.shape[2] // 2, e_ref.shape[3]
    group = rows // span
    row = lax.broadcasted_iota(jnp.int32, (span, span), 0)
    column = lax.broadcasted_iota(jnp.int32, (span, span), 1)
    slots = range(2)
    kv_refs = ((prev_a, own_a), (prev_b, own_b))
    halves, biases = [], []
    for slot in slots:
        half = info_ref[slot]
        first = info_ref[2 + slot] * span
        start = starts_ref[half]
        prev_bias = jnp.where(first - span + row >= start, 0.0, NEG)
        own_bias = jnp.where((first + row >= start) & (row <= column), 0.0, NEG)
        halves.append(half)
        biases.append(jnp.concatenate([prev_bias, own_bias], axis=0))

    def one_head(m, carry):
        scores, grads = [], []
        for i in slots:
            keys, values = (
                jnp.concatenate([ref[m, which] for ref in kv_refs[i]], axis=0) for which in range(2)
            )
            scores.append(contract(keys, group_of(q_ref, halves[i], m, group), 1, 1))
            grads.append(contract(values, group_of(do_ref, halves[i], m, group), 1, 1))
        scores = [x + jnp.concatenate([biases[i]] * group, axis=1) for i, x in enumerate(scores)]
        top = [jnp.max(x, axis=0, keepdims=True) for x in scores]
        e = [jnp.exp2((scores[i] - top[i]) * (scale * LOG2E)) for i in slots]
        for i in slots:
            e_ref[i, m] = e[i]
            dp_ref[i, m] = grads[i]
            stats_ref[i, m, 0:1] = top[i]
            stats_ref[i, m, 1:2] = jnp.sum(e[i], axis=0, keepdims=True)
            stats_ref[i, m, 2:3] = jnp.sum(e[i] * grads[i], axis=0, keepdims=True)
        return carry

    lax.fori_loop(0, heads, one_head, 0)


def far_kernel(scale, info_ref, starts_ref, q_ref, do_ref, far_a, far_b, stats_ref, deep_a, deep_b, low_ref, ds_ref, norm_ref):
    heads, span, rows = low_ref.shape[1:]
    group = rows // span
    row = lax.broadcasted_iota(jnp.int32, (span, span), 0)
    column = lax.broadcasted_iota(jnp.int32, (span, span), 1)
    factor = scale * LOG2E
    slots = range(2)
    halves, biases = [], []
    for slot in slots:
        half = info_ref[slot]
        first = info_ref[2 + slot] * span
        allowed = (first - 2 * span + row >= starts_ref[half]) & (row > column)
        halves.append(half)
        biases.append(jnp.where(allowed, 0.0, NEG))
    far_refs = (far_a, far_b)
    deep_refs = (deep_a, deep_b)

    def one_head(m, carry):
        queries = [group_of(q_ref, halves[i], m, group) for i in slots]
        grad_out = [group_of(do_ref, halves[i], m, group) for i in slots]
        scores = [
            contract(far_refs[i][m, 0], queries[i], 1, 1)
            + jnp.concatenate([biases[i]] * group, axis=1)
            for i in slots
        ]
        grads = [contract(far_refs[i][m, 1], grad_out[i], 1, 1) for i in slots]
        near_top = [stats_ref[i, m, 0:1] for i in slots]
        top = [
            jnp.maximum(near_top[i], jnp.max(scores[i], axis=0, keepdims=True)) for i in slots
        ]
        near = [jnp.exp2((near_top[i] - top[i]) * factor) for i in slots]
        e = [jnp.exp2((scores[i] - top[i]) * factor) for i in slots]
        inverse = [
            1.0 / (near[i] * stats_ref[i, m, 1:2] + jnp.sum(e[i], axis=0, keepdims=True))
            for i in slots
        ]
        delta = [
            (
                near[i] * stats_ref[i, m, 2:3]
                + jnp.sum(e[i] * grads[i], axis=0, keepdims=True)
            )
            * inverse[i]
            for i in slots
        ]
        weights = [e[i] * inverse[i] for i in slots]
        low = [x.astype(jnp.bfloat16) for x in weights]
        ds = [(weights[i] * (grads[i] - delta[i])).astype(jnp.bfloat16) for i in slots]
        for i in slots:
            low_ref[i, m] = low[i]
            ds_ref[i, m] = ds[i]
            norm_ref[i, m, 0:1] = near[i] * inverse[i]
            norm_ref[i, m, 1:2] = delta[i]
        for i in slots:
            deep_refs[i][m, 0] = (contract(ds[i], queries[i], 1, 0) * scale).astype(jnp.bfloat16)
            deep_refs[i][m, 1] = contract(low[i], grad_out[i], 1, 0).astype(jnp.bfloat16)
        return carry

    lax.fori_loop(0, heads, one_head, 0, unroll=True)


def rest_kernel(scale, info_ref, q_ref, do_ref, e_ref, dp_ref, *refs):
    far_low, far_ds, norm = refs[:3]
    own_kv, prev_kv, far_kv = refs[3:5], refs[5:7], refs[7:9]
    prev_refs, own_refs = refs[9:11], refs[11:13]
    o_ref, dq_ref = refs[13:]
    heads, span, rows = e_ref.shape[1], e_ref.shape[2] // 2, e_ref.shape[3]
    group = rows // span
    slots = range(2)

    def one_head(m, carry):
        queries = [group_of(q_ref, info_ref[i], m, group) for i in slots]
        grad_out = [group_of(do_ref, info_ref[i], m, group) for i in slots]
        low, ds = [], []
        for i in slots:
            weights = e_ref[i, m] * norm[i, m, 0:1]
            near_ds = (weights * (dp_ref[i, m] - norm[i, m, 1:2])).astype(jnp.bfloat16)
            low.append(jnp.concatenate([weights.astype(jnp.bfloat16), far_low[i, m]], axis=0))
            ds.append(jnp.concatenate([near_ds, far_ds[i, m]], axis=0))
        for i in slots:
            grad_key = contract(ds[i][: 2 * span], queries[i], 1, 0) * scale
            grad_value = contract(low[i][: 2 * span], grad_out[i], 1, 0)
            prev_refs[i][m, 0] = grad_key[:span]
            prev_refs[i][m, 1] = grad_value[:span]
            own_refs[i][m, 0] = grad_key[span:]
            own_refs[i][m, 1] = grad_value[span:]
        for i in slots:
            half = info_ref[i]
            keys, values = (
                jnp.concatenate([ref[i][m, which] for ref in (prev_kv, own_kv, far_kv)], axis=0)
                for which in range(2)
            )
            out = contract(values, low[i], 0, 0)
            grad_query = contract(keys, ds[i], 0, 0) * scale
            for g in range(group):
                columns = slice(g * span, (g + 1) * span)
                o_ref[half, m * group + g] = out[:, columns].T.astype(jnp.bfloat16)
                dq_ref[half, m * group + g] = grad_query[:, columns].T.astype(jnp.bfloat16)
        return carry

    lax.fori_loop(0, heads, one_head, 0)


def unpack_kernel(info_ref, own_a, own_b, last_a, last_b, grad_keys_ref, grad_values_ref):
    for slot, (own, last) in enumerate(((own_a, last_b), (own_b, last_a))):
        half = info_ref[slot]
        for which, ref in enumerate((grad_keys_ref, grad_values_ref)):
            total = own[:, which] + last[:, which].astype(jnp.float32)
            ref[half, 0] = jnp.swapaxes(total, 0, 1).astype(jnp.bfloat16)


def by_half(info, final_a, final_b):
    even = info[:1].reshape((1,) * (final_a.ndim + 1)) == 1
    halves = jnp.where(even, jnp.stack([final_b, final_a]), jnp.stack([final_a, final_b]))
    halves = jnp.transpose(halves, (2, 0, 3, 1, 4))[:, :, None]
    return halves[0], halves[1]


def two_span_window(info, q_t, do_t, starts, own_a, own_b, pairs_a, pairs_b, scale):
    kv_heads, _, span, dim = own_a.shape
    heads = q_t.shape[1]
    rows = heads // kv_heads * span
    block = 2 * kv_heads * rows * span * dim
    shape = jax.ShapeDtypeStruct
    near = [shape((2, kv_heads, 2 * span, rows), jnp.float32)] * 2
    near.append(shape((2, kv_heads, 8, rows), jnp.float32))
    deeps = [shape(own_a.shape, jnp.bfloat16)] * 2
    lows = [shape((2, kv_heads, span, rows), jnp.bfloat16)] * 2
    norm = shape((2, kv_heads, 8, rows), jnp.float32)
    terms = [shape(own_a.shape, jnp.float32)] * 4
    outs = [shape(q_t.shape, jnp.bfloat16)] * 2

    b1 = lax.ppermute(own_a, "seq", pairs_b)
    a1 = lax.ppermute(own_b, "seq", pairs_a)
    b2 = lax.ppermute(a1, "seq", pairs_b)
    a2 = lax.ppermute(b1, "seq", pairs_a)
    e, dp, stats = vmem_call(
        functools.partial(near_kernel, scale), near, 4 * block, "near",
        info, starts, q_t, do_t, own_a, own_b, a1, b1,
    )
    deep_a, deep_b, *far_parts = vmem_call(
        functools.partial(far_kernel, scale), deeps + lows + [norm], 2 * block, "far",
        info, starts, q_t, do_t, a2, b2, stats,
    )
    from_a = lax.ppermute(deep_a, "seq", pairs_a)
    from_b = lax.ppermute(deep_b, "seq", pairs_b)
    prev_a, prev_b, own_term_a, own_term_b, out, dq = vmem_call(
        functools.partial(rest_kernel, scale), terms + outs, 10 * block, "rest",
        info, q_t, do_t, e, dp, *far_parts, own_a, own_b, a1, b1, a2, b2,
    )
    from_a, from_b = lax.optimization_barrier((from_a, from_b))
    next_a = (prev_a + from_b.astype(jnp.float32)).astype(jnp.bfloat16)
    next_b = (prev_b + from_a.astype(jnp.float32)).astype(jnp.bfloat16)
    last_a = lax.ppermute(next_a, "seq", pairs_a)
    last_b = lax.ppermute(next_b, "seq", pairs_b)
    grads = [shape((2, 1, span, kv_heads, dim), jnp.bfloat16)] * 2
    grad_keys, grad_values = vmem_call(
        unpack_kernel, grads, 1024, "unpack", info, own_term_a, own_term_b, last_a, last_b
    )
    return out, dq, grad_keys, grad_values


def any_window(info, q_t, do_t, starts, own_a, own_b, pairs_a, pairs_b, window, scale):
    kv_heads = own_a.shape[0]
    chunks = 2
    chunk = kv_heads // chunks
    parts = []
    for c in range(chunks):
        line_a = [jnp.swapaxes(own_a[c * chunk : (c + 1) * chunk], 0, 1)]
        line_b = [jnp.swapaxes(own_b[c * chunk : (c + 1) * chunk], 0, 1)]
        for _ in range(window):
            next_a = lax.ppermute(line_b[-1], "seq", pairs_a)
            next_b = lax.ppermute(line_a[-1], "seq", pairs_b)
            line_a.append(next_a)
            line_b.append(next_b)
        out, dq, now_a, now_b, rest_a, rest_b = attention_chunk(
            info, q_t, do_t, starts, (line_a, line_b), c * chunk, scale
        )
        for t in range(window - 1, -1, -1):
            from_a = lax.ppermute(now_a, "seq", pairs_a)
            from_b = lax.ppermute(now_b, "seq", pairs_b)
            now_a = (rest_a[t] + from_b.astype(jnp.float32)).astype(jnp.bfloat16)
            now_b = (rest_b[t] + from_a.astype(jnp.float32)).astype(jnp.bfloat16)
        parts.append((out, dq, now_a, now_b))
    out, dq, final_a, final_b = (jnp.concatenate(arrays, axis=1) for arrays in zip(*parts))
    return out, dq, *by_half(info, jnp.swapaxes(final_a, 0, 1), jnp.swapaxes(final_b, 0, 1))


def body(query, keys, values, grad_out, doc_starts):
    count = lax.axis_size("seq")
    device = lax.axis_index("seq")
    window = min(16, count // 2)
    span = query.shape[2]
    dim = query.shape[4]
    scale = dim ** (-0.5)
    pairs_a, pairs_b = swap_pairs(count)
    parity = device % 2

    half_a, half_b = 1 - parity, parity
    span_a = jnp.where(half_a == 0, device, 2 * count - 1 - device)
    info = jnp.stack([half_a, half_b, span_a, 2 * count - 1 - span_a]).astype(jnp.int32)

    def payload(half):
        pair = [lax.dynamic_index_in_dim(x[:, 0], half, 0, keepdims=False) for x in (keys, values)]
        return jnp.transpose(jnp.stack(pair), (2, 0, 1, 3))

    own_a, own_b = payload(half_a), payload(half_b)
    q_t = jnp.transpose(query[:, 0], (0, 2, 1, 3))
    do_t = jnp.transpose(grad_out[:, 0], (0, 2, 1, 3))
    spans = jnp.stack([device, 2 * count - 1 - device])
    token = spans[:, None] * span + jnp.arange(span, dtype=jnp.int32)[None, :]
    below = doc_starts[None, None, :] <= token[:, :, None]
    starts = jnp.max(jnp.where(below, doc_starts[None, None, :], 0), axis=2)[:, None, :]

    if window == 2:
        out, dq, grad_keys, grad_values = two_span_window(
            info, q_t, do_t, starts, own_a, own_b, pairs_a, pairs_b, scale
        )
    else:
        out, dq, grad_keys, grad_values = any_window(
            info, q_t, do_t, starts, own_a, own_b, pairs_a, pairs_b, window, scale
        )
    out = jnp.transpose(out, (0, 2, 1, 3))[:, None]
    dq = jnp.transpose(dq, (0, 2, 1, 3))[:, None]
    return out, dq, grad_keys, grad_values


def solution(mesh):
    spec = P("batch", "seq", None, "head", None)
    return jax.shard_map(
        body,
        mesh=mesh,
        in_specs=(spec, spec, spec, spec, P("batch")),
        out_specs=(spec, spec, spec, spec),
        check_vma=False,
    )
```

```python
import functools

import jax
import jax.numpy as jnp
from jax import lax
from jax.experimental import pallas as pl
from jax.experimental.pallas import tpu as pltpu
from jax.sharding import PartitionSpec as P

LOG2E = 1.4426950408889634
NEG = -1e30


def swap_pairs(count):
    pairs_a = []
    for i in range(0, count - 1, 2):
        pairs_a += [(i, i + 1), (i + 1, i)]
    pairs_b = []
    for i in range(1, count - 1, 2):
        pairs_b += [(i, i + 1), (i + 1, i)]
    pairs_b.append((count - 1, count - 1))
    return pairs_a, pairs_b


def everyone_swaps(pairs, count, batch):
    swaps = []
    for b in range(batch):
        lone = set(range(count)) - {source for source, target in pairs if source != target}
        swaps += [(i * batch + b, j * batch + b) for i, j in pairs if i != j]
        swaps += [(i * batch + b, i * batch + (b ^ 1)) for i in sorted(lone)]
    return swaps


def contract(lhs, rhs, lhs_dim, rhs_dim):
    return lax.dot_general(
        lhs, rhs, (((lhs_dim,), (rhs_dim,)), ((), ())), preferred_element_type=jnp.float32
    )


def attention_kernel(blocks, scale, info_ref, q_ref, do_ref, starts_ref, *refs):
    kv_refs = (refs[0:blocks], refs[blocks : 2 * blocks])
    o_ref, dq_ref = refs[2 * blocks : 2 * blocks + 2]
    deep_refs = refs[2 * blocks + 2 : 2 * blocks + 4]
    rest_refs = refs[2 * blocks + 4 : 2 * blocks + 6]
    k_all, v_all, s_all, p_all = refs[2 * blocks + 6 :]
    group, span, dim = q_ref.shape[1:]
    rows = group * span

    def each(body, init):
        if blocks <= 4:
            for t in range(blocks):
                init = body(t, init)
            return init
        return lax.fori_loop(0, blocks, body, init)

    for slot in range(2):
        half = info_ref[slot]
        span_first = info_ref[2 + slot] * span
        for t in range(blocks):
            k_all[t] = kv_refs[slot][t][0, 0]
            v_all[t] = kv_refs[slot][t][1, 0]
        queries = q_ref[half].reshape(rows, dim)
        grad_out = do_ref[half].reshape(rows, dim)
        start = starts_ref[half]
        token = span_first + lax.broadcasted_iota(jnp.int32, (1, span), 1)
        key_row = span_first + lax.broadcasted_iota(jnp.int32, (span, span), 0)

        def scores(t, top):
            key_pos = key_row - t * span
            allowed = (key_pos >= start) & (key_pos <= token)
            bias = jnp.where(allowed, 0.0, NEG)
            value = contract(k_all[t], queries, 1, 1) + jnp.concatenate([bias] * group, axis=1)
            s_all[t] = value
            return jnp.maximum(top, jnp.max(value, axis=0, keepdims=True))

        top = each(scores, jnp.full((1, rows), NEG, jnp.float32))

        def expons(t, total):
            value = jnp.exp2((s_all[t] - top) * (scale * LOG2E))
            s_all[t] = value
            return total + jnp.sum(value, axis=0, keepdims=True)

        total = each(expons, jnp.zeros((1, rows), jnp.float32))
        inverse = 1.0 / total

        def forward(t, carry):
            out, delta = carry
            weights = s_all[t] * inverse
            low = weights.astype(jnp.bfloat16)
            grad_weights = contract(v_all[t], grad_out, 1, 1)
            s_all[t] = weights
            p_all[t] = grad_weights
            delta = delta + jnp.sum(weights * grad_weights, axis=0, keepdims=True)
            out = out + contract(v_all[t], low, 0, 0)
            grad_value = contract(low, grad_out, 1, 0)
            store_term(t, 1, grad_value)
            return out, delta

        def store_term(t, which, value):
            if isinstance(t, int):
                if t == blocks - 1:
                    deep_refs[slot][which, 0] = value.astype(jnp.bfloat16)
                else:
                    rest_refs[slot][t, which, 0] = value
            else:
                @pl.when(t == blocks - 1)
                def _():
                    deep_refs[slot][which, 0] = value.astype(jnp.bfloat16)

                @pl.when(t < blocks - 1)
                def _():
                    rest_refs[slot][t, which, 0] = value

        out, delta = each(
            forward, (jnp.zeros((dim, rows), jnp.float32), jnp.zeros((1, rows), jnp.float32))
        )

        def backward(t, grad_query):
            low = (s_all[t] * (p_all[t] - delta)).astype(jnp.bfloat16)
            store_term(t, 0, contract(low, queries, 1, 0) * scale)
            return grad_query + contract(k_all[t], low, 0, 0)

        grad_query = each(backward, jnp.zeros((dim, rows), jnp.float32)) * scale
        for g in range(group):
            columns = slice(g * span, (g + 1) * span)
            o_ref[half, g] = out[:, columns].T.astype(jnp.bfloat16)
            dq_ref[half, g] = grad_query[:, columns].T.astype(jnp.bfloat16)


def attention_chunk(info, q_t, do_t, starts, kv_blocks, first_head, scale):
    blocks = len(kv_blocks[0])
    _, heads, span, dim = q_t.shape
    chunk = kv_blocks[0][0].shape[1]
    group = 4
    rows = group * span
    window = blocks - 1
    q_spec = pl.BlockSpec((2, group, span, dim), lambda m, info: (0, first_head + m, 0, 0))
    o_spec = pl.BlockSpec((2, group, span, dim), lambda m, info: (0, m, 0, 0))
    kv_spec = pl.BlockSpec((2, 1, span, dim), lambda m, info: (0, m, 0, 0))
    rest_spec = pl.BlockSpec((window, 2, 1, span, dim), lambda m, info: (0, 0, m, 0, 0))
    starts_spec = pl.BlockSpec((2, 1, span), lambda m, info: (0, 0, 0))
    deep = jax.ShapeDtypeStruct((2, chunk, span, dim), jnp.bfloat16)
    rest = jax.ShapeDtypeStruct((window, 2, chunk, span, dim), jnp.float32)
    out = jax.ShapeDtypeStruct((2, chunk * group, span, dim), jnp.bfloat16)
    macs = 2 * chunk * 5 * rows * blocks * span * dim
    return pl.pallas_call(
        functools.partial(attention_kernel, blocks, scale),
        grid_spec=pltpu.PrefetchScalarGridSpec(
            num_scalar_prefetch=1,
            grid=(chunk,),
            in_specs=[q_spec, q_spec, starts_spec] + [kv_spec] * (2 * blocks),
            out_specs=[o_spec, o_spec, kv_spec, kv_spec, rest_spec, rest_spec],
            scratch_shapes=[
                pltpu.VMEM((blocks, span, dim), jnp.bfloat16),
                pltpu.VMEM((blocks, span, dim), jnp.bfloat16),
                pltpu.VMEM((blocks, span, rows), jnp.float32),
                pltpu.VMEM((blocks, span, rows), jnp.float32),
            ],
        ),
        out_shape=[out, out, deep, deep, rest, rest],
        compiler_params=pltpu.CompilerParams(vmem_limit_bytes=48 * 1024 * 1024),
        cost_estimate=pl.CostEstimate(
            flops=2 * macs, bytes_accessed=8 * 1024 * 1024, transcendentals=0
        ),
        name="attention",
    )(info, q_t, do_t, starts, *kv_blocks[0], *kv_blocks[1])


def vmem_call(kernel, out_shape, macs, name, *args, aliases=None):
    whole = pl.BlockSpec(memory_space=pltpu.VMEM)
    moved = sum(a.size * a.dtype.itemsize for a in args)
    return pl.pallas_call(
        kernel,
        in_specs=[whole] * len(args),
        out_specs=[whole] * len(out_shape),
        out_shape=out_shape,
        input_output_aliases=aliases or {},
        compiler_params=pltpu.CompilerParams(vmem_limit_bytes=16 * 1024 * 1024),
        cost_estimate=pl.CostEstimate(flops=8 * macs, bytes_accessed=moved, transcendentals=0),
        name=name,
    )(*args)


def place(count):
    device = lax.axis_index("seq")
    half_a = 1 - device % 2
    span_a = jnp.where(half_a == 0, device, 2 * count - 1 - device)
    return (half_a, 1 - half_a), (span_a, 2 * count - 1 - span_a), device == count - 1


def group_of(ref, half, m, group):
    return ref[half, pl.ds(m * group, group)].reshape(group * ref.shape[2], ref.shape[3])


def near_kernel(scale, count, starts_ref, q_ref, do_ref, own_a, own_b, prev_a, prev_b, e_ref, dp_ref, stats_ref):
    heads, span, rows = e_ref.shape[1], e_ref.shape[2] // 2, e_ref.shape[3]
    group = rows // span
    row = lax.broadcasted_iota(jnp.int32, (span, span), 0)
    column = lax.broadcasted_iota(jnp.int32, (span, span), 1)
    slots = range(2)
    kv_refs = ((prev_a, own_a), (prev_b, own_b))
    halves, spans, _ = place(count)
    biases = []
    for slot in slots:
        first = spans[slot] * span
        start = starts_ref[spans[slot]]
        prev_bias = jnp.where(first - span + row >= start, 0.0, NEG)
        own_bias = jnp.where((first + row >= start) & (row <= column), 0.0, NEG)
        biases.append(jnp.concatenate([prev_bias, own_bias], axis=0))

    def one_head(m, carry):
        scores, grads = [], []
        for i in slots:
            keys, values = (
                jnp.concatenate([ref[m, which] for ref in kv_refs[i]], axis=0) for which in range(2)
            )
            scores.append(contract(keys, group_of(q_ref, halves[i], m, group), 1, 1))
            grads.append(contract(values, group_of(do_ref, halves[i], m, group), 1, 1))
        scores = [x + jnp.concatenate([biases[i]] * group, axis=1) for i, x in enumerate(scores)]
        top = [jnp.max(x, axis=0, keepdims=True) for x in scores]
        e = [jnp.exp2((scores[i] - top[i]) * (scale * LOG2E)) for i in slots]
        for i in slots:
            e_ref[i, m] = e[i]
            dp_ref[i, m] = grads[i]
            stats_ref[i, m, 0:1] = top[i]
            stats_ref[i, m, 1:2] = jnp.sum(e[i], axis=0, keepdims=True)
            stats_ref[i, m, 2:3] = jnp.sum(e[i] * grads[i], axis=0, keepdims=True)
        return carry

    lax.fori_loop(0, heads, one_head, 0)


def far_kernel(scale, count, starts_ref, q_ref, do_ref, prev_a, far_a, far_b, stats_ref, deep_a, deep_b,
               low_ref, ds_ref, norm_ref):
    heads, span, rows = low_ref.shape[1:]
    group = rows // span
    row = lax.broadcasted_iota(jnp.int32, (span, span), 0)
    column = lax.broadcasted_iota(jnp.int32, (span, span), 1)
    factor = scale * LOG2E
    slots = range(2)
    halves, spans, is_last = place(count)
    biases = []
    for slot in slots:
        first = spans[slot] * span
        allowed = (first - 2 * span + row >= starts_ref[spans[slot]]) & (row > column)
        biases.append(jnp.where(allowed, 0.0, NEG))
    deep_refs = (deep_a, deep_b)


    def one_head(m, carry):
        far_kv = [far_a[m], jnp.where(is_last, prev_a[m], far_b[m])]
        queries = [group_of(q_ref, halves[i], m, group) for i in slots]
        grad_out = [group_of(do_ref, halves[i], m, group) for i in slots]
        scores = [
            contract(far_kv[i][0], queries[i], 1, 1)
            + jnp.concatenate([biases[i]] * group, axis=1)
            for i in slots
        ]
        grads = [contract(far_kv[i][1], grad_out[i], 1, 1) for i in slots]
        near_top = [stats_ref[i, m, 0:1] for i in slots]
        top = [
            jnp.maximum(near_top[i], jnp.max(scores[i], axis=0, keepdims=True)) for i in slots
        ]
        near = [jnp.exp2((near_top[i] - top[i]) * factor) for i in slots]
        e = [jnp.exp2((scores[i] - top[i]) * factor) for i in slots]
        inverse = [
            1.0 / (near[i] * stats_ref[i, m, 1:2] + jnp.sum(e[i], axis=0, keepdims=True))
            for i in slots
        ]
        delta = [
            (
                near[i] * stats_ref[i, m, 2:3]
                + jnp.sum(e[i] * grads[i], axis=0, keepdims=True)
            )
            * inverse[i]
            for i in slots
        ]
        weights = [e[i] * inverse[i] for i in slots]
        low = [x.astype(jnp.bfloat16) for x in weights]
        ds = [(weights[i] * (grads[i] - delta[i])).astype(jnp.bfloat16) for i in slots]
        for i in slots:
            low_ref[i, m] = low[i]
            ds_ref[i, m] = ds[i]
            norm_ref[i, m, 0:1] = near[i] * inverse[i]
            norm_ref[i, m, 1:2] = delta[i]
        for i in slots:
            deep_refs[i][m, 0] = (contract(ds[i], queries[i], 1, 0) * scale).astype(jnp.bfloat16)
            deep_refs[i][m, 1] = contract(low[i], grad_out[i], 1, 0).astype(jnp.bfloat16)
        return carry

    lax.fori_loop(0, heads, one_head, 0, unroll=True)


def rest_kernel(scale, count, q_ref, do_ref, e_ref, dp_ref, *refs):
    far_low, far_ds, norm = refs[:3]
    own_kv, prev_kv, far_kv = refs[3:5], refs[5:7], refs[7:9]
    prev_refs, own_refs = refs[9:11], refs[11:13]
    o_ref, dq_ref = refs[13:]
    halves, _, is_last = place(count)
    heads, span, rows = e_ref.shape[1], e_ref.shape[2] // 2, e_ref.shape[3]
    group = rows // span
    slots = range(2)

    def one_head(m, carry):
        queries = [group_of(q_ref, halves[i], m, group) for i in slots]
        grad_out = [group_of(do_ref, halves[i], m, group) for i in slots]
        low, ds = [], []
        for i in slots:
            weights = e_ref[i, m] * norm[i, m, 0:1]
            near_ds = (weights * (dp_ref[i, m] - norm[i, m, 1:2])).astype(jnp.bfloat16)
            low.append(jnp.concatenate([weights.astype(jnp.bfloat16), far_low[i, m]], axis=0))
            ds.append(jnp.concatenate([near_ds, far_ds[i, m]], axis=0))
        for i in slots:
            grad_key = contract(ds[i][: 2 * span], queries[i], 1, 0) * scale
            grad_value = contract(low[i][: 2 * span], grad_out[i], 1, 0)
            prev_refs[i][m, 0] = grad_key[:span]
            prev_refs[i][m, 1] = grad_value[:span]
            own_refs[i][m, 0] = grad_key[span:]
            own_refs[i][m, 1] = grad_value[span:]
        for i in slots:
            half = halves[i]
            far = far_kv[0][m] if i == 0 else jnp.where(is_last, prev_kv[0][m], far_kv[1][m])
            keys, values = (
                jnp.concatenate([prev_kv[i][m, which], own_kv[i][m, which], far[which]], axis=0)
                for which in range(2)
            )
            out = contract(values, low[i], 0, 0)
            grad_query = contract(keys, ds[i], 0, 0) * scale
            for g in range(group):
                columns = slice(g * span, (g + 1) * span)
                o_ref[half, m * group + g] = out[:, columns].T.astype(jnp.bfloat16)
                dq_ref[half, m * group + g] = grad_query[:, columns].T.astype(jnp.bfloat16)
        return carry

    lax.fori_loop(0, heads, one_head, 0)


def unpack_kernel(count, own_a, own_b, last_a, last_b, next_b, grad_keys_ref, grad_values_ref):
    halves, _, is_last = place(count)
    for which, ref in enumerate((grad_keys_ref, grad_values_ref)):
        sums = (
            own_a[:, which]
            + jnp.where(is_last, next_b[:, which], last_b[:, which]).astype(jnp.float32),
            own_b[:, which] + last_a[:, which].astype(jnp.float32),
        )
        for slot, total in enumerate(sums):
            ref[halves[slot], 0] = jnp.swapaxes(total, 0, 1).astype(jnp.bfloat16)


def by_half(info, final_a, final_b):
    even = info[:1].reshape((1,) * (final_a.ndim + 1)) == 1
    halves = jnp.where(even, jnp.stack([final_b, final_a]), jnp.stack([final_a, final_b]))
    halves = jnp.transpose(halves, (2, 0, 3, 1, 4))[:, :, None]
    return halves[0], halves[1]


def two_span_window(count, q_t, do_t, starts, own_a, own_b, pairs_a, pairs_b, scale):
    kv_heads, _, span, dim = own_a.shape
    heads = q_t.shape[1]
    rows = heads // kv_heads * span
    block = 2 * kv_heads * rows * span * dim
    shape = jax.ShapeDtypeStruct
    near = [shape((2, kv_heads, 2 * span, rows), jnp.float32)] * 2
    near.append(shape((2, kv_heads, 8, rows), jnp.float32))
    deeps = [shape(own_a.shape, jnp.bfloat16)] * 2
    lows = [shape((2, kv_heads, span, rows), jnp.bfloat16)] * 2
    norm = shape((2, kv_heads, 8, rows), jnp.float32)
    terms = [shape(own_a.shape, jnp.float32)] * 4
    outs = [shape(q_t.shape, jnp.bfloat16)] * 2

    both_axes = ("seq", "batch")
    swaps_b = everyone_swaps(pairs_b, count, lax.axis_size("batch"))
    last = jnp.full((dim,), lax.axis_index("seq") == count - 1).astype(jnp.int32)
    own_a, own_b, last = lax.optimization_barrier((own_a, own_b, last))
    is_last = last == 1
    b1 = lax.ppermute(own_a, both_axes, swaps_b)
    a1 = lax.ppermute(own_b, "seq", pairs_a)
    b1 = jnp.where(is_last, own_a, b1)
    b2 = lax.ppermute(a1, both_axes, swaps_b)
    a2 = lax.ppermute(b1, "seq", pairs_a)
    e, dp, stats = vmem_call(
        functools.partial(near_kernel, scale, count), near, 4 * block, "near",
        starts, q_t, do_t, own_a, own_b, a1, b1,
    )
    deep_a, deep_b, *far_parts = vmem_call(
        functools.partial(far_kernel, scale, count), deeps + lows + [norm], 2 * block, "far",
        starts, q_t, do_t, a1, a2, b2, stats,
    )
    from_a = lax.ppermute(deep_a, "seq", pairs_a)
    from_b = lax.ppermute(deep_b, both_axes, swaps_b)
    prev_a, prev_b, own_term_a, own_term_b, out, dq = vmem_call(
        functools.partial(rest_kernel, scale, count), terms + outs, 10 * block, "rest",
        q_t, do_t, e, dp, *far_parts, own_a, own_b, a1, b1, a2, b2,
    )
    from_a, from_b = lax.optimization_barrier((from_a, from_b))
    from_b = jnp.where(is_last, deep_b, from_b)
    next_a = (prev_a + from_b.astype(jnp.float32)).astype(jnp.bfloat16)
    next_b = (prev_b + from_a.astype(jnp.float32)).astype(jnp.bfloat16)
    last_a = lax.ppermute(next_a, "seq", pairs_a)
    last_b = lax.ppermute(next_b, both_axes, swaps_b)
    grads = [shape((2, 1, span, kv_heads, dim), jnp.bfloat16)] * 2
    grad_keys, grad_values = vmem_call(
        functools.partial(unpack_kernel, count), grads, 1024, "unpack",
        own_term_a, own_term_b, last_a, last_b, next_b,
    )
    return out, dq, grad_keys, grad_values


def any_window(info, q_t, do_t, starts, own_a, own_b, pairs_a, pairs_b, window, scale):
    kv_heads = own_a.shape[0]
    chunks = 2
    chunk = kv_heads // chunks
    parts = []
    for c in range(chunks):
        line_a = [jnp.swapaxes(own_a[c * chunk : (c + 1) * chunk], 0, 1)]
        line_b = [jnp.swapaxes(own_b[c * chunk : (c + 1) * chunk], 0, 1)]
        for _ in range(window):
            next_a = lax.ppermute(line_b[-1], "seq", pairs_a)
            next_b = lax.ppermute(line_a[-1], "seq", pairs_b)
            line_a.append(next_a)
            line_b.append(next_b)
        out, dq, now_a, now_b, rest_a, rest_b = attention_chunk(
            info, q_t, do_t, starts, (line_a, line_b), c * chunk, scale
        )
        for t in range(window - 1, -1, -1):
            from_a = lax.ppermute(now_a, "seq", pairs_a)
            from_b = lax.ppermute(now_b, "seq", pairs_b)
            now_a = (rest_a[t] + from_b.astype(jnp.float32)).astype(jnp.bfloat16)
            now_b = (rest_b[t] + from_a.astype(jnp.float32)).astype(jnp.bfloat16)
        parts.append((out, dq, now_a, now_b))
    out, dq, final_a, final_b = (jnp.concatenate(arrays, axis=1) for arrays in zip(*parts))
    return out, dq, *by_half(info, jnp.swapaxes(final_a, 0, 1), jnp.swapaxes(final_b, 0, 1))


def first_of_document(doc_starts, spans, span):
    token = spans[:, None] * span + jnp.arange(span, dtype=jnp.int32)[None, :]
    below = doc_starts[None, None, :] <= token[:, :, None]
    return jnp.max(jnp.where(below, doc_starts[None, None, :], 0), axis=2)[:, None, :]


def body(query, keys, values, grad_out, doc_starts):
    count = lax.axis_size("seq")
    device = lax.axis_index("seq")
    window = min(16, count // 2)
    span = query.shape[2]
    dim = query.shape[4]
    scale = dim ** (-0.5)
    pairs_a, pairs_b = swap_pairs(count)
    half_a = 1 - device % 2

    def payload(half):
        pair = [lax.dynamic_index_in_dim(x[:, 0], half, 0, keepdims=False) for x in (keys, values)]
        return jnp.transpose(jnp.stack(pair), (2, 0, 1, 3))

    own_a, own_b = payload(half_a), payload(1 - half_a)
    q_t = jnp.transpose(query[:, 0], (0, 2, 1, 3))
    do_t = jnp.transpose(grad_out[:, 0], (0, 2, 1, 3))
    if window == 2:
        starts = first_of_document(doc_starts, jnp.arange(2 * count, dtype=jnp.int32), span)
        out, dq, grad_keys, grad_values = two_span_window(
            count, q_t, do_t, starts, own_a, own_b, pairs_a, pairs_b, scale
        )
    else:
        spans = jnp.stack([device, 2 * count - 1 - device])
        starts = first_of_document(doc_starts, spans, span)
        span_a = jnp.where(half_a == 0, device, 2 * count - 1 - device)
        info = jnp.stack([half_a, 1 - half_a, span_a, 2 * count - 1 - span_a]).astype(jnp.int32)
        out, dq, grad_keys, grad_values = any_window(
            info, q_t, do_t, starts, own_a, own_b, pairs_a, pairs_b, window, scale
        )
    out = jnp.transpose(out, (0, 2, 1, 3))[:, None]
    dq = jnp.transpose(dq, (0, 2, 1, 3))[:, None]
    return out, dq, grad_keys, grad_values


def solution(mesh):
    spec = P("batch", "seq", None, "head", None)
    return jax.shard_map(
        body,
        mesh=mesh,
        in_specs=(spec, spec, spec, spec, P("batch")),
        out_specs=(spec, spec, spec, spec),
        check_vma=False,
    )
```

```python
import functools

import jax
import jax.numpy as jnp
from jax import lax
from jax.experimental import pallas as pl
from jax.experimental.pallas import tpu as pltpu
from jax.sharding import PartitionSpec as P

LOG2E = 1.4426950408889634
NEG = -1e30


def swap_pairs(count):
    pairs_a = []
    for i in range(0, count - 1, 2):
        pairs_a += [(i, i + 1), (i + 1, i)]
    pairs_b = []
    for i in range(1, count - 1, 2):
        pairs_b += [(i, i + 1), (i + 1, i)]
    pairs_b.append((count - 1, count - 1))
    return pairs_a, pairs_b


def everyone_swaps(pairs, count, batch):
    swaps = []
    for b in range(batch):
        lone = set(range(count)) - {source for source, target in pairs if source != target}
        swaps += [(i * batch + b, j * batch + b) for i, j in pairs if i != j]
        swaps += [(i * batch + b, i * batch + (b ^ 1)) for i in sorted(lone)]
    return swaps


def contract(lhs, rhs, lhs_dim, rhs_dim):
    return lax.dot_general(
        lhs, rhs, (((lhs_dim,), (rhs_dim,)), ((), ())), preferred_element_type=jnp.float32
    )


def attention_kernel(blocks, scale, info_ref, q_ref, do_ref, starts_ref, *refs):
    kv_refs = (refs[0:blocks], refs[blocks : 2 * blocks])
    o_ref, dq_ref = refs[2 * blocks : 2 * blocks + 2]
    deep_refs = refs[2 * blocks + 2 : 2 * blocks + 4]
    rest_refs = refs[2 * blocks + 4 : 2 * blocks + 6]
    k_all, v_all, s_all, p_all = refs[2 * blocks + 6 :]
    group, span, dim = q_ref.shape[1:]
    rows = group * span

    def each(body, init):
        if blocks <= 4:
            for t in range(blocks):
                init = body(t, init)
            return init
        return lax.fori_loop(0, blocks, body, init)

    for slot in range(2):
        half = info_ref[slot]
        span_first = info_ref[2 + slot] * span
        for t in range(blocks):
            k_all[t] = kv_refs[slot][t][0, 0]
            v_all[t] = kv_refs[slot][t][1, 0]
        queries = q_ref[half].reshape(rows, dim)
        grad_out = do_ref[half].reshape(rows, dim)
        start = starts_ref[half]
        token = span_first + lax.broadcasted_iota(jnp.int32, (1, span), 1)
        key_row = span_first + lax.broadcasted_iota(jnp.int32, (span, span), 0)

        def scores(t, top):
            key_pos = key_row - t * span
            allowed = (key_pos >= start) & (key_pos <= token)
            bias = jnp.where(allowed, 0.0, NEG)
            value = contract(k_all[t], queries, 1, 1) + jnp.concatenate([bias] * group, axis=1)
            s_all[t] = value
            return jnp.maximum(top, jnp.max(value, axis=0, keepdims=True))

        top = each(scores, jnp.full((1, rows), NEG, jnp.float32))

        def expons(t, total):
            value = jnp.exp2((s_all[t] - top) * (scale * LOG2E))
            s_all[t] = value
            return total + jnp.sum(value, axis=0, keepdims=True)

        total = each(expons, jnp.zeros((1, rows), jnp.float32))
        inverse = 1.0 / total

        def forward(t, carry):
            out, delta = carry
            weights = s_all[t] * inverse
            low = weights.astype(jnp.bfloat16)
            grad_weights = contract(v_all[t], grad_out, 1, 1)
            s_all[t] = weights
            p_all[t] = grad_weights
            delta = delta + jnp.sum(weights * grad_weights, axis=0, keepdims=True)
            out = out + contract(v_all[t], low, 0, 0)
            grad_value = contract(low, grad_out, 1, 0)
            store_term(t, 1, grad_value)
            return out, delta

        def store_term(t, which, value):
            if isinstance(t, int):
                if t == blocks - 1:
                    deep_refs[slot][which, 0] = value.astype(jnp.bfloat16)
                else:
                    rest_refs[slot][t, which, 0] = value
            else:
                @pl.when(t == blocks - 1)
                def _():
                    deep_refs[slot][which, 0] = value.astype(jnp.bfloat16)

                @pl.when(t < blocks - 1)
                def _():
                    rest_refs[slot][t, which, 0] = value

        out, delta = each(
            forward, (jnp.zeros((dim, rows), jnp.float32), jnp.zeros((1, rows), jnp.float32))
        )

        def backward(t, grad_query):
            low = (s_all[t] * (p_all[t] - delta)).astype(jnp.bfloat16)
            store_term(t, 0, contract(low, queries, 1, 0) * scale)
            return grad_query + contract(k_all[t], low, 0, 0)

        grad_query = each(backward, jnp.zeros((dim, rows), jnp.float32)) * scale
        for g in range(group):
            columns = slice(g * span, (g + 1) * span)
            o_ref[half, g] = out[:, columns].T.astype(jnp.bfloat16)
            dq_ref[half, g] = grad_query[:, columns].T.astype(jnp.bfloat16)


def attention_chunk(info, q_t, do_t, starts, kv_blocks, first_head, scale):
    blocks = len(kv_blocks[0])
    _, heads, span, dim = q_t.shape
    chunk = kv_blocks[0][0].shape[1]
    group = 4
    rows = group * span
    window = blocks - 1
    q_spec = pl.BlockSpec((2, group, span, dim), lambda m, info: (0, first_head + m, 0, 0))
    o_spec = pl.BlockSpec((2, group, span, dim), lambda m, info: (0, m, 0, 0))
    kv_spec = pl.BlockSpec((2, 1, span, dim), lambda m, info: (0, m, 0, 0))
    rest_spec = pl.BlockSpec((window, 2, 1, span, dim), lambda m, info: (0, 0, m, 0, 0))
    starts_spec = pl.BlockSpec((2, 1, span), lambda m, info: (0, 0, 0))
    deep = jax.ShapeDtypeStruct((2, chunk, span, dim), jnp.bfloat16)
    rest = jax.ShapeDtypeStruct((window, 2, chunk, span, dim), jnp.float32)
    out = jax.ShapeDtypeStruct((2, chunk * group, span, dim), jnp.bfloat16)
    macs = 2 * chunk * 5 * rows * blocks * span * dim
    return pl.pallas_call(
        functools.partial(attention_kernel, blocks, scale),
        grid_spec=pltpu.PrefetchScalarGridSpec(
            num_scalar_prefetch=1,
            grid=(chunk,),
            in_specs=[q_spec, q_spec, starts_spec] + [kv_spec] * (2 * blocks),
            out_specs=[o_spec, o_spec, kv_spec, kv_spec, rest_spec, rest_spec],
            scratch_shapes=[
                pltpu.VMEM((blocks, span, dim), jnp.bfloat16),
                pltpu.VMEM((blocks, span, dim), jnp.bfloat16),
                pltpu.VMEM((blocks, span, rows), jnp.float32),
                pltpu.VMEM((blocks, span, rows), jnp.float32),
            ],
        ),
        out_shape=[out, out, deep, deep, rest, rest],
        compiler_params=pltpu.CompilerParams(vmem_limit_bytes=48 * 1024 * 1024),
        cost_estimate=pl.CostEstimate(
            flops=2 * macs, bytes_accessed=8 * 1024 * 1024, transcendentals=0
        ),
        name="attention",
    )(info, q_t, do_t, starts, *kv_blocks[0], *kv_blocks[1])


def vmem_call(kernel, out_shape, macs, name, *args, aliases=None):
    whole = pl.BlockSpec(memory_space=pltpu.VMEM)
    moved = sum(a.size * a.dtype.itemsize for a in args)
    return pl.pallas_call(
        kernel,
        in_specs=[whole] * len(args),
        out_specs=[whole] * len(out_shape),
        out_shape=out_shape,
        input_output_aliases=aliases or {},
        compiler_params=pltpu.CompilerParams(vmem_limit_bytes=16 * 1024 * 1024),
        cost_estimate=pl.CostEstimate(flops=8 * macs, bytes_accessed=moved, transcendentals=0),
        name=name,
    )(*args)


def place(count):
    device = lax.axis_index("seq")
    half_a = 1 - device % 2
    span_a = jnp.where(half_a == 0, device, 2 * count - 1 - device)
    return (half_a, 1 - half_a), (span_a, 2 * count - 1 - span_a), device == count - 1


def group_of(ref, half, m, group):
    return ref[half, pl.ds(m * group, group)].reshape(group * ref.shape[2], ref.shape[3])


def near_kernel(scale, count, starts_ref, q_ref, do_ref, own_a, own_b, prev_a, prev_b, e_ref, dp_ref, stats_ref):
    heads, span, rows = e_ref.shape[1], e_ref.shape[2] // 2, e_ref.shape[3]
    group = rows // span
    row = lax.broadcasted_iota(jnp.int32, (span, span), 0)
    column = lax.broadcasted_iota(jnp.int32, (span, span), 1)
    slots = range(2)
    kv_refs = ((prev_a, own_a), (prev_b, own_b))
    halves, spans, _ = place(count)
    biases = []
    for slot in slots:
        first = spans[slot] * span
        start = starts_ref[spans[slot]]
        prev_bias = jnp.where(first - span + row >= start, 0.0, NEG)
        own_bias = jnp.where((first + row >= start) & (row <= column), 0.0, NEG)
        biases.append(jnp.concatenate([prev_bias, own_bias], axis=0))

    def one_head(m, carry):
        scores, grads = [], []
        for i in slots:
            keys, values = (
                jnp.concatenate([ref[m, which] for ref in kv_refs[i]], axis=0) for which in range(2)
            )
            scores.append(contract(keys, group_of(q_ref, halves[i], m, group), 1, 1))
            grads.append(contract(values, group_of(do_ref, halves[i], m, group), 1, 1))
        scores = [x + jnp.concatenate([biases[i]] * group, axis=1) for i, x in enumerate(scores)]
        top = [jnp.max(x, axis=0, keepdims=True) for x in scores]
        e = [jnp.exp2((scores[i] - top[i]) * (scale * LOG2E)) for i in slots]
        for i in slots:
            e_ref[i, m] = e[i]
            dp_ref[i, m] = grads[i]
            stats_ref[i, m, 0:1] = top[i]
            stats_ref[i, m, 1:2] = jnp.sum(e[i], axis=0, keepdims=True)
            stats_ref[i, m, 2:3] = jnp.sum(e[i] * grads[i], axis=0, keepdims=True)
        return carry

    lax.fori_loop(0, heads, one_head, 0)


def far_kernel(scale, count, starts_ref, q_ref, do_ref, prev_a, far_a, far_b, stats_ref, deep_a, deep_b,
               low_ref, ds_ref, norm_ref):
    heads, span, rows = low_ref.shape[1:]
    group = rows // span
    row = lax.broadcasted_iota(jnp.int32, (span, span), 0)
    column = lax.broadcasted_iota(jnp.int32, (span, span), 1)
    factor = scale * LOG2E
    slots = range(2)
    halves, spans, is_last = place(count)
    biases = []
    for slot in slots:
        first = spans[slot] * span
        allowed = (first - 2 * span + row >= starts_ref[spans[slot]]) & (row > column)
        biases.append(jnp.where(allowed, 0.0, NEG))
    deep_refs = (deep_a, deep_b)


    def one_head(m, carry):
        far_kv = [far_a[m], jnp.where(is_last, prev_a[m], far_b[m])]
        queries = [group_of(q_ref, halves[i], m, group) for i in slots]
        grad_out = [group_of(do_ref, halves[i], m, group) for i in slots]
        scores = [
            contract(far_kv[i][0], queries[i], 1, 1)
            + jnp.concatenate([biases[i]] * group, axis=1)
            for i in slots
        ]
        grads = [contract(far_kv[i][1], grad_out[i], 1, 1) for i in slots]
        near_top = [stats_ref[i, m, 0:1] for i in slots]
        top = [
            jnp.maximum(near_top[i], jnp.max(scores[i], axis=0, keepdims=True)) for i in slots
        ]
        near = [jnp.exp2((near_top[i] - top[i]) * factor) for i in slots]
        e = [jnp.exp2((scores[i] - top[i]) * factor) for i in slots]
        inverse = [
            1.0 / (near[i] * stats_ref[i, m, 1:2] + jnp.sum(e[i], axis=0, keepdims=True))
            for i in slots
        ]
        delta = [
            (
                near[i] * stats_ref[i, m, 2:3]
                + jnp.sum(e[i] * grads[i], axis=0, keepdims=True)
            )
            * inverse[i]
            for i in slots
        ]
        weights = [e[i] * inverse[i] for i in slots]
        low = [x.astype(jnp.bfloat16) for x in weights]
        ds = [(weights[i] * (grads[i] - delta[i])).astype(jnp.bfloat16) for i in slots]
        for i in slots:
            low_ref[i, m] = low[i]
            ds_ref[i, m] = ds[i]
            norm_ref[i, m, 0:1] = near[i] * inverse[i]
            norm_ref[i, m, 1:2] = delta[i]
        for i in slots:
            deep_refs[i][m, 0] = (contract(ds[i], queries[i], 1, 0) * scale).astype(jnp.bfloat16)
            deep_refs[i][m, 1] = contract(low[i], grad_out[i], 1, 0).astype(jnp.bfloat16)
        return carry

    lax.fori_loop(0, heads, one_head, 0, unroll=True)


def rest_kernel(scale, count, q_ref, do_ref, e_ref, dp_ref, *refs):
    far_low, far_ds, norm = refs[:3]
    own_kv, prev_kv, far_kv = refs[3:5], refs[5:7], refs[7:9]
    prev_refs, own_refs = refs[9:11], refs[11:13]
    o_ref, dq_ref = refs[13:]
    halves, _, is_last = place(count)
    heads, span, rows = e_ref.shape[1], e_ref.shape[2] // 2, e_ref.shape[3]
    group = rows // span
    slots = range(2)

    def one_head(m, carry):
        queries = [group_of(q_ref, halves[i], m, group) for i in slots]
        grad_out = [group_of(do_ref, halves[i], m, group) for i in slots]
        low, ds = [], []
        for i in slots:
            weights = e_ref[i, m] * norm[i, m, 0:1]
            near_ds = (weights * (dp_ref[i, m] - norm[i, m, 1:2])).astype(jnp.bfloat16)
            low.append(jnp.concatenate([weights.astype(jnp.bfloat16), far_low[i, m]], axis=0))
            ds.append(jnp.concatenate([near_ds, far_ds[i, m]], axis=0))
        for i in slots:
            grad_key = contract(ds[i][: 2 * span], queries[i], 1, 0) * scale
            grad_value = contract(low[i][: 2 * span], grad_out[i], 1, 0)
            prev_refs[i][m, 0] = grad_key[:span]
            prev_refs[i][m, 1] = grad_value[:span]
            own_refs[i][m, 0] = grad_key[span:]
            own_refs[i][m, 1] = grad_value[span:]
        for i in slots:
            half = halves[i]
            far = far_kv[0][m] if i == 0 else jnp.where(is_last, prev_kv[0][m], far_kv[1][m])
            keys, values = (
                jnp.concatenate([prev_kv[i][m, which], own_kv[i][m, which], far[which]], axis=0)
                for which in range(2)
            )
            out = contract(values, low[i], 0, 0)
            grad_query = contract(keys, ds[i], 0, 0) * scale
            for g in range(group):
                columns = slice(g * span, (g + 1) * span)
                o_ref[half, m * group + g] = out[:, columns].T.astype(jnp.bfloat16)
                dq_ref[half, m * group + g] = grad_query[:, columns].T.astype(jnp.bfloat16)
        return carry

    lax.fori_loop(0, heads, one_head, 0)


def merge_kernel(count, prev_a, prev_b, from_a, from_b, deep_b, next_a_ref, next_b_ref):
    _, _, is_last = place(count)
    from_far = jnp.where(is_last, deep_b[...], from_b[...])
    next_a_ref[...] = (prev_a[...] + from_far.astype(jnp.float32)).astype(jnp.bfloat16)
    next_b_ref[...] = (prev_b[...] + from_a[...].astype(jnp.float32)).astype(jnp.bfloat16)


def unpack_kernel(count, own_a, own_b, last_a, last_b, next_b, grad_keys_ref, grad_values_ref):
    halves, _, is_last = place(count)
    for which, ref in enumerate((grad_keys_ref, grad_values_ref)):
        sums = (
            own_a[:, which]
            + jnp.where(is_last, next_b[:, which], last_b[:, which]).astype(jnp.float32),
            own_b[:, which] + last_a[:, which].astype(jnp.float32),
        )
        for slot, total in enumerate(sums):
            ref[halves[slot], 0] = jnp.swapaxes(total, 0, 1).astype(jnp.bfloat16)


def by_half(info, final_a, final_b):
    even = info[:1].reshape((1,) * (final_a.ndim + 1)) == 1
    halves = jnp.where(even, jnp.stack([final_b, final_a]), jnp.stack([final_a, final_b]))
    halves = jnp.transpose(halves, (2, 0, 3, 1, 4))[:, :, None]
    return halves[0], halves[1]


def two_span_window(count, q_t, do_t, starts, own_a, own_b, pairs_a, pairs_b, scale):
    kv_heads, _, span, dim = own_a.shape
    heads = q_t.shape[1]
    rows = heads // kv_heads * span
    block = 2 * kv_heads * rows * span * dim
    shape = jax.ShapeDtypeStruct
    near = [shape((2, kv_heads, 2 * span, rows), jnp.float32)] * 2
    near.append(shape((2, kv_heads, 8, rows), jnp.float32))
    deeps = [shape(own_a.shape, jnp.bfloat16)] * 2
    lows = [shape((2, kv_heads, span, rows), jnp.bfloat16)] * 2
    norm = shape((2, kv_heads, 8, rows), jnp.float32)
    terms = [shape(own_a.shape, jnp.float32)] * 4
    outs = [shape(q_t.shape, jnp.bfloat16)] * 2

    both_axes = ("seq", "batch")
    swaps_b = everyone_swaps(pairs_b, count, lax.axis_size("batch"))
    last = jnp.full((dim,), lax.axis_index("seq") == count - 1).astype(jnp.int32)
    own_a, own_b, last = lax.optimization_barrier((own_a, own_b, last))
    is_last = last == 1
    b1 = lax.ppermute(own_a, both_axes, swaps_b)
    a1 = lax.ppermute(own_b, "seq", pairs_a)
    b1 = jnp.where(is_last, own_a, b1)
    b2 = lax.ppermute(a1, both_axes, swaps_b)
    a2 = lax.ppermute(b1, "seq", pairs_a)
    e, dp, stats = vmem_call(
        functools.partial(near_kernel, scale, count), near, 4 * block, "near",
        starts, q_t, do_t, own_a, own_b, a1, b1,
    )
    deep_a, deep_b, *far_parts = vmem_call(
        functools.partial(far_kernel, scale, count), deeps + lows + [norm], 2 * block, "far",
        starts, q_t, do_t, a1, a2, b2, stats,
    )
    from_a = lax.ppermute(deep_a, "seq", pairs_a)
    from_b = lax.ppermute(deep_b, both_axes, swaps_b)
    prev_a, prev_b, own_term_a, own_term_b, out, dq = vmem_call(
        functools.partial(rest_kernel, scale, count), terms + outs, 10 * block, "rest",
        q_t, do_t, e, dp, *far_parts, own_a, own_b, a1, b1, a2, b2,
    )
    next_a, next_b = vmem_call(
        functools.partial(merge_kernel, count), deeps, 1024, "merge",
        prev_a, prev_b, from_a, from_b, deep_b,
    )
    last_a = lax.ppermute(next_a, "seq", pairs_a)
    last_b = lax.ppermute(next_b, both_axes, swaps_b)
    grads = [shape((2, 1, span, kv_heads, dim), jnp.bfloat16)] * 2
    grad_keys, grad_values = vmem_call(
        functools.partial(unpack_kernel, count), grads, 1024, "unpack",
        own_term_a, own_term_b, last_a, last_b, next_b,
    )
    return out, dq, grad_keys, grad_values


def any_window(info, q_t, do_t, starts, own_a, own_b, pairs_a, pairs_b, window, scale):
    kv_heads = own_a.shape[0]
    chunks = 2
    chunk = kv_heads // chunks
    parts = []
    for c in range(chunks):
        line_a = [jnp.swapaxes(own_a[c * chunk : (c + 1) * chunk], 0, 1)]
        line_b = [jnp.swapaxes(own_b[c * chunk : (c + 1) * chunk], 0, 1)]
        for _ in range(window):
            next_a = lax.ppermute(line_b[-1], "seq", pairs_a)
            next_b = lax.ppermute(line_a[-1], "seq", pairs_b)
            line_a.append(next_a)
            line_b.append(next_b)
        out, dq, now_a, now_b, rest_a, rest_b = attention_chunk(
            info, q_t, do_t, starts, (line_a, line_b), c * chunk, scale
        )
        for t in range(window - 1, -1, -1):
            from_a = lax.ppermute(now_a, "seq", pairs_a)
            from_b = lax.ppermute(now_b, "seq", pairs_b)
            now_a = (rest_a[t] + from_b.astype(jnp.float32)).astype(jnp.bfloat16)
            now_b = (rest_b[t] + from_a.astype(jnp.float32)).astype(jnp.bfloat16)
        parts.append((out, dq, now_a, now_b))
    out, dq, final_a, final_b = (jnp.concatenate(arrays, axis=1) for arrays in zip(*parts))
    return out, dq, *by_half(info, jnp.swapaxes(final_a, 0, 1), jnp.swapaxes(final_b, 0, 1))


def first_of_document(doc_starts, spans, span):
    token = spans[:, None] * span + jnp.arange(span, dtype=jnp.int32)[None, :]
    below = doc_starts[None, None, :] <= token[:, :, None]
    return jnp.max(jnp.where(below, doc_starts[None, None, :], 0), axis=2)[:, None, :]


def body(query, keys, values, grad_out, doc_starts):
    count = lax.axis_size("seq")
    device = lax.axis_index("seq")
    window = min(16, count // 2)
    span = query.shape[2]
    dim = query.shape[4]
    scale = dim ** (-0.5)
    pairs_a, pairs_b = swap_pairs(count)
    half_a = 1 - device % 2

    def payload(half):
        pair = [lax.dynamic_index_in_dim(x[:, 0], half, 0, keepdims=False) for x in (keys, values)]
        return jnp.transpose(jnp.stack(pair), (2, 0, 1, 3))

    own_a, own_b = payload(half_a), payload(1 - half_a)
    q_t = jnp.transpose(query[:, 0], (0, 2, 1, 3))
    do_t = jnp.transpose(grad_out[:, 0], (0, 2, 1, 3))
    if window == 2:
        starts = first_of_document(doc_starts, jnp.arange(2 * count, dtype=jnp.int32), span)
        out, dq, grad_keys, grad_values = two_span_window(
            count, q_t, do_t, starts, own_a, own_b, pairs_a, pairs_b, scale
        )
    else:
        spans = jnp.stack([device, 2 * count - 1 - device])
        starts = first_of_document(doc_starts, spans, span)
        span_a = jnp.where(half_a == 0, device, 2 * count - 1 - device)
        info = jnp.stack([half_a, 1 - half_a, span_a, 2 * count - 1 - span_a]).astype(jnp.int32)
        out, dq, grad_keys, grad_values = any_window(
            info, q_t, do_t, starts, own_a, own_b, pairs_a, pairs_b, window, scale
        )
    out = jnp.transpose(out, (0, 2, 1, 3))[:, None]
    dq = jnp.transpose(dq, (0, 2, 1, 3))[:, None]
    return out, dq, grad_keys, grad_values


def solution(mesh):
    spec = P("batch", "seq", None, "head", None)
    return jax.shard_map(
        body,
        mesh=mesh,
        in_specs=(spec, spec, spec, spec, P("batch")),
        out_specs=(spec, spec, spec, spec),
        check_vma=False,
    )
```

```python
import functools

import jax
import jax.numpy as jnp
from jax import lax
from jax.experimental import pallas as pl
from jax.experimental.pallas import tpu as pltpu
from jax.sharding import PartitionSpec as P

LOG2E = 1.4426950408889634
NEG = -1e30


def swap_pairs(count):
    pairs_a = []
    for i in range(0, count - 1, 2):
        pairs_a += [(i, i + 1), (i + 1, i)]
    pairs_b = []
    for i in range(1, count - 1, 2):
        pairs_b += [(i, i + 1), (i + 1, i)]
    pairs_b.append((count - 1, count - 1))
    return pairs_a, pairs_b


def everyone_swaps(pairs, count, batch):
    swaps = []
    for b in range(batch):
        lone = set(range(count)) - {source for source, target in pairs if source != target}
        swaps += [(i * batch + b, j * batch + b) for i, j in pairs if i != j]
        swaps += [(i * batch + b, i * batch + (b ^ 1)) for i in sorted(lone)]
    return swaps


def contract(lhs, rhs, lhs_dim, rhs_dim):
    return lax.dot_general(
        lhs, rhs, (((lhs_dim,), (rhs_dim,)), ((), ())), preferred_element_type=jnp.float32
    )


def attention_kernel(blocks, scale, info_ref, q_ref, do_ref, starts_ref, *refs):
    kv_refs = (refs[0:blocks], refs[blocks : 2 * blocks])
    o_ref, dq_ref = refs[2 * blocks : 2 * blocks + 2]
    deep_refs = refs[2 * blocks + 2 : 2 * blocks + 4]
    rest_refs = refs[2 * blocks + 4 : 2 * blocks + 6]
    k_all, v_all, s_all, p_all = refs[2 * blocks + 6 :]
    group, span, dim = q_ref.shape[1:]
    rows = group * span

    def each(body, init):
        if blocks <= 4:
            for t in range(blocks):
                init = body(t, init)
            return init
        return lax.fori_loop(0, blocks, body, init)

    for slot in range(2):
        half = info_ref[slot]
        span_first = info_ref[2 + slot] * span
        for t in range(blocks):
            k_all[t] = kv_refs[slot][t][0, 0]
            v_all[t] = kv_refs[slot][t][1, 0]
        queries = q_ref[half].reshape(rows, dim)
        grad_out = do_ref[half].reshape(rows, dim)
        start = starts_ref[half]
        token = span_first + lax.broadcasted_iota(jnp.int32, (1, span), 1)
        key_row = span_first + lax.broadcasted_iota(jnp.int32, (span, span), 0)

        def scores(t, top):
            key_pos = key_row - t * span
            allowed = (key_pos >= start) & (key_pos <= token)
            bias = jnp.where(allowed, 0.0, NEG)
            value = contract(k_all[t], queries, 1, 1) + jnp.concatenate([bias] * group, axis=1)
            s_all[t] = value
            return jnp.maximum(top, jnp.max(value, axis=0, keepdims=True))

        top = each(scores, jnp.full((1, rows), NEG, jnp.float32))

        def expons(t, total):
            value = jnp.exp2((s_all[t] - top) * (scale * LOG2E))
            s_all[t] = value
            return total + jnp.sum(value, axis=0, keepdims=True)

        total = each(expons, jnp.zeros((1, rows), jnp.float32))
        inverse = 1.0 / total

        def forward(t, carry):
            out, delta = carry
            weights = s_all[t] * inverse
            low = weights.astype(jnp.bfloat16)
            grad_weights = contract(v_all[t], grad_out, 1, 1)
            s_all[t] = weights
            p_all[t] = grad_weights
            delta = delta + jnp.sum(weights * grad_weights, axis=0, keepdims=True)
            out = out + contract(v_all[t], low, 0, 0)
            grad_value = contract(low, grad_out, 1, 0)
            store_term(t, 1, grad_value)
            return out, delta

        def store_term(t, which, value):
            if isinstance(t, int):
                if t == blocks - 1:
                    deep_refs[slot][which, 0] = value.astype(jnp.bfloat16)
                else:
                    rest_refs[slot][t, which, 0] = value
            else:
                @pl.when(t == blocks - 1)
                def _():
                    deep_refs[slot][which, 0] = value.astype(jnp.bfloat16)

                @pl.when(t < blocks - 1)
                def _():
                    rest_refs[slot][t, which, 0] = value

        out, delta = each(
            forward, (jnp.zeros((dim, rows), jnp.float32), jnp.zeros((1, rows), jnp.float32))
        )

        def backward(t, grad_query):
            low = (s_all[t] * (p_all[t] - delta)).astype(jnp.bfloat16)
            store_term(t, 0, contract(low, queries, 1, 0) * scale)
            return grad_query + contract(k_all[t], low, 0, 0)

        grad_query = each(backward, jnp.zeros((dim, rows), jnp.float32)) * scale
        for g in range(group):
            columns = slice(g * span, (g + 1) * span)
            o_ref[half, g] = out[:, columns].T.astype(jnp.bfloat16)
            dq_ref[half, g] = grad_query[:, columns].T.astype(jnp.bfloat16)


def attention_chunk(info, q_t, do_t, starts, kv_blocks, first_head, scale):
    blocks = len(kv_blocks[0])
    _, heads, span, dim = q_t.shape
    chunk = kv_blocks[0][0].shape[1]
    group = 4
    rows = group * span
    window = blocks - 1
    q_spec = pl.BlockSpec((2, group, span, dim), lambda m, info: (0, first_head + m, 0, 0))
    o_spec = pl.BlockSpec((2, group, span, dim), lambda m, info: (0, m, 0, 0))
    kv_spec = pl.BlockSpec((2, 1, span, dim), lambda m, info: (0, m, 0, 0))
    rest_spec = pl.BlockSpec((window, 2, 1, span, dim), lambda m, info: (0, 0, m, 0, 0))
    starts_spec = pl.BlockSpec((2, 1, span), lambda m, info: (0, 0, 0))
    deep = jax.ShapeDtypeStruct((2, chunk, span, dim), jnp.bfloat16)
    rest = jax.ShapeDtypeStruct((window, 2, chunk, span, dim), jnp.float32)
    out = jax.ShapeDtypeStruct((2, chunk * group, span, dim), jnp.bfloat16)
    macs = 2 * chunk * 5 * rows * blocks * span * dim
    return pl.pallas_call(
        functools.partial(attention_kernel, blocks, scale),
        grid_spec=pltpu.PrefetchScalarGridSpec(
            num_scalar_prefetch=1,
            grid=(chunk,),
            in_specs=[q_spec, q_spec, starts_spec] + [kv_spec] * (2 * blocks),
            out_specs=[o_spec, o_spec, kv_spec, kv_spec, rest_spec, rest_spec],
            scratch_shapes=[
                pltpu.VMEM((blocks, span, dim), jnp.bfloat16),
                pltpu.VMEM((blocks, span, dim), jnp.bfloat16),
                pltpu.VMEM((blocks, span, rows), jnp.float32),
                pltpu.VMEM((blocks, span, rows), jnp.float32),
            ],
        ),
        out_shape=[out, out, deep, deep, rest, rest],
        compiler_params=pltpu.CompilerParams(vmem_limit_bytes=48 * 1024 * 1024),
        cost_estimate=pl.CostEstimate(
            flops=2 * macs, bytes_accessed=8 * 1024 * 1024, transcendentals=0
        ),
        name="attention",
    )(info, q_t, do_t, starts, *kv_blocks[0], *kv_blocks[1])


def vmem_call(kernel, out_shape, macs, name, *args, aliases=None):
    whole = pl.BlockSpec(memory_space=pltpu.VMEM)
    moved = sum(a.size * a.dtype.itemsize for a in args)
    return pl.pallas_call(
        kernel,
        in_specs=[whole] * len(args),
        out_specs=[whole] * len(out_shape),
        out_shape=out_shape,
        input_output_aliases=aliases or {},
        compiler_params=pltpu.CompilerParams(vmem_limit_bytes=16 * 1024 * 1024),
        cost_estimate=pl.CostEstimate(flops=8 * macs, bytes_accessed=moved, transcendentals=0),
        name=name,
    )(*args)


def place(count):
    device = lax.axis_index("seq")
    half_a = 1 - device % 2
    span_a = jnp.where(half_a == 0, device, 2 * count - 1 - device)
    return (half_a, 1 - half_a), (span_a, 2 * count - 1 - span_a), device == count - 1


def group_of(ref, half, m, group):
    return ref[half, pl.ds(m * group, group)].reshape(group * ref.shape[2], ref.shape[3])


def near_kernel(scale, count, starts_ref, q_ref, do_ref, own_a, own_b, prev_a, prev_b, e_ref, dp_ref, stats_ref):
    heads, span, rows = e_ref.shape[1], e_ref.shape[2] // 2, e_ref.shape[3]
    group = rows // span
    row = lax.broadcasted_iota(jnp.int32, (span, span), 0)
    column = lax.broadcasted_iota(jnp.int32, (span, span), 1)
    slots = range(2)
    kv_refs = ((prev_a, own_a), (prev_b, own_b))
    halves, spans, _ = place(count)
    biases = []
    for slot in slots:
        first = spans[slot] * span
        start = starts_ref[spans[slot]]
        prev_bias = jnp.where(first - span + row >= start, 0.0, NEG)
        own_bias = jnp.where((first + row >= start) & (row <= column), 0.0, NEG)
        biases.append(jnp.concatenate([prev_bias, own_bias], axis=0))

    def one_head(m, carry):
        scores, grads = [], []
        for i in slots:
            keys, values = (
                jnp.concatenate([ref[m, which] for ref in kv_refs[i]], axis=0) for which in range(2)
            )
            scores.append(contract(keys, group_of(q_ref, halves[i], m, group), 1, 1))
            grads.append(contract(values, group_of(do_ref, halves[i], m, group), 1, 1))
        scores = [x + jnp.concatenate([biases[i]] * group, axis=1) for i, x in enumerate(scores)]
        top = [jnp.max(x, axis=0, keepdims=True) for x in scores]
        e = [jnp.exp2((scores[i] - top[i]) * (scale * LOG2E)) for i in slots]
        for i in slots:
            e_ref[i, m] = e[i]
            dp_ref[i, m] = grads[i]
            stats_ref[i, m, 0:1] = top[i]
            stats_ref[i, m, 1:2] = jnp.sum(e[i], axis=0, keepdims=True)
            stats_ref[i, m, 2:3] = jnp.sum(e[i] * grads[i], axis=0, keepdims=True)
        return carry

    lax.fori_loop(0, heads, one_head, 0)


def far_kernel(scale, count, starts_ref, q_ref, do_ref, prev_a, far_a, far_b, stats_ref, deep_a, deep_b,
               low_ref, ds_ref, norm_ref):
    heads, span, rows = low_ref.shape[1:]
    group = rows // span
    row = lax.broadcasted_iota(jnp.int32, (span, span), 0)
    column = lax.broadcasted_iota(jnp.int32, (span, span), 1)
    factor = scale * LOG2E
    slots = range(2)
    halves, spans, is_last = place(count)
    biases = []
    for slot in slots:
        first = spans[slot] * span
        allowed = (first - 2 * span + row >= starts_ref[spans[slot]]) & (row > column)
        biases.append(jnp.where(allowed, 0.0, NEG))
    deep_refs = (deep_a, deep_b)


    def one_head(m, carry):
        far_kv = [far_a[m], jnp.where(is_last, prev_a[m], far_b[m])]
        queries = [group_of(q_ref, halves[i], m, group) for i in slots]
        grad_out = [group_of(do_ref, halves[i], m, group) for i in slots]
        scores = [
            contract(far_kv[i][0], queries[i], 1, 1)
            + jnp.concatenate([biases[i]] * group, axis=1)
            for i in slots
        ]
        grads = [contract(far_kv[i][1], grad_out[i], 1, 1) for i in slots]
        near_top = [stats_ref[i, m, 0:1] for i in slots]
        top = [
            jnp.maximum(near_top[i], jnp.max(scores[i], axis=0, keepdims=True)) for i in slots
        ]
        near = [jnp.exp2((near_top[i] - top[i]) * factor) for i in slots]
        e = [jnp.exp2((scores[i] - top[i]) * factor) for i in slots]
        inverse = [
            1.0 / (near[i] * stats_ref[i, m, 1:2] + jnp.sum(e[i], axis=0, keepdims=True))
            for i in slots
        ]
        delta = [
            (
                near[i] * stats_ref[i, m, 2:3]
                + jnp.sum(e[i] * grads[i], axis=0, keepdims=True)
            )
            * inverse[i]
            for i in slots
        ]
        weights = [e[i] * inverse[i] for i in slots]
        low = [x.astype(jnp.bfloat16) for x in weights]
        ds = [(weights[i] * (grads[i] - delta[i])).astype(jnp.bfloat16) for i in slots]
        for i in slots:
            low_ref[i, m] = low[i]
            ds_ref[i, m] = ds[i]
            norm_ref[i, m, 0:1] = near[i] * inverse[i]
            norm_ref[i, m, 1:2] = delta[i]
        for i in slots:
            deep_refs[i][m, 0] = (contract(ds[i], queries[i], 1, 0) * scale).astype(jnp.bfloat16)
            deep_refs[i][m, 1] = contract(low[i], grad_out[i], 1, 0).astype(jnp.bfloat16)
        return carry

    lax.fori_loop(0, heads, one_head, 0, unroll=True)


def rest_kernel(scale, count, q_ref, do_ref, e_ref, dp_ref, *refs):
    far_low, far_ds, norm = refs[:3]
    own_kv, prev_kv, far_kv = refs[3:5], refs[5:7], refs[7:9]
    prev_refs, own_refs = refs[9:11], refs[11:13]
    o_ref, dq_ref = refs[13:]
    halves, _, is_last = place(count)
    heads, span, rows = e_ref.shape[1], e_ref.shape[2] // 2, e_ref.shape[3]
    group = rows // span
    slots = range(2)

    def one_head(m, carry):
        queries = [group_of(q_ref, halves[i], m, group) for i in slots]
        grad_out = [group_of(do_ref, halves[i], m, group) for i in slots]
        low, ds = [], []
        for i in slots:
            weights = e_ref[i, m] * norm[i, m, 0:1]
            near_ds = (weights * (dp_ref[i, m] - norm[i, m, 1:2])).astype(jnp.bfloat16)
            low.append(jnp.concatenate([weights.astype(jnp.bfloat16), far_low[i, m]], axis=0))
            ds.append(jnp.concatenate([near_ds, far_ds[i, m]], axis=0))
        for i in slots:
            grad_key = contract(ds[i][: 2 * span], queries[i], 1, 0) * scale
            grad_value = contract(low[i][: 2 * span], grad_out[i], 1, 0)
            prev_refs[i][m, 0] = grad_key[:span]
            prev_refs[i][m, 1] = grad_value[:span]
            own_refs[i][m, 0] = grad_key[span:]
            own_refs[i][m, 1] = grad_value[span:]
        for i in slots:
            half = halves[i]
            far = far_kv[0][m] if i == 0 else jnp.where(is_last, prev_kv[0][m], far_kv[1][m])
            keys, values = (
                jnp.concatenate([prev_kv[i][m, which], own_kv[i][m, which], far[which]], axis=0)
                for which in range(2)
            )
            out = contract(values, low[i], 0, 0)
            grad_query = contract(keys, ds[i], 0, 0) * scale
            for g in range(group):
                columns = slice(g * span, (g + 1) * span)
                o_ref[half, m * group + g] = out[:, columns].T.astype(jnp.bfloat16)
                dq_ref[half, m * group + g] = grad_query[:, columns].T.astype(jnp.bfloat16)
        return carry

    lax.fori_loop(0, heads, one_head, 0)


def unpack_kernel(count, own_a, own_b, last_a, last_b, next_b, grad_keys_ref, grad_values_ref):
    halves, _, is_last = place(count)
    for which, ref in enumerate((grad_keys_ref, grad_values_ref)):
        sums = (
            own_a[:, which]
            + jnp.where(is_last, next_b[:, which], last_b[:, which]).astype(jnp.float32),
            own_b[:, which] + last_a[:, which].astype(jnp.float32),
        )
        for slot, total in enumerate(sums):
            ref[halves[slot], 0] = jnp.swapaxes(total, 0, 1).astype(jnp.bfloat16)


def by_half(info, final_a, final_b):
    even = info[:1].reshape((1,) * (final_a.ndim + 1)) == 1
    halves = jnp.where(even, jnp.stack([final_b, final_a]), jnp.stack([final_a, final_b]))
    halves = jnp.transpose(halves, (2, 0, 3, 1, 4))[:, :, None]
    return halves[0], halves[1]


def two_span_window(count, q_t, do_t, starts, own_a, own_b, pairs_a, pairs_b, scale):
    kv_heads, _, span, dim = own_a.shape
    heads = q_t.shape[1]
    rows = heads // kv_heads * span
    block = 2 * kv_heads * rows * span * dim
    shape = jax.ShapeDtypeStruct
    near = [shape((2, kv_heads, 2 * span, rows), jnp.float32)] * 2
    near.append(shape((2, kv_heads, 8, rows), jnp.float32))
    deeps = [shape(own_a.shape, jnp.bfloat16)] * 2
    lows = [shape((2, kv_heads, span, rows), jnp.bfloat16)] * 2
    norm = shape((2, kv_heads, 8, rows), jnp.float32)
    terms = [shape(own_a.shape, jnp.float32)] * 4
    outs = [shape(q_t.shape, jnp.bfloat16)] * 2

    both_axes = ("seq", "batch")
    swaps_b = everyone_swaps(pairs_b, count, lax.axis_size("batch"))
    last = jnp.full((dim,), lax.axis_index("seq") == count - 1).astype(jnp.int32)
    own_a, own_b, last = lax.optimization_barrier((own_a, own_b, last))
    is_last = last == 1
    b1 = lax.ppermute(own_a, both_axes, swaps_b)
    a1 = lax.ppermute(own_b, "seq", pairs_a)
    b1 = jnp.where(is_last, own_a, b1)
    b2 = lax.ppermute(lax.optimization_barrier((a1, own_b))[0], both_axes, swaps_b)
    a2 = lax.ppermute(b1, "seq", pairs_a)
    e, dp, stats = vmem_call(
        functools.partial(near_kernel, scale, count), near, 4 * block, "near",
        starts, q_t, do_t, own_a, own_b, a1, b1,
    )
    deep_a, deep_b, *far_parts = vmem_call(
        functools.partial(far_kernel, scale, count), deeps + lows + [norm], 2 * block, "far",
        starts, q_t, do_t, a1, a2, b2, stats,
    )
    from_a = lax.ppermute(deep_a, "seq", pairs_a)
    from_b = lax.ppermute(deep_b, both_axes, swaps_b)
    prev_a, prev_b, own_term_a, own_term_b, out, dq = vmem_call(
        functools.partial(rest_kernel, scale, count), terms + outs, 10 * block, "rest",
        q_t, do_t, e, dp, *far_parts, own_a, own_b, a1, b1, a2, b2,
    )
    from_a, from_b = lax.optimization_barrier((from_a, from_b))
    from_b = jnp.where(is_last, deep_b, from_b)
    next_a = (prev_a + from_b.astype(jnp.float32)).astype(jnp.bfloat16)
    next_b = (prev_b + from_a.astype(jnp.float32)).astype(jnp.bfloat16)
    last_a = lax.ppermute(next_a, "seq", pairs_a)
    last_b = lax.ppermute(next_b, both_axes, swaps_b)
    grads = [shape((2, 1, span, kv_heads, dim), jnp.bfloat16)] * 2
    grad_keys, grad_values = vmem_call(
        functools.partial(unpack_kernel, count), grads, 1024, "unpack",
        own_term_a, own_term_b, last_a, last_b, next_b,
    )
    return out, dq, grad_keys, grad_values


def any_window(info, q_t, do_t, starts, own_a, own_b, pairs_a, pairs_b, window, scale):
    kv_heads = own_a.shape[0]
    chunks = 2
    chunk = kv_heads // chunks
    parts = []
    for c in range(chunks):
        line_a = [jnp.swapaxes(own_a[c * chunk : (c + 1) * chunk], 0, 1)]
        line_b = [jnp.swapaxes(own_b[c * chunk : (c + 1) * chunk], 0, 1)]
        for _ in range(window):
            next_a = lax.ppermute(line_b[-1], "seq", pairs_a)
            next_b = lax.ppermute(line_a[-1], "seq", pairs_b)
            line_a.append(next_a)
            line_b.append(next_b)
        out, dq, now_a, now_b, rest_a, rest_b = attention_chunk(
            info, q_t, do_t, starts, (line_a, line_b), c * chunk, scale
        )
        for t in range(window - 1, -1, -1):
            from_a = lax.ppermute(now_a, "seq", pairs_a)
            from_b = lax.ppermute(now_b, "seq", pairs_b)
            now_a = (rest_a[t] + from_b.astype(jnp.float32)).astype(jnp.bfloat16)
            now_b = (rest_b[t] + from_a.astype(jnp.float32)).astype(jnp.bfloat16)
        parts.append((out, dq, now_a, now_b))
    out, dq, final_a, final_b = (jnp.concatenate(arrays, axis=1) for arrays in zip(*parts))
    return out, dq, *by_half(info, jnp.swapaxes(final_a, 0, 1), jnp.swapaxes(final_b, 0, 1))


def first_of_document(doc_starts, spans, span):
    token = spans[:, None] * span + jnp.arange(span, dtype=jnp.int32)[None, :]
    below = doc_starts[None, None, :] <= token[:, :, None]
    return jnp.max(jnp.where(below, doc_starts[None, None, :], 0), axis=2)[:, None, :]


def body(query, keys, values, grad_out, doc_starts):
    count = lax.axis_size("seq")
    device = lax.axis_index("seq")
    window = min(16, count // 2)
    span = query.shape[2]
    dim = query.shape[4]
    scale = dim ** (-0.5)
    pairs_a, pairs_b = swap_pairs(count)
    half_a = 1 - device % 2

    def payload(half):
        pair = [lax.dynamic_index_in_dim(x[:, 0], half, 0, keepdims=False) for x in (keys, values)]
        return jnp.transpose(jnp.stack(pair), (2, 0, 1, 3))

    own_a, own_b = payload(half_a), payload(1 - half_a)
    q_t = jnp.transpose(query[:, 0], (0, 2, 1, 3))
    do_t = jnp.transpose(grad_out[:, 0], (0, 2, 1, 3))
    if window == 2:
        starts = first_of_document(doc_starts, jnp.arange(2 * count, dtype=jnp.int32), span)
        out, dq, grad_keys, grad_values = two_span_window(
            count, q_t, do_t, starts, own_a, own_b, pairs_a, pairs_b, scale
        )
    else:
        spans = jnp.stack([device, 2 * count - 1 - device])
        starts = first_of_document(doc_starts, spans, span)
        span_a = jnp.where(half_a == 0, device, 2 * count - 1 - device)
        info = jnp.stack([half_a, 1 - half_a, span_a, 2 * count - 1 - span_a]).astype(jnp.int32)
        out, dq, grad_keys, grad_values = any_window(
            info, q_t, do_t, starts, own_a, own_b, pairs_a, pairs_b, window, scale
        )
    out = jnp.transpose(out, (0, 2, 1, 3))[:, None]
    dq = jnp.transpose(dq, (0, 2, 1, 3))[:, None]
    return out, dq, grad_keys, grad_values


def solution(mesh):
    spec = P("batch", "seq", None, "head", None)
    return jax.shard_map(
        body,
        mesh=mesh,
        in_specs=(spec, spec, spec, spec, P("batch")),
        out_specs=(spec, spec, spec, spec),
        check_vma=False,
    )
```

```python
import functools

import jax
import jax.numpy as jnp
from jax import lax
from jax.experimental import pallas as pl
from jax.experimental.pallas import tpu as pltpu
from jax.sharding import PartitionSpec as P

LOG2E = 1.4426950408889634
NEG = -1e30


def swap_pairs(count):
    pairs_a = []
    for i in range(0, count - 1, 2):
        pairs_a += [(i, i + 1), (i + 1, i)]
    pairs_b = []
    for i in range(1, count - 1, 2):
        pairs_b += [(i, i + 1), (i + 1, i)]
    pairs_b.append((count - 1, count - 1))
    return pairs_a, pairs_b


def everyone_swaps(pairs, count, batch):
    swaps = []
    for b in range(batch):
        lone = set(range(count)) - {source for source, target in pairs if source != target}
        swaps += [(i * batch + b, j * batch + b) for i, j in pairs if i != j]
        swaps += [(i * batch + b, i * batch + (b ^ 1)) for i in sorted(lone)]
    return swaps


def contract(lhs, rhs, lhs_dim, rhs_dim):
    return lax.dot_general(
        lhs, rhs, (((lhs_dim,), (rhs_dim,)), ((), ())), preferred_element_type=jnp.float32
    )


def attention_kernel(blocks, scale, info_ref, q_ref, do_ref, starts_ref, *refs):
    kv_refs = (refs[0:blocks], refs[blocks : 2 * blocks])
    o_ref, dq_ref = refs[2 * blocks : 2 * blocks + 2]
    deep_refs = refs[2 * blocks + 2 : 2 * blocks + 4]
    rest_refs = refs[2 * blocks + 4 : 2 * blocks + 6]
    k_all, v_all, s_all, p_all = refs[2 * blocks + 6 :]
    group, span, dim = q_ref.shape[1:]
    rows = group * span

    def each(body, init):
        if blocks <= 4:
            for t in range(blocks):
                init = body(t, init)
            return init
        return lax.fori_loop(0, blocks, body, init)

    for slot in range(2):
        half = info_ref[slot]
        span_first = info_ref[2 + slot] * span
        for t in range(blocks):
            k_all[t] = kv_refs[slot][t][0, 0]
            v_all[t] = kv_refs[slot][t][1, 0]
        queries = q_ref[half].reshape(rows, dim)
        grad_out = do_ref[half].reshape(rows, dim)
        start = starts_ref[half]
        token = span_first + lax.broadcasted_iota(jnp.int32, (1, span), 1)
        key_row = span_first + lax.broadcasted_iota(jnp.int32, (span, span), 0)

        def scores(t, top):
            key_pos = key_row - t * span
            allowed = (key_pos >= start) & (key_pos <= token)
            bias = jnp.where(allowed, 0.0, NEG)
            value = contract(k_all[t], queries, 1, 1) + jnp.concatenate([bias] * group, axis=1)
            s_all[t] = value
            return jnp.maximum(top, jnp.max(value, axis=0, keepdims=True))

        top = each(scores, jnp.full((1, rows), NEG, jnp.float32))

        def expons(t, total):
            value = jnp.exp2((s_all[t] - top) * (scale * LOG2E))
            s_all[t] = value
            return total + jnp.sum(value, axis=0, keepdims=True)

        total = each(expons, jnp.zeros((1, rows), jnp.float32))
        inverse = 1.0 / total

        def forward(t, carry):
            out, delta = carry
            weights = s_all[t] * inverse
            low = weights.astype(jnp.bfloat16)
            grad_weights = contract(v_all[t], grad_out, 1, 1)
            s_all[t] = weights
            p_all[t] = grad_weights
            delta = delta + jnp.sum(weights * grad_weights, axis=0, keepdims=True)
            out = out + contract(v_all[t], low, 0, 0)
            grad_value = contract(low, grad_out, 1, 0)
            store_term(t, 1, grad_value)
            return out, delta

        def store_term(t, which, value):
            if isinstance(t, int):
                if t == blocks - 1:
                    deep_refs[slot][which, 0] = value.astype(jnp.bfloat16)
                else:
                    rest_refs[slot][t, which, 0] = value
            else:
                @pl.when(t == blocks - 1)
                def _():
                    deep_refs[slot][which, 0] = value.astype(jnp.bfloat16)

                @pl.when(t < blocks - 1)
                def _():
                    rest_refs[slot][t, which, 0] = value

        out, delta = each(
            forward, (jnp.zeros((dim, rows), jnp.float32), jnp.zeros((1, rows), jnp.float32))
        )

        def backward(t, grad_query):
            low = (s_all[t] * (p_all[t] - delta)).astype(jnp.bfloat16)
            store_term(t, 0, contract(low, queries, 1, 0) * scale)
            return grad_query + contract(k_all[t], low, 0, 0)

        grad_query = each(backward, jnp.zeros((dim, rows), jnp.float32)) * scale
        for g in range(group):
            columns = slice(g * span, (g + 1) * span)
            o_ref[half, g] = out[:, columns].T.astype(jnp.bfloat16)
            dq_ref[half, g] = grad_query[:, columns].T.astype(jnp.bfloat16)


def attention_chunk(info, q_t, do_t, starts, kv_blocks, first_head, scale):
    blocks = len(kv_blocks[0])
    _, heads, span, dim = q_t.shape
    chunk = kv_blocks[0][0].shape[1]
    group = 4
    rows = group * span
    window = blocks - 1
    q_spec = pl.BlockSpec((2, group, span, dim), lambda m, info: (0, first_head + m, 0, 0))
    o_spec = pl.BlockSpec((2, group, span, dim), lambda m, info: (0, m, 0, 0))
    kv_spec = pl.BlockSpec((2, 1, span, dim), lambda m, info: (0, m, 0, 0))
    rest_spec = pl.BlockSpec((window, 2, 1, span, dim), lambda m, info: (0, 0, m, 0, 0))
    starts_spec = pl.BlockSpec((2, 1, span), lambda m, info: (0, 0, 0))
    deep = jax.ShapeDtypeStruct((2, chunk, span, dim), jnp.bfloat16)
    rest = jax.ShapeDtypeStruct((window, 2, chunk, span, dim), jnp.float32)
    out = jax.ShapeDtypeStruct((2, chunk * group, span, dim), jnp.bfloat16)
    macs = 2 * chunk * 5 * rows * blocks * span * dim
    return pl.pallas_call(
        functools.partial(attention_kernel, blocks, scale),
        grid_spec=pltpu.PrefetchScalarGridSpec(
            num_scalar_prefetch=1,
            grid=(chunk,),
            in_specs=[q_spec, q_spec, starts_spec] + [kv_spec] * (2 * blocks),
            out_specs=[o_spec, o_spec, kv_spec, kv_spec, rest_spec, rest_spec],
            scratch_shapes=[
                pltpu.VMEM((blocks, span, dim), jnp.bfloat16),
                pltpu.VMEM((blocks, span, dim), jnp.bfloat16),
                pltpu.VMEM((blocks, span, rows), jnp.float32),
                pltpu.VMEM((blocks, span, rows), jnp.float32),
            ],
        ),
        out_shape=[out, out, deep, deep, rest, rest],
        compiler_params=pltpu.CompilerParams(vmem_limit_bytes=48 * 1024 * 1024),
        cost_estimate=pl.CostEstimate(
            flops=2 * macs, bytes_accessed=8 * 1024 * 1024, transcendentals=0
        ),
        name="attention",
    )(info, q_t, do_t, starts, *kv_blocks[0], *kv_blocks[1])


def vmem_call(kernel, out_shape, macs, name, *args, aliases=None):
    whole = pl.BlockSpec(memory_space=pltpu.VMEM)
    moved = sum(a.size * a.dtype.itemsize for a in args)
    return pl.pallas_call(
        kernel,
        in_specs=[whole] * len(args),
        out_specs=[whole] * len(out_shape),
        out_shape=out_shape,
        input_output_aliases=aliases or {},
        compiler_params=pltpu.CompilerParams(vmem_limit_bytes=16 * 1024 * 1024),
        cost_estimate=pl.CostEstimate(flops=8 * macs, bytes_accessed=moved, transcendentals=0),
        name=name,
    )(*args)


def place(count):
    device = lax.axis_index("seq")
    half_a = 1 - device % 2
    span_a = jnp.where(half_a == 0, device, 2 * count - 1 - device)
    return (half_a, 1 - half_a), (span_a, 2 * count - 1 - span_a), device == count - 1


def group_of(ref, half, m, group):
    return ref[half, pl.ds(m * group, group)].reshape(group * ref.shape[2], ref.shape[3])


def near_kernel(scale, count, starts_ref, q_ref, do_ref, own_a, own_b, prev_a, prev_b, e_ref, dp_ref, stats_ref):
    heads, span, rows = e_ref.shape[1], e_ref.shape[2] // 2, e_ref.shape[3]
    group = rows // span
    row = lax.broadcasted_iota(jnp.int32, (span, span), 0)
    column = lax.broadcasted_iota(jnp.int32, (span, span), 1)
    slots = range(2)
    kv_refs = ((prev_a, own_a), (prev_b, own_b))
    halves, spans, _ = place(count)
    biases = []
    for slot in slots:
        first = spans[slot] * span
        start = starts_ref[spans[slot]]
        prev_bias = jnp.where(first - span + row >= start, 0.0, NEG)
        own_bias = jnp.where((first + row >= start) & (row <= column), 0.0, NEG)
        biases.append(jnp.concatenate([prev_bias, own_bias], axis=0))

    def one_head(m, carry):
        scores, grads = [], []
        for i in slots:
            keys, values = (
                jnp.concatenate([ref[m, which] for ref in kv_refs[i]], axis=0) for which in range(2)
            )
            scores.append(contract(keys, group_of(q_ref, halves[i], m, group), 1, 1))
            grads.append(contract(values, group_of(do_ref, halves[i], m, group), 1, 1))
        scores = [x + jnp.concatenate([biases[i]] * group, axis=1) for i, x in enumerate(scores)]
        top = [jnp.max(x, axis=0, keepdims=True) for x in scores]
        e = [jnp.exp2((scores[i] - top[i]) * (scale * LOG2E)) for i in slots]
        for i in slots:
            e_ref[i, m] = e[i]
            dp_ref[i, m] = grads[i]
            stats_ref[i, m, 0:1] = top[i]
            stats_ref[i, m, 1:2] = jnp.sum(e[i], axis=0, keepdims=True)
            stats_ref[i, m, 2:3] = jnp.sum(e[i] * grads[i], axis=0, keepdims=True)
        return carry

    lax.fori_loop(0, heads, one_head, 0)


def far_kernel(scale, count, starts_ref, q_ref, do_ref, prev_a, far_a, far_b, stats_ref, deep_a, deep_b,
               low_ref, ds_ref, norm_ref):
    heads, span, rows = low_ref.shape[1:]
    group = rows // span
    row = lax.broadcasted_iota(jnp.int32, (span, span), 0)
    column = lax.broadcasted_iota(jnp.int32, (span, span), 1)
    factor = scale * LOG2E
    slots = range(2)
    halves, spans, is_last = place(count)
    biases = []
    for slot in slots:
        first = spans[slot] * span
        allowed = (first - 2 * span + row >= starts_ref[spans[slot]]) & (row > column)
        biases.append(jnp.where(allowed, 0.0, NEG))
    deep_refs = (deep_a, deep_b)


    def one_head(m, carry):
        far_kv = [far_a[m], jnp.where(is_last, prev_a[m], far_b[m])]
        queries = [group_of(q_ref, halves[i], m, group) for i in slots]
        grad_out = [group_of(do_ref, halves[i], m, group) for i in slots]
        scores = [
            contract(far_kv[i][0], queries[i], 1, 1)
            + jnp.concatenate([biases[i]] * group, axis=1)
            for i in slots
        ]
        grads = [contract(far_kv[i][1], grad_out[i], 1, 1) for i in slots]
        near_top = [stats_ref[i, m, 0:1] for i in slots]
        top = [
            jnp.maximum(near_top[i], jnp.max(scores[i], axis=0, keepdims=True)) for i in slots
        ]
        near = [jnp.exp2((near_top[i] - top[i]) * factor) for i in slots]
        e = [jnp.exp2((scores[i] - top[i]) * factor) for i in slots]
        inverse = [
            1.0 / (near[i] * stats_ref[i, m, 1:2] + jnp.sum(e[i], axis=0, keepdims=True))
            for i in slots
        ]
        delta = [
            (
                near[i] * stats_ref[i, m, 2:3]
                + jnp.sum(e[i] * grads[i], axis=0, keepdims=True)
            )
            * inverse[i]
            for i in slots
        ]
        weights = [e[i] * inverse[i] for i in slots]
        low = [x.astype(jnp.bfloat16) for x in weights]
        ds = [(weights[i] * (grads[i] - delta[i])).astype(jnp.bfloat16) for i in slots]
        for i in slots:
            low_ref[i, m] = low[i]
            ds_ref[i, m] = ds[i]
            norm_ref[i, m, 0:1] = near[i] * inverse[i]
            norm_ref[i, m, 1:2] = delta[i]
        for i in slots:
            deep_refs[i][m, 0] = (contract(ds[i], queries[i], 1, 0) * scale).astype(jnp.bfloat16)
            deep_refs[i][m, 1] = contract(low[i], grad_out[i], 1, 0).astype(jnp.bfloat16)
        return carry

    lax.fori_loop(0, heads, one_head, 0, unroll=True)


def rest_kernel(scale, count, q_ref, do_ref, e_ref, dp_ref, *refs):
    far_low, far_ds, norm = refs[:3]
    own_kv, prev_kv, far_kv = refs[3:5], refs[5:7], refs[7:9]
    prev_refs, own_refs = refs[9:11], refs[11:13]
    o_ref, dq_ref = refs[13:]
    halves, _, is_last = place(count)
    heads, span, rows = e_ref.shape[1], e_ref.shape[2] // 2, e_ref.shape[3]
    group = rows // span
    slots = range(2)

    def one_head(m, carry):
        queries = [group_of(q_ref, halves[i], m, group) for i in slots]
        grad_out = [group_of(do_ref, halves[i], m, group) for i in slots]
        low, ds = [], []
        for i in slots:
            weights = e_ref[i, m] * norm[i, m, 0:1]
            near_ds = (weights * (dp_ref[i, m] - norm[i, m, 1:2])).astype(jnp.bfloat16)
            low.append(jnp.concatenate([weights.astype(jnp.bfloat16), far_low[i, m]], axis=0))
            ds.append(jnp.concatenate([near_ds, far_ds[i, m]], axis=0))
        for i in slots:
            grad_key = contract(ds[i][: 2 * span], queries[i], 1, 0) * scale
            grad_value = contract(low[i][: 2 * span], grad_out[i], 1, 0)
            prev_refs[i][m, 0] = grad_key[:span]
            prev_refs[i][m, 1] = grad_value[:span]
            own_refs[i][m, 0] = grad_key[span:]
            own_refs[i][m, 1] = grad_value[span:]
        for i in slots:
            half = halves[i]
            far = far_kv[0][m] if i == 0 else jnp.where(is_last, prev_kv[0][m], far_kv[1][m])
            keys, values = (
                jnp.concatenate([prev_kv[i][m, which], own_kv[i][m, which], far[which]], axis=0)
                for which in range(2)
            )
            out = contract(values, low[i], 0, 0)
            grad_query = contract(keys, ds[i], 0, 0) * scale
            for g in range(group):
                columns = slice(g * span, (g + 1) * span)
                o_ref[half, m * group + g] = out[:, columns].T.astype(jnp.bfloat16)
                dq_ref[half, m * group + g] = grad_query[:, columns].T.astype(jnp.bfloat16)
        return carry

    lax.fori_loop(0, heads, one_head, 0)


def merge_kernel(count, prev_a, prev_b, from_a, from_b, deep_b, next_a_ref, next_b_ref):
    _, _, is_last = place(count)
    from_far = jnp.where(is_last, deep_b[...], from_b[...])
    next_a_ref[...] = (prev_a[...] + from_far.astype(jnp.float32)).astype(jnp.bfloat16)
    next_b_ref[...] = (prev_b[...] + from_a[...].astype(jnp.float32)).astype(jnp.bfloat16)


def unpack_kernel(count, own_a, own_b, last_a, last_b, next_b, grad_keys_ref, grad_values_ref):
    halves, _, is_last = place(count)
    for which, ref in enumerate((grad_keys_ref, grad_values_ref)):
        sums = (
            own_a[:, which]
            + jnp.where(is_last, next_b[:, which], last_b[:, which]).astype(jnp.float32),
            own_b[:, which] + last_a[:, which].astype(jnp.float32),
        )
        for slot, total in enumerate(sums):
            ref[halves[slot], 0] = jnp.swapaxes(total, 0, 1).astype(jnp.bfloat16)


def by_half(info, final_a, final_b):
    even = info[:1].reshape((1,) * (final_a.ndim + 1)) == 1
    halves = jnp.where(even, jnp.stack([final_b, final_a]), jnp.stack([final_a, final_b]))
    halves = jnp.transpose(halves, (2, 0, 3, 1, 4))[:, :, None]
    return halves[0], halves[1]


def two_span_window(count, q_t, do_t, starts, own_a, own_b, pairs_a, pairs_b, scale):
    kv_heads, _, span, dim = own_a.shape
    heads = q_t.shape[1]
    rows = heads // kv_heads * span
    block = 2 * kv_heads * rows * span * dim
    shape = jax.ShapeDtypeStruct
    near = [shape((2, kv_heads, 2 * span, rows), jnp.float32)] * 2
    near.append(shape((2, kv_heads, 8, rows), jnp.float32))
    deeps = [shape(own_a.shape, jnp.bfloat16)] * 2
    lows = [shape((2, kv_heads, span, rows), jnp.bfloat16)] * 2
    norm = shape((2, kv_heads, 8, rows), jnp.float32)
    terms = [shape(own_a.shape, jnp.float32)] * 4
    outs = [shape(q_t.shape, jnp.bfloat16)] * 2

    both_axes = ("seq", "batch")
    swaps_b = everyone_swaps(pairs_b, count, lax.axis_size("batch"))
    last = jnp.full((dim,), lax.axis_index("seq") == count - 1).astype(jnp.int32)
    own_a, own_b, last = lax.optimization_barrier((own_a, own_b, last))
    is_last = last == 1
    b1 = lax.ppermute(own_a, both_axes, swaps_b)
    a1 = lax.ppermute(own_b, "seq", pairs_a)
    b1 = jnp.where(is_last, own_a, b1)
    b2 = lax.ppermute(lax.optimization_barrier((a1, own_b))[0], both_axes, swaps_b)
    a2 = lax.ppermute(b1, "seq", pairs_a)
    e, dp, stats = vmem_call(
        functools.partial(near_kernel, scale, count), near, 4 * block, "near",
        starts, q_t, do_t, own_a, own_b, a1, b1,
    )
    deep_a, deep_b, *far_parts = vmem_call(
        functools.partial(far_kernel, scale, count), deeps + lows + [norm], 2 * block, "far",
        starts, q_t, do_t, a1, a2, b2, stats,
    )
    from_a = lax.ppermute(deep_a, "seq", pairs_a)
    from_b = lax.ppermute(deep_b, both_axes, swaps_b)
    prev_a, prev_b, own_term_a, own_term_b, out, dq = vmem_call(
        functools.partial(rest_kernel, scale, count), terms + outs, 10 * block, "rest",
        q_t, do_t, e, dp, *far_parts, own_a, own_b, a1, b1, a2, b2,
    )
    next_a, next_b = vmem_call(
        functools.partial(merge_kernel, count), deeps, 1024, "merge",
        prev_a, prev_b, from_a, from_b, deep_b,
    )
    last_a = lax.ppermute(next_a, "seq", pairs_a)
    last_b = lax.ppermute(next_b, both_axes, swaps_b)
    grads = [shape((2, 1, span, kv_heads, dim), jnp.bfloat16)] * 2
    grad_keys, grad_values = vmem_call(
        functools.partial(unpack_kernel, count), grads, 1024, "unpack",
        own_term_a, own_term_b, last_a, last_b, next_b,
    )
    return out, dq, grad_keys, grad_values


def any_window(info, q_t, do_t, starts, own_a, own_b, pairs_a, pairs_b, window, scale):
    kv_heads = own_a.shape[0]
    chunks = 2
    chunk = kv_heads // chunks
    parts = []
    for c in range(chunks):
        line_a = [jnp.swapaxes(own_a[c * chunk : (c + 1) * chunk], 0, 1)]
        line_b = [jnp.swapaxes(own_b[c * chunk : (c + 1) * chunk], 0, 1)]
        for _ in range(window):
            next_a = lax.ppermute(line_b[-1], "seq", pairs_a)
            next_b = lax.ppermute(line_a[-1], "seq", pairs_b)
            line_a.append(next_a)
            line_b.append(next_b)
        out, dq, now_a, now_b, rest_a, rest_b = attention_chunk(
            info, q_t, do_t, starts, (line_a, line_b), c * chunk, scale
        )
        for t in range(window - 1, -1, -1):
            from_a = lax.ppermute(now_a, "seq", pairs_a)
            from_b = lax.ppermute(now_b, "seq", pairs_b)
            now_a = (rest_a[t] + from_b.astype(jnp.float32)).astype(jnp.bfloat16)
            now_b = (rest_b[t] + from_a.astype(jnp.float32)).astype(jnp.bfloat16)
        parts.append((out, dq, now_a, now_b))
    out, dq, final_a, final_b = (jnp.concatenate(arrays, axis=1) for arrays in zip(*parts))
    return out, dq, *by_half(info, jnp.swapaxes(final_a, 0, 1), jnp.swapaxes(final_b, 0, 1))


def first_of_document(doc_starts, spans, span):
    token = spans[:, None] * span + jnp.arange(span, dtype=jnp.int32)[None, :]
    below = doc_starts[None, None, :] <= token[:, :, None]
    return jnp.max(jnp.where(below, doc_starts[None, None, :], 0), axis=2)[:, None, :]


def body(query, keys, values, grad_out, doc_starts):
    count = lax.axis_size("seq")
    device = lax.axis_index("seq")
    window = min(16, count // 2)
    span = query.shape[2]
    dim = query.shape[4]
    scale = dim ** (-0.5)
    pairs_a, pairs_b = swap_pairs(count)
    half_a = 1 - device % 2

    def payload(half):
        pair = [lax.dynamic_index_in_dim(x[:, 0], half, 0, keepdims=False) for x in (keys, values)]
        return jnp.transpose(jnp.stack(pair), (2, 0, 1, 3))

    own_a, own_b = payload(half_a), payload(1 - half_a)
    q_t = jnp.transpose(query[:, 0], (0, 2, 1, 3))
    do_t = jnp.transpose(grad_out[:, 0], (0, 2, 1, 3))
    if window == 2:
        starts = first_of_document(doc_starts, jnp.arange(2 * count, dtype=jnp.int32), span)
        out, dq, grad_keys, grad_values = two_span_window(
            count, q_t, do_t, starts, own_a, own_b, pairs_a, pairs_b, scale
        )
    else:
        spans = jnp.stack([device, 2 * count - 1 - device])
        starts = first_of_document(doc_starts, spans, span)
        span_a = jnp.where(half_a == 0, device, 2 * count - 1 - device)
        info = jnp.stack([half_a, 1 - half_a, span_a, 2 * count - 1 - span_a]).astype(jnp.int32)
        out, dq, grad_keys, grad_values = any_window(
            info, q_t, do_t, starts, own_a, own_b, pairs_a, pairs_b, window, scale
        )
    out = jnp.transpose(out, (0, 2, 1, 3))[:, None]
    dq = jnp.transpose(dq, (0, 2, 1, 3))[:, None]
    return out, dq, grad_keys, grad_values


def solution(mesh):
    spec = P("batch", "seq", None, "head", None)
    return jax.shard_map(
        body,
        mesh=mesh,
        in_specs=(spec, spec, spec, spec, P("batch")),
        out_specs=(spec, spec, spec, spec),
        check_vma=False,
    )
```

```python
import functools

import jax
import jax.numpy as jnp
from jax import lax
from jax.experimental import pallas as pl
from jax.experimental.pallas import tpu as pltpu
from jax.sharding import PartitionSpec as P

LOG2E = 1.4426950408889634
NEG = -1e30


def swap_pairs(count):
    pairs_a = []
    for i in range(0, count - 1, 2):
        pairs_a += [(i, i + 1), (i + 1, i)]
    pairs_b = []
    for i in range(1, count - 1, 2):
        pairs_b += [(i, i + 1), (i + 1, i)]
    pairs_b.append((count - 1, count - 1))
    return pairs_a, pairs_b


def everyone_swaps(pairs, count, batch):
    swaps = []
    for b in range(batch):
        lone = set(range(count)) - {source for source, target in pairs if source != target}
        swaps += [(i * batch + b, j * batch + b) for i, j in pairs if i != j]
        swaps += [(i * batch + b, i * batch + (b ^ 1)) for i in sorted(lone)]
    return swaps


def contract(lhs, rhs, lhs_dim, rhs_dim):
    return lax.dot_general(
        lhs, rhs, (((lhs_dim,), (rhs_dim,)), ((), ())), preferred_element_type=jnp.float32
    )


def attention_kernel(blocks, scale, info_ref, q_ref, do_ref, starts_ref, *refs):
    kv_refs = (refs[0:blocks], refs[blocks : 2 * blocks])
    o_ref, dq_ref = refs[2 * blocks : 2 * blocks + 2]
    deep_refs = refs[2 * blocks + 2 : 2 * blocks + 4]
    rest_refs = refs[2 * blocks + 4 : 2 * blocks + 6]
    k_all, v_all, s_all, p_all = refs[2 * blocks + 6 :]
    group, span, dim = q_ref.shape[1:]
    rows = group * span

    def each(body, init):
        if blocks <= 4:
            for t in range(blocks):
                init = body(t, init)
            return init
        return lax.fori_loop(0, blocks, body, init)

    for slot in range(2):
        half = info_ref[slot]
        span_first = info_ref[2 + slot] * span
        for t in range(blocks):
            k_all[t] = kv_refs[slot][t][0, 0]
            v_all[t] = kv_refs[slot][t][1, 0]
        queries = q_ref[half].reshape(rows, dim)
        grad_out = do_ref[half].reshape(rows, dim)
        start = starts_ref[half]
        token = span_first + lax.broadcasted_iota(jnp.int32, (1, span), 1)
        key_row = span_first + lax.broadcasted_iota(jnp.int32, (span, span), 0)

        def scores(t, top):
            key_pos = key_row - t * span
            allowed = (key_pos >= start) & (key_pos <= token)
            bias = jnp.where(allowed, 0.0, NEG)
            value = contract(k_all[t], queries, 1, 1) + jnp.concatenate([bias] * group, axis=1)
            s_all[t] = value
            return jnp.maximum(top, jnp.max(value, axis=0, keepdims=True))

        top = each(scores, jnp.full((1, rows), NEG, jnp.float32))

        def expons(t, total):
            value = jnp.exp2((s_all[t] - top) * (scale * LOG2E))
            s_all[t] = value
            return total + jnp.sum(value, axis=0, keepdims=True)

        total = each(expons, jnp.zeros((1, rows), jnp.float32))
        inverse = 1.0 / total

        def forward(t, carry):
            out, delta = carry
            weights = s_all[t] * inverse
            low = weights.astype(jnp.bfloat16)
            grad_weights = contract(v_all[t], grad_out, 1, 1)
            s_all[t] = weights
            p_all[t] = grad_weights
            delta = delta + jnp.sum(weights * grad_weights, axis=0, keepdims=True)
            out = out + contract(v_all[t], low, 0, 0)
            grad_value = contract(low, grad_out, 1, 0)
            store_term(t, 1, grad_value)
            return out, delta

        def store_term(t, which, value):
            if isinstance(t, int):
                if t == blocks - 1:
                    deep_refs[slot][which, 0] = value.astype(jnp.bfloat16)
                else:
                    rest_refs[slot][t, which, 0] = value
            else:
                @pl.when(t == blocks - 1)
                def _():
                    deep_refs[slot][which, 0] = value.astype(jnp.bfloat16)

                @pl.when(t < blocks - 1)
                def _():
                    rest_refs[slot][t, which, 0] = value

        out, delta = each(
            forward, (jnp.zeros((dim, rows), jnp.float32), jnp.zeros((1, rows), jnp.float32))
        )

        def backward(t, grad_query):
            low = (s_all[t] * (p_all[t] - delta)).astype(jnp.bfloat16)
            store_term(t, 0, contract(low, queries, 1, 0) * scale)
            return grad_query + contract(k_all[t], low, 0, 0)

        grad_query = each(backward, jnp.zeros((dim, rows), jnp.float32)) * scale
        for g in range(group):
            columns = slice(g * span, (g + 1) * span)
            o_ref[half, g] = out[:, columns].T.astype(jnp.bfloat16)
            dq_ref[half, g] = grad_query[:, columns].T.astype(jnp.bfloat16)


def attention_chunk(info, q_t, do_t, starts, kv_blocks, first_head, scale):
    blocks = len(kv_blocks[0])
    _, heads, span, dim = q_t.shape
    chunk = kv_blocks[0][0].shape[1]
    group = 4
    rows = group * span
    window = blocks - 1
    q_spec = pl.BlockSpec((2, group, span, dim), lambda m, info: (0, first_head + m, 0, 0))
    o_spec = pl.BlockSpec((2, group, span, dim), lambda m, info: (0, m, 0, 0))
    kv_spec = pl.BlockSpec((2, 1, span, dim), lambda m, info: (0, m, 0, 0))
    rest_spec = pl.BlockSpec((window, 2, 1, span, dim), lambda m, info: (0, 0, m, 0, 0))
    starts_spec = pl.BlockSpec((2, 1, span), lambda m, info: (0, 0, 0))
    deep = jax.ShapeDtypeStruct((2, chunk, span, dim), jnp.bfloat16)
    rest = jax.ShapeDtypeStruct((window, 2, chunk, span, dim), jnp.float32)
    out = jax.ShapeDtypeStruct((2, chunk * group, span, dim), jnp.bfloat16)
    macs = 2 * chunk * 5 * rows * blocks * span * dim
    return pl.pallas_call(
        functools.partial(attention_kernel, blocks, scale),
        grid_spec=pltpu.PrefetchScalarGridSpec(
            num_scalar_prefetch=1,
            grid=(chunk,),
            in_specs=[q_spec, q_spec, starts_spec] + [kv_spec] * (2 * blocks),
            out_specs=[o_spec, o_spec, kv_spec, kv_spec, rest_spec, rest_spec],
            scratch_shapes=[
                pltpu.VMEM((blocks, span, dim), jnp.bfloat16),
                pltpu.VMEM((blocks, span, dim), jnp.bfloat16),
                pltpu.VMEM((blocks, span, rows), jnp.float32),
                pltpu.VMEM((blocks, span, rows), jnp.float32),
            ],
        ),
        out_shape=[out, out, deep, deep, rest, rest],
        compiler_params=pltpu.CompilerParams(vmem_limit_bytes=48 * 1024 * 1024),
        cost_estimate=pl.CostEstimate(
            flops=2 * macs, bytes_accessed=8 * 1024 * 1024, transcendentals=0
        ),
        name="attention",
    )(info, q_t, do_t, starts, *kv_blocks[0], *kv_blocks[1])


def vmem_call(kernel, out_shape, macs, name, *args, aliases=None):
    whole = pl.BlockSpec(memory_space=pltpu.VMEM)
    moved = sum(a.size * a.dtype.itemsize for a in args)
    return pl.pallas_call(
        kernel,
        in_specs=[whole] * len(args),
        out_specs=[whole] * len(out_shape),
        out_shape=out_shape,
        input_output_aliases=aliases or {},
        compiler_params=pltpu.CompilerParams(vmem_limit_bytes=16 * 1024 * 1024),
        cost_estimate=pl.CostEstimate(flops=8 * macs, bytes_accessed=moved, transcendentals=0),
        name=name,
    )(*args)


def place(count):
    device = lax.axis_index("seq")
    half_a = 1 - device % 2
    span_a = jnp.where(half_a == 0, device, 2 * count - 1 - device)
    return (half_a, 1 - half_a), (span_a, 2 * count - 1 - span_a), device == count - 1


def group_of(ref, half, m, group):
    return ref[half, pl.ds(m * group, group)].reshape(group * ref.shape[2], ref.shape[3])


def near_kernel(scale, count, starts_ref, q_ref, do_ref, own_a, own_b, prev_a, prev_b, e_ref, dp_ref, stats_ref):
    heads, span, rows = e_ref.shape[1], e_ref.shape[2] // 2, e_ref.shape[3]
    group = rows // span
    row = lax.broadcasted_iota(jnp.int32, (span, span), 0)
    column = lax.broadcasted_iota(jnp.int32, (span, span), 1)
    slots = range(2)
    kv_refs = ((prev_a, own_a), (prev_b, own_b))
    halves, spans, _ = place(count)
    biases = []
    for slot in slots:
        first = spans[slot] * span
        start = starts_ref[spans[slot]]
        prev_bias = jnp.where(first - span + row >= start, 0.0, NEG)
        own_bias = jnp.where((first + row >= start) & (row <= column), 0.0, NEG)
        biases.append(jnp.concatenate([prev_bias, own_bias], axis=0))

    def one_head(m, carry):
        scores, grads = [], []
        for i in slots:
            keys, values = (
                jnp.concatenate([ref[m, which] for ref in kv_refs[i]], axis=0) for which in range(2)
            )
            scores.append(contract(keys, group_of(q_ref, halves[i], m, group), 1, 1))
            grads.append(contract(values, group_of(do_ref, halves[i], m, group), 1, 1))
        scores = [x + jnp.concatenate([biases[i]] * group, axis=1) for i, x in enumerate(scores)]
        top = [jnp.max(x, axis=0, keepdims=True) for x in scores]
        e = [jnp.exp2((scores[i] - top[i]) * (scale * LOG2E)) for i in slots]
        for i in slots:
            e_ref[i, m] = e[i]
            dp_ref[i, m] = grads[i]
            stats_ref[i, m, 0:1] = top[i]
            stats_ref[i, m, 1:2] = jnp.sum(e[i], axis=0, keepdims=True)
            stats_ref[i, m, 2:3] = jnp.sum(e[i] * grads[i], axis=0, keepdims=True)
        return carry

    lax.fori_loop(0, heads, one_head, 0)


def far_kernel(scale, count, starts_ref, q_ref, do_ref, prev_a, far_a, far_b, stats_ref, deep_a, deep_b,
               low_ref, ds_ref, norm_ref):
    heads, span, rows = low_ref.shape[1:]
    group = rows // span
    row = lax.broadcasted_iota(jnp.int32, (span, span), 0)
    column = lax.broadcasted_iota(jnp.int32, (span, span), 1)
    factor = scale * LOG2E
    slots = range(2)
    halves, spans, is_last = place(count)
    biases = []
    for slot in slots:
        first = spans[slot] * span
        allowed = (first - 2 * span + row >= starts_ref[spans[slot]]) & (row > column)
        biases.append(jnp.where(allowed, 0.0, NEG))
    deep_refs = (deep_a, deep_b)


    def one_head(m, carry):
        far_kv = [far_a[m], jnp.where(is_last, prev_a[m], far_b[m])]
        queries = [group_of(q_ref, halves[i], m, group) for i in slots]
        grad_out = [group_of(do_ref, halves[i], m, group) for i in slots]
        scores = [
            contract(far_kv[i][0], queries[i], 1, 1)
            + jnp.concatenate([biases[i]] * group, axis=1)
            for i in slots
        ]
        grads = [contract(far_kv[i][1], grad_out[i], 1, 1) for i in slots]
        near_top = [stats_ref[i, m, 0:1] for i in slots]
        top = [
            jnp.maximum(near_top[i], jnp.max(scores[i], axis=0, keepdims=True)) for i in slots
        ]
        near = [jnp.exp2((near_top[i] - top[i]) * factor) for i in slots]
        e = [jnp.exp2((scores[i] - top[i]) * factor) for i in slots]
        inverse = [
            1.0 / (near[i] * stats_ref[i, m, 1:2] + jnp.sum(e[i], axis=0, keepdims=True))
            for i in slots
        ]
        delta = [
            (
                near[i] * stats_ref[i, m, 2:3]
                + jnp.sum(e[i] * grads[i], axis=0, keepdims=True)
            )
            * inverse[i]
            for i in slots
        ]
        weights = [e[i] * inverse[i] for i in slots]
        low = [x.astype(jnp.bfloat16) for x in weights]
        ds = [(weights[i] * (grads[i] - delta[i])).astype(jnp.bfloat16) for i in slots]
        for i in slots:
            low_ref[i, m] = low[i]
            ds_ref[i, m] = ds[i]
            norm_ref[i, m, 0:1] = near[i] * inverse[i]
            norm_ref[i, m, 1:2] = delta[i]
        for i in slots:
            deep_refs[i][m, 0] = (contract(ds[i], queries[i], 1, 0) * scale).astype(jnp.bfloat16)
            deep_refs[i][m, 1] = contract(low[i], grad_out[i], 1, 0).astype(jnp.bfloat16)
        return carry

    lax.fori_loop(0, heads, one_head, 0, unroll=True)


def rest_kernel(scale, count, q_ref, do_ref, e_ref, dp_ref, *refs):
    far_low, far_ds, norm = refs[:3]
    own_kv, prev_kv, far_kv = refs[3:5], refs[5:7], refs[7:9]
    prev_refs, own_refs = refs[9:11], refs[11:13]
    o_ref, dq_ref = refs[13:]
    halves, _, is_last = place(count)
    heads, span, rows = e_ref.shape[1], e_ref.shape[2] // 2, e_ref.shape[3]
    group = rows // span
    slots = range(2)

    def one_head(m, carry):
        queries = [group_of(q_ref, halves[i], m, group) for i in slots]
        grad_out = [group_of(do_ref, halves[i], m, group) for i in slots]
        low, ds = [], []
        for i in slots:
            weights = e_ref[i, m] * norm[i, m, 0:1]
            near_ds = (weights * (dp_ref[i, m] - norm[i, m, 1:2])).astype(jnp.bfloat16)
            low.append(jnp.concatenate([weights.astype(jnp.bfloat16), far_low[i, m]], axis=0))
            ds.append(jnp.concatenate([near_ds, far_ds[i, m]], axis=0))
        for i in slots:
            grad_key = contract(ds[i][: 2 * span], queries[i], 1, 0) * scale
            grad_value = contract(low[i][: 2 * span], grad_out[i], 1, 0)
            prev_refs[i][m, 0] = grad_key[:span]
            prev_refs[i][m, 1] = grad_value[:span]
            own_refs[i][m, 0] = grad_key[span:]
            own_refs[i][m, 1] = grad_value[span:]
        for i in slots:
            half = halves[i]
            far = far_kv[0][m] if i == 0 else jnp.where(is_last, prev_kv[0][m], far_kv[1][m])
            keys, values = (
                jnp.concatenate([prev_kv[i][m, which], own_kv[i][m, which], far[which]], axis=0)
                for which in range(2)
            )
            out = contract(values, low[i], 0, 0)
            grad_query = contract(keys, ds[i], 0, 0) * scale
            for g in range(group):
                columns = slice(g * span, (g + 1) * span)
                o_ref[half, m * group + g] = out[:, columns].T.astype(jnp.bfloat16)
                dq_ref[half, m * group + g] = grad_query[:, columns].T.astype(jnp.bfloat16)
        return carry

    lax.fori_loop(0, heads, one_head, 0)


def merge_kernel(count, prev_a, prev_b, from_a, from_b, deep_b, next_a_ref, next_b_ref):
    _, _, is_last = place(count)
    from_far = jnp.where(is_last, deep_b[...], from_b[...])
    next_a_ref[...] = (prev_a[...] + from_far.astype(jnp.float32)).astype(jnp.bfloat16)
    next_b_ref[...] = (prev_b[...] + from_a[...].astype(jnp.float32)).astype(jnp.bfloat16)


def unpack_kernel(count, own_a, own_b, last_a, last_b, next_b, grad_keys_ref, grad_values_ref):
    halves, _, is_last = place(count)
    for which, ref in enumerate((grad_keys_ref, grad_values_ref)):
        sums = (
            own_a[:, which]
            + jnp.where(is_last, next_b[:, which], last_b[:, which]).astype(jnp.float32),
            own_b[:, which] + last_a[:, which].astype(jnp.float32),
        )
        for slot, total in enumerate(sums):
            ref[halves[slot], 0] = jnp.swapaxes(total.astype(jnp.bfloat16), 0, 1)


def by_half(info, final_a, final_b):
    even = info[:1].reshape((1,) * (final_a.ndim + 1)) == 1
    halves = jnp.where(even, jnp.stack([final_b, final_a]), jnp.stack([final_a, final_b]))
    halves = jnp.transpose(halves, (2, 0, 3, 1, 4))[:, :, None]
    return halves[0], halves[1]


def two_span_window(count, q_t, do_t, starts, own_a, own_b, pairs_a, pairs_b, scale):
    kv_heads, _, span, dim = own_a.shape
    heads = q_t.shape[1]
    rows = heads // kv_heads * span
    block = 2 * kv_heads * rows * span * dim
    shape = jax.ShapeDtypeStruct
    near = [shape((2, kv_heads, 2 * span, rows), jnp.float32)] * 2
    near.append(shape((2, kv_heads, 8, rows), jnp.float32))
    deeps = [shape(own_a.shape, jnp.bfloat16)] * 2
    lows = [shape((2, kv_heads, span, rows), jnp.bfloat16)] * 2
    norm = shape((2, kv_heads, 8, rows), jnp.float32)
    terms = [shape(own_a.shape, jnp.float32)] * 4
    outs = [shape(q_t.shape, jnp.bfloat16)] * 2

    both_axes = ("seq", "batch")
    swaps_b = everyone_swaps(pairs_b, count, lax.axis_size("batch"))
    last = jnp.full((dim,), lax.axis_index("seq") == count - 1).astype(jnp.int32)
    own_a, own_b, last = lax.optimization_barrier((own_a, own_b, last))
    is_last = last == 1
    b1 = lax.ppermute(own_a, both_axes, swaps_b)
    a1 = lax.ppermute(own_b, "seq", pairs_a)
    b1 = jnp.where(is_last, own_a, b1)
    b2 = lax.ppermute(lax.optimization_barrier((a1, own_b))[0], both_axes, swaps_b)
    a2 = lax.ppermute(b1, "seq", pairs_a)
    e, dp, stats = vmem_call(
        functools.partial(near_kernel, scale, count), near, 4 * block, "near",
        starts, q_t, do_t, own_a, own_b, a1, b1,
    )
    deep_a, deep_b, *far_parts = vmem_call(
        functools.partial(far_kernel, scale, count), deeps + lows + [norm], 2 * block, "far",
        starts, q_t, do_t, a1, a2, b2, stats,
    )
    from_a = lax.ppermute(deep_a, "seq", pairs_a)
    from_b = lax.ppermute(deep_b, both_axes, swaps_b)
    prev_a, prev_b, own_term_a, own_term_b, out, dq = vmem_call(
        functools.partial(rest_kernel, scale, count), terms + outs, 10 * block, "rest",
        q_t, do_t, e, dp, *far_parts, own_a, own_b, a1, b1, a2, b2,
    )
    next_a, next_b = vmem_call(
        functools.partial(merge_kernel, count), deeps, 1024, "merge",
        prev_a, prev_b, from_a, from_b, deep_b,
    )
    last_a = lax.ppermute(next_a, "seq", pairs_a)
    last_b = lax.ppermute(next_b, both_axes, swaps_b)
    grads = [shape((2, 1, span, kv_heads, dim), jnp.bfloat16)] * 2
    grad_keys, grad_values = vmem_call(
        functools.partial(unpack_kernel, count), grads, 1024, "unpack",
        own_term_a, own_term_b, last_a, last_b, next_b,
    )
    return out, dq, grad_keys, grad_values


def any_window(info, q_t, do_t, starts, own_a, own_b, pairs_a, pairs_b, window, scale):
    kv_heads = own_a.shape[0]
    chunks = 2
    chunk = kv_heads // chunks
    parts = []
    for c in range(chunks):
        line_a = [jnp.swapaxes(own_a[c * chunk : (c + 1) * chunk], 0, 1)]
        line_b = [jnp.swapaxes(own_b[c * chunk : (c + 1) * chunk], 0, 1)]
        for _ in range(window):
            next_a = lax.ppermute(line_b[-1], "seq", pairs_a)
            next_b = lax.ppermute(line_a[-1], "seq", pairs_b)
            line_a.append(next_a)
            line_b.append(next_b)
        out, dq, now_a, now_b, rest_a, rest_b = attention_chunk(
            info, q_t, do_t, starts, (line_a, line_b), c * chunk, scale
        )
        for t in range(window - 1, -1, -1):
            from_a = lax.ppermute(now_a, "seq", pairs_a)
            from_b = lax.ppermute(now_b, "seq", pairs_b)
            now_a = (rest_a[t] + from_b.astype(jnp.float32)).astype(jnp.bfloat16)
            now_b = (rest_b[t] + from_a.astype(jnp.float32)).astype(jnp.bfloat16)
        parts.append((out, dq, now_a, now_b))
    out, dq, final_a, final_b = (jnp.concatenate(arrays, axis=1) for arrays in zip(*parts))
    return out, dq, *by_half(info, jnp.swapaxes(final_a, 0, 1), jnp.swapaxes(final_b, 0, 1))


def first_of_document(doc_starts, spans, span):
    token = spans[:, None] * span + jnp.arange(span, dtype=jnp.int32)[None, :]
    below = doc_starts[None, None, :] <= token[:, :, None]
    return jnp.max(jnp.where(below, doc_starts[None, None, :], 0), axis=2)[:, None, :]


def body(query, keys, values, grad_out, doc_starts):
    count = lax.axis_size("seq")
    device = lax.axis_index("seq")
    window = min(16, count // 2)
    span = query.shape[2]
    dim = query.shape[4]
    scale = dim ** (-0.5)
    pairs_a, pairs_b = swap_pairs(count)
    half_a = 1 - device % 2

    def payload(half):
        pair = [lax.dynamic_index_in_dim(x[:, 0], half, 0, keepdims=False) for x in (keys, values)]
        return jnp.transpose(jnp.stack(pair), (2, 0, 1, 3))

    own_a, own_b = payload(half_a), payload(1 - half_a)
    q_t = jnp.transpose(query[:, 0], (0, 2, 1, 3))
    do_t = jnp.transpose(grad_out[:, 0], (0, 2, 1, 3))
    if window == 2:
        starts = first_of_document(doc_starts, jnp.arange(2 * count, dtype=jnp.int32), span)
        out, dq, grad_keys, grad_values = two_span_window(
            count, q_t, do_t, starts, own_a, own_b, pairs_a, pairs_b, scale
        )
    else:
        spans = jnp.stack([device, 2 * count - 1 - device])
        starts = first_of_document(doc_starts, spans, span)
        span_a = jnp.where(half_a == 0, device, 2 * count - 1 - device)
        info = jnp.stack([half_a, 1 - half_a, span_a, 2 * count - 1 - span_a]).astype(jnp.int32)
        out, dq, grad_keys, grad_values = any_window(
            info, q_t, do_t, starts, own_a, own_b, pairs_a, pairs_b, window, scale
        )
    out = jnp.transpose(out, (0, 2, 1, 3))[:, None]
    dq = jnp.transpose(dq, (0, 2, 1, 3))[:, None]
    return out, dq, grad_keys, grad_values


def solution(mesh):
    spec = P("batch", "seq", None, "head", None)
    return jax.shard_map(
        body,
        mesh=mesh,
        in_specs=(spec, spec, spec, spec, P("batch")),
        out_specs=(spec, spec, spec, spec),
        check_vma=False,
    )
```
